32 devices in a mesh: grp: 2 (over x), run: 8 (over z, y), sub: 2 (over core).
Axes of the slice: x: 2, y: 2, z: 4, core: 2. Of those that a mesh axis runs over, the one named last changes fastest.
Arguments:
- load_field: float32 [3, 128, 64, 128], P(None, ('grp', 'run'), 'sub'), parts along dimension 1, may hold values from -6 to 6
- initial_guess: float32 [3, 128, 64, 128], P(None, ('grp', 'run'), 'sub'), parts along dimension 1, may hold values from -4 to 4
- occupancy: int32 [128, 64, 128], P(('grp', 'run'), 'sub'), parts along dimension 0, may hold values from 0 to 1, as said below
- density: float32 [128, 64, 128], P(('grp', 'run'), 'sub'), parts along dimension 0, may hold values from 0.3 to 1
Outputs:
- displacement: float32 [3, 128, 64, 128], P(None, ('grp', 'run'), 'sub'), parts along dimension 1
- new_density: float32 [128, 64, 128], P(('grp', 'run'), 'sub'), parts along dimension 0
The draws below stay inside these ranges and needn't reach their ends.
There are 2 independent parts, one for each index of `grp`. The reference program is written for one: setup_inputs(seed, part) draws one part's arguments, and reference() takes and returns one part's arrays. A program takes and returns all parts, laid end to end along the dimension named above; each array names one. Nothing has to cross between parts.
Inputs may be any that keep to these rules, and one draw needn't show every extreme that they name: `occupancy`: 1 marks a bone voxel, 0 marrow; every part has bone voxels.
All inputs are finite; a program needn't handle non-finite values.
Results may differ from the reference program's by a relative error of at most 0.0018.
Values sent between devices are 32-bit elements; how exact they have to be, the bound alone decides.
No kernel may reach another device: no remote copies, remote signals or barrier semaphores. Data moves between devices by JAX's collectives and lax.ppermute only.
A program may use at most 64 MiB of HBM per device.

```python
import math
import jax
import jax.numpy as jnp
import numpy as np
from jax import lax

XCELLS = 128
REACH = 32
ITERS = 2
NZ = 64
NY = 64


def draw_occupancy(key, part):
    layers = jnp.arange(NZ)
    threshold = 250 + 500 * layers // max(NZ - 1, 1)
    ticket = jax.random.randint(key, (NZ, NY, XCELLS), 0, 1000)
    return (ticket < threshold[:, None, None]).astype(jnp.int32)


def shard_levels(own_key, dims, shards, smallest, largest):
    factor_of = 1.0
    for dim, shards_of in shards:
        draws = jax.random.uniform(jax.random.fold_in(jax.random.fold_in(own_key, 6), dim), (shards_of,), jnp.float32, smallest / len(shards), largest / len(shards))
        factor_of = factor_of * jnp.repeat(jnp.exp(draws), dims[dim] // shards_of).reshape((-1,) + (1,) * (len(dims) - 1 - dim))
    return factor_of


def scatter_about(own_key, shape, width, most, split=(), dtype=jnp.bfloat16):
    values = jax.random.normal(own_key, shape, jnp.float32) * width
    if len(split) > 0:
        values = shard_levels(own_key, shape, split, -0.22, 0.18) * values
    return jnp.clip(values, min=-most, max=most).astype(dtype)


def setup_inputs(seed: int = 0, part: int = 0) -> dict:
    seeds = jax.random.split(jax.random.key(seed), 5)
    part_splits = jax.random.split(jax.random.fold_in(seeds[4], part), 5)
    return {
        "load_field": scatter_about(part_splits[0], (3, NZ, NY, XCELLS), 1.0, 6.0, ((1, 8), (2, 2)), jnp.float32),
        "initial_guess": scatter_about(part_splits[1], (3, NZ, NY, XCELLS), 0.5, 4.0, ((1, 8), (2, 2)), jnp.float32),
        "occupancy": draw_occupancy(jax.random.fold_in(jax.random.fold_in(seeds[4], part), 71), part),
        "density": jnp.clip(0.3 + 0.7 * jax.random.uniform(part_splits[3], (NZ, NY, XCELLS), jnp.float32) ** shard_levels(part_splits[3], (NZ, NY, XCELLS), ((0, 8), (1, 2)), -0.2, 0.2), 0.3, 1.0),
    }


POISSON = 0.3
MARROW = 0.05
RATE = 0.5
SLOPE = 4.0
HIGHEST = lax.Precision.HIGHEST

def element_stiffness():
    lame = POISSON / ((1.0 + POISSON) * (1.0 - 2.0 * POISSON))
    shear = 0.5 / (1.0 + POISSON)
    elastic = np.zeros((6, 6))
    elastic[:3, :3] = lame
    for index in range(3):
        elastic[index, index] += 2.0 * shear
        elastic[index + 3, index + 3] = shear
    points = [0.5 - 0.5 / math.sqrt(3.0), 0.5 + 0.5 / math.sqrt(3.0)]
    matrix = np.zeros((24, 24))
    for point_z in points:
        for point_y in points:
            for point_x in points:
                strain = np.zeros((6, 24))
                for corner in range(8):
                    high_z, high_y, high_x = (corner // 4, corner // 2 % 2, corner % 2)
                    weight_x = point_x if high_x else 1.0 - point_x
                    weight_y = point_y if high_y else 1.0 - point_y
                    weight_z = point_z if high_z else 1.0 - point_z
                    slope_x = 1.0 if high_x else -1.0
                    slope_y = 1.0 if high_y else -1.0
                    slope_z = 1.0 if high_z else -1.0
                    grad_x = slope_x * weight_y * weight_z
                    grad_y = weight_x * slope_y * weight_z
                    grad_z = weight_x * weight_y * slope_z
                    column = 3 * corner
                    strain[0, column] = grad_x
                    strain[1, column + 1] = grad_y
                    strain[2, column + 2] = grad_z
                    strain[3, column + 1] = grad_z
                    strain[3, column + 2] = grad_y
                    strain[4, column] = grad_z
                    strain[4, column + 2] = grad_x
                    strain[5, column] = grad_y
                    strain[5, column + 1] = grad_x
                matrix += strain.T @ elastic @ strain / 8.0
    return matrix

def smooth_band(rows, cols, offset):
    row_index = jnp.arange(rows)[:, None]
    col_index = jnp.arange(cols)[None, :]
    distance = (col_index - offset - row_index).astype(jnp.float32)
    decay = REACH / 4.0
    taps = jnp.arange(-REACH, REACH + 1).astype(jnp.float32)
    total = jnp.sum(jnp.exp(-jnp.abs(taps) / decay))
    inside = jnp.abs(distance) <= REACH
    return jnp.where(inside, jnp.exp(-jnp.abs(distance) / decay) / total, 0.0)

def corner_views(field):
    depth, rows, cols = (field.shape[1], field.shape[2], field.shape[3])
    padded = jnp.pad(field, ((0, 0), (1, 0), (1, 0), (1, 0)))
    views = []
    for corner in range(8):
        high_z, high_y, high_x = (corner // 4, corner // 2 % 2, corner % 2)
        views.append(padded[:, high_z:high_z + depth, high_y:high_y + rows, high_x:high_x + cols])
    return views

def element_forces(corners, modulus, stiffness):
    forces = []
    for outer in range(8):
        total = jnp.zeros_like(corners[0])
        for inner in range(8):
            block = stiffness[3 * outer:3 * outer + 3, 3 * inner:3 * inner + 3]
            total = total + jnp.einsum('ab,bzyx->azyx', block, corners[inner], precision=HIGHEST)
        forces.append(modulus[None] * total)
    return forces

def assemble(forces):
    depth, rows, cols = (forces[0].shape[1], forces[0].shape[2], forces[0].shape[3])
    result = jnp.zeros((3, depth + 1, rows + 1, cols + 1), jnp.float32)
    for corner in range(8):
        high_z, high_y, high_x = (corner // 4, corner // 2 % 2, corner % 2)
        result = result.at[:, high_z:high_z + depth, high_y:high_y + rows, high_x:high_x + cols].add(forces[corner])
    return result[:, 1:, 1:, 1:]

def operate(field, modulus, stiffness):
    return assemble(element_forces(corner_views(field), modulus, stiffness))

def reference(load_field, initial_guess, occupancy, density):
    stiffness = jnp.asarray(element_stiffness(), jnp.float32)
    bone = occupancy == 1
    bone_share = occupancy.astype(jnp.float32)
    modulus = jnp.where(bone, density * density, MARROW)
    entries = jnp.diagonal(stiffness)
    diagonal = assemble([modulus[None] * entries[3 * corner:3 * corner + 3, None, None, None] for corner in range(8)])
    displacement = initial_guess
    residual = load_field - operate(initial_guess, modulus, stiffness)
    precond = residual / diagonal
    direction = precond
    product = jnp.sum(residual * precond)
    for iteration in range(ITERS):
        image = operate(direction, modulus, stiffness)
        alpha = product / jnp.sum(direction * image)
        displacement = displacement + alpha * direction
        residual = residual - alpha * image
        if iteration + 1 < ITERS:
            precond = residual / diagonal
            fresh = jnp.sum(residual * precond)
            direction = precond + fresh / product * direction
            product = fresh
    corners = corner_views(displacement)
    forces = element_forces(corners, modulus, stiffness)
    energy = jnp.zeros_like(density)
    for corner in range(8):
        energy = energy + lax.optimization_barrier(jnp.sum(corners[corner] * forces[corner], axis=0))
    energy = 0.5 * energy
    specific = bone_share * energy / density
    depth, rows, cols = density.shape
    along_x = jnp.einsum('zyj,ij->zyi', specific, smooth_band(cols, cols, 0), precision=HIGHEST)
    along_y = jnp.einsum('zjx,ij->zix', along_x, smooth_band(rows, rows, 0), precision=HIGHEST)
    stimulus = jnp.einsum('jyx,ij->iyx', along_y, smooth_band(depth, depth, 0), precision=HIGHEST)
    count = jnp.sum(bone_share)
    total = jnp.sum(bone_share * stimulus)
    mean = total / count
    updated = jnp.minimum(density * (1.0 + RATE * jnp.tanh(SLOPE * (stimulus / mean - 1.0))), 1.0)
    new_density = jnp.where(bone, updated, density)
    return (displacement, new_density)
```

```python
import functools
import math

import jax
import jax.numpy as jnp
from jax import lax
from jax.experimental import pallas as pl
from jax.experimental.pallas import tpu as pltpu
from jax.sharding import PartitionSpec as P

REACH = 32
POISSON = 0.3
MARROW = 0.05
RATE = 0.5
SLOPE = 4.0
DECAY = REACH / 4.0

LAME = POISSON / ((1.0 + POISSON) * (1.0 - 2.0 * POISSON)) / 16.0
SHEAR = 0.5 / (1.0 + POISSON) / 16.0
ENTRY = 16.0 * (LAME + 4.0 * SHEAR) / 9.0
NORM = 1.0 / sum(math.exp(-abs(k) / DECAY) for k in range(-REACH, REACH + 1))

DEEP = 3
WIN = 13
ROWS = 40
SLOT_LO = 17
SLOT_HI = 11
SIDE = 39 + 33 + 12
PAIR = ("run", "sub")

VMEM = pl.BlockSpec(memory_space=pltpu.VMEM)


def weight(distance):
    return NORM * math.exp(-distance / DECAY)


def call(kernel, outs, ins, scratch=()):
    return pl.pallas_call(
        kernel,
        out_shape=[jax.ShapeDtypeStruct(s, jnp.float32) for s in outs],
        in_specs=[VMEM] * len(ins),
        out_specs=[VMEM] * len(outs),
        scratch_shapes=[pltpu.VMEM(s, jnp.float32) for s in scratch],
        compiler_params=pltpu.CompilerParams(vmem_limit_bytes=40 * 1024 * 1024),
    )(*ins)


def lane_right(block):
    lane = lax.broadcasted_iota(jnp.int32, block.shape, 1)
    return jnp.where(lane == 0, 0.0, pltpu.roll(block, 1, 1))


def lane_left(block):
    lane = lax.broadcasted_iota(jnp.int32, block.shape, 1)
    return jnp.where(lane == block.shape[1] - 1, 0.0, pltpu.roll(block, block.shape[1] - 1, 1))


def row_up(block):
    row = lax.broadcasted_iota(jnp.int32, block.shape, 0)
    return jnp.where(row == 0, 0.0, pltpu.roll(block, 1, 0))


def row_down(block):
    row = lax.broadcasted_iota(jnp.int32, block.shape, 0)
    return jnp.where(row == block.shape[0] - 1, 0.0, pltpu.roll(block, block.shape[0] - 1, 0))


def faces(block):
    other = lane_right(block)
    total, change = block + other, block - other
    a, b = row_up(total), row_up(change)
    return total + a, change + b, total - a, change - b


def unfaces(modes):
    columns = []
    for x in range(2):
        total, change = modes[x], modes[2 + x]
        columns.append(total + change + row_down(total - change))
    return columns[0] + columns[1] + lane_left(columns[0] - columns[1])


def modes_of(low, high):
    out = []
    for c in range(3):
        modes = [None] * 8
        for m in range(4):
            if m:
                modes[m] = high[4 * c + m] + low[4 * c + m]
            modes[4 + m] = high[4 * c + m] - low[4 * c + m]
        out.append(modes)
    return out


X, Y, Z = 1, 2, 4


def stress(u, mod):
    g = [[None] * 8 for _ in range(3)]
    bulk, rigid = mod * LAME, mod * SHEAR
    twice = rigid + rigid
    bulk3, rigid3 = mod * (LAME / 3.0), mod * (SHEAR / 3.0)
    last = mod * ((LAME + 4.0 * SHEAR) / 9.0)
    t = (u[0][X] + u[1][Y] + u[2][Z]) * bulk
    g[0][X] = t + u[0][X] * twice
    g[1][Y] = t + u[1][Y] * twice
    g[2][Z] = t + u[2][Z] * twice
    g[0][Y] = g[1][X] = (u[0][Y] + u[1][X]) * rigid
    g[0][Z] = g[2][X] = (u[0][Z] + u[2][X]) * rigid
    g[1][Z] = g[2][Y] = (u[1][Z] + u[2][Y]) * rigid
    for (c, m), (d, n) in (
        ((1, X | Y), (2, X | Z)),
        ((0, X | Y), (2, Y | Z)),
        ((0, X | Z), (1, Y | Z)),
    ):
        s = (u[c][m] + u[d][n]) * bulk3
        g[c][m] = s + u[c][m] * rigid
        g[d][n] = s + u[d][n] * rigid
    s = u[0][Y | Z] + u[1][X | Z] + u[2][X | Y]
    g[0][Y | Z] = (s + u[0][Y | Z]) * rigid3
    g[1][X | Z] = (s + u[1][X | Z]) * rigid3
    g[2][X | Y] = (s + u[2][X | Y]) * rigid3
    for c in range(3):
        g[c][7] = u[c][7] * last
    return g


def quadratic(u):
    def sq(v):
        return v * v

    t = sq(u[0][X] + u[1][Y] + u[2][Z])
    r2 = sq(u[0][X]) + sq(u[1][Y]) + sq(u[2][Z])
    r = sq(u[0][Y] + u[1][X]) + sq(u[0][Z] + u[2][X]) + sq(u[1][Z] + u[2][Y])
    t3 = 0.0
    for (c, m), (d, n) in (
        ((1, X | Y), (2, X | Z)),
        ((0, X | Y), (2, Y | Z)),
        ((0, X | Z), (1, Y | Z)),
    ):
        t3 = t3 + sq(u[c][m] + u[d][n])
        r = r + (sq(u[c][m]) + sq(u[d][n]))
    p, q, s = u[0][Y | Z], u[1][X | Z], u[2][X | Y]
    r3 = sq(p + q) + sq(p + s) + sq(q + s)
    last = sq(u[0][7]) + sq(u[1][7]) + sq(u[2][7])
    return (
        LAME * (t + t3 * (1.0 / 3.0))
        + SHEAR * (r + r2 + r2 + r3 * (1.0 / 3.0))
        + ((LAME + 4.0 * SHEAR) / 9.0) * last
    )


def pack_planes(load, guess, occupancy, density, modulus, up, down):
    modulus[...] = jnp.where(occupancy[...] == 1, density[...] * density[...], MARROW)
    for c in range(3):
        for k in range(3):
            up[3 * c + k] = guess[c, 5 + k]
        for k in range(2):
            up[9 + 2 * c + k] = load[c, 6 + k]
            down[2 * c + k] = guess[c, k]
        down[6 + c] = load[c, 0]
    for k in range(2):
        up[15 + k] = modulus[6 + k]
        down[9 + k] = modulus[k]


def pack_rows(load, guess, modulus, low, high, side):
    sub = lax.axis_index("sub")
    rows = pl.ds(pl.multiple_of(24 * (1 - sub), 8), 8)
    for c in range(3):
        for k in range(3):
            side[13 * c + k] = low[3 * c + k, rows]
        for k in range(8):
            side[13 * c + 3 + k] = guess[c, k, rows]
        for k in range(2):
            side[13 * c + 11 + k] = high[2 * c + k, rows]
        for k in range(2):
            side[39 + 11 * c + k] = low[9 + 2 * c + k, rows]
        for k in range(8):
            side[39 + 11 * c + 2 + k] = load[c, k, rows]
        side[39 + 11 * c + 10] = high[6 + c, rows]
    for k in range(2):
        side[72 + k] = low[15 + k, rows]
        side[72 + 10 + k] = high[9 + k, rows]
    for k in range(8):
        side[72 + 2 + k] = modulus[k, rows]


def krylov(
    load, guess, modulus, low, high, side, row_out, guess_w, first, second,
    load_w, mod_w, inverse, plane, total, carry, sums,
):
    sub = lax.axis_index("sub")
    run = lax.axis_index("run")
    own = pl.ds(pl.multiple_of(8 * sub, 8), 32)
    rest = pl.ds(pl.multiple_of(32 * (1 - sub), 8), 8)
    for c in range(3):
        for k in range(3):
            guess_w[c, k, own] = low[3 * c + k]
        for k in range(8):
            guess_w[c, 3 + k, own] = guess[c, k]
        for k in range(2):
            guess_w[c, 11 + k, own] = high[2 * c + k]
        for k in range(13):
            guess_w[c, k, rest] = side[13 * c + k]
        for k in range(2):
            load_w[c, k, own] = low[9 + 2 * c + k]
        for k in range(8):
            load_w[c, 2 + k, own] = load[c, k]
        load_w[c, 10, own] = high[6 + c]
        for k in range(11):
            load_w[c, k, rest] = side[39 + 11 * c + k]
    for k in range(2):
        mod_w[k, own] = low[15 + k]
        mod_w[10 + k, own] = high[9 + k]
    for k in range(8):
        mod_w[2 + k, own] = modulus[k]
    for k in range(12):
        mod_w[k, rest] = side[72 + k]

    def invert(k, _):
        t = mod_w[k] + mod_w[k + 1]
        t = t + row_down(t)
        t = (t + lane_left(t)) * ENTRY
        fine = (t > 0.0) & (run * 8 + k - 2 >= 0)
        inverse[k] = jnp.where(fine, 1.0 / jnp.where(fine, t, 1.0), 0.0)
        return 0

    lax.fori_loop(0, 11, invert, 0)

    sums[...] = jnp.zeros_like(sums)

    def enter(field, k, slot):
        for c in range(3):
            for m, value in enumerate(faces(field[c, k])):
                plane[slot, 4 * c + m] = value

    def voxels(k, mod_at):
        now, before = lax.rem(k, 2), lax.rem(k + 1, 2)
        for tile in range(ROWS // 8):
            rows = slice(8 * tile, 8 * tile + 8)
            high_m = [plane[now, m, rows] for m in range(12)]
            low_m = [plane[before, m, rows] for m in range(12)]
            g = stress(modes_of(low_m, high_m), mod_w[mod_at, rows])
            for c in range(3):
                for m in range(4):
                    d = g[c][4 + m]
                    at = 4 * c + m
                    if m:
                        s = g[c][m]
                        total[at, rows] = carry[at, rows] + (s - d)
                        carry[at, rows] = s + d
                    else:
                        total[at, rows] = carry[at, rows] - d
                        carry[at, rows] = d

    def image(c):
        return unfaces([total[4 * c + m] for m in range(4)])

    enter(guess_w, 0, 0)
    carry[...] = jnp.zeros_like(carry)

    def pass_one(k, _):
        enter(guess_w, k, lax.rem(k, 2))
        voxels(k, k - 1)

        @pl.when(k >= 2)
        def _():
            dot = 0.0
            for c in range(3):
                residual = load_w[c, k - 2] - image(c)
                z = residual * inverse[k - 2]
                first[c, k - 2] = z
                dot = dot + residual * z

            @pl.when((k >= 4) & (k < 12))
            def _():
                sums[0] += dot

        return 0

    lax.fori_loop(1, 13, pass_one, 0)

    enter(first, 0, 0)
    carry[...] = jnp.zeros_like(carry)

    def pass_two(k, _):
        enter(first, k, lax.rem(k, 2))
        voxels(k, k)

        @pl.when(k >= 2)
        def _():
            dot, cross = 0.0, 0.0
            for c in range(3):
                w = image(c)
                s = w * inverse[k - 1]
                second[c, k - 2] = s
                dot = dot + w * first[c, k - 1]
                cross = cross + w * s

            @pl.when(k >= 3)
            def _():
                sums[1] += dot
                sums[2] += cross

        return 0

    lax.fori_loop(1, 11, pass_two, 0)

    enter(second, 0, 0)

    def pass_three(k, _):
        enter(second, k, lax.rem(k, 2))
        now, before = lax.rem(k, 2), lax.rem(k + 1, 2)
        for tile in range(ROWS // 8):
            rows = slice(8 * tile, 8 * tile + 8)
            u = modes_of(
                [plane[before, m, rows] for m in range(12)],
                [plane[now, m, rows] for m in range(12)],
            )
            sums[3, rows] += quadratic(u) * mod_w[k + 1, rows]
        return 0

    lax.fori_loop(1, 9, pass_three, 0)

    lane = lax.broadcasted_iota(jnp.int32, (1, 128), 1)
    line = jnp.zeros((1, 128), jnp.float32)
    for k in range(4):
        value = jnp.sum(jnp.sum(sums[k, own], axis=0, keepdims=True), axis=1, keepdims=True)
        line = jnp.where(lane == k, value, line)
    row_out[...] = jnp.broadcast_to(line, row_out.shape)


def pick(line, k):
    lane = lax.broadcasted_iota(jnp.int32, line.shape, 1)
    return jnp.sum(jnp.where(lane == k, line, 0.0), axis=1, keepdims=True)


def energies(lines, guess_w, first, second, occupancy, density, out, smooth, plane, field, specific):
    sub = lax.axis_index("sub")
    own = pl.ds(pl.multiple_of(8 * sub, 8), 32)
    line = jnp.sum(lines[...], axis=0, keepdims=True)
    a, b, c, e = (pick(line, k) for k in range(4))
    alpha = a / b
    fresh = alpha * alpha * c - a
    beta = fresh / a
    square = alpha * alpha * e - (1.0 + beta) * (1.0 + beta) * b
    after = fresh / square
    p = jnp.broadcast_to(alpha + after * (1.0 + beta), (ROWS, 128))
    q = jnp.broadcast_to(-after * alpha, (ROWS, 128))

    def enter(k, slot):
        for c in range(3):
            value = guess_w[c, k + 2] + p * first[c, k + 1] + q * second[c, k]
            field[c] = value
            for m, mode in enumerate(faces(value)):
                plane[slot, 4 * c + m] = mode

    enter(0, 0)

    def body(k, _):
        now, before = lax.rem(k, 2), lax.rem(k + 1, 2)
        enter(k, now)
        for c in range(3):
            out[c, k - 1] = field[c, own]
        for tile in range(4):
            rows = pl.ds(pl.multiple_of(8 * sub + 8 * tile, 8), 8)
            here = slice(8 * tile, 8 * tile + 8)
            u = modes_of(
                [plane[before, m, rows] for m in range(12)],
                [plane[now, m, rows] for m in range(12)],
            )
            rho = density[k - 1, here]
            bone = occupancy[k - 1, here] == 1
            share = jnp.where(bone, rho * rho / rho, 0.0)
            specific[pl.ds(pl.multiple_of(32 * (k - 1) + 8 * tile, 8), 8), :] = (
                0.5 * share * quadratic(u)
            )
        return 0

    lax.fori_loop(1, 9, body, 0)
    row = lax.broadcasted_iota(jnp.int32, (128, 128), 0)
    col = lax.broadcasted_iota(jnp.int32, (128, 128), 1)
    gap = jnp.abs(row - col).astype(jnp.float32)
    band = jnp.where(gap <= REACH, NORM * jnp.exp(gap * (-1.0 / DECAY)), 0.0)
    smooth[...] = jnp.dot(
        specific[...], band, precision=lax.Precision.HIGHEST, preferred_element_type=jnp.float32
    ).reshape(smooth.shape)


def along_y(mine, other, out, planes):
    sub = lax.axis_index("sub")
    run = lax.axis_index("run")
    row = lax.broadcasted_iota(jnp.int32, (32, 32), 0)
    col = lax.broadcasted_iota(jnp.int32, (32, 32), 1)

    def band(offset):
        gap = jnp.abs(col + offset - row).astype(jnp.float32)
        return jnp.where(gap <= REACH, NORM * jnp.exp(gap * (-1.0 / DECAY)), 0.0)

    near = band(0)
    far = band(32 - 64 * sub)
    upward, downward = 0.0, 0.0
    for k in range(8):
        value = jnp.dot(
            near, mine[k], precision=lax.Precision.HIGHEST, preferred_element_type=jnp.float32
        ) + jnp.dot(
            far, other[k], precision=lax.Precision.HIGHEST, preferred_element_type=jnp.float32
        )
        out[k] = value
        upward = upward + math.exp(-(7 - k) / DECAY) * value
        downward = downward + math.exp(-k / DECAY) * value
    for k in range(planes.shape[0]):
        planes[k] = jnp.where(k > run, upward, downward)


def along_z(count, mine, planes, below, above, occupancy, stimulus, row_out):
    run = lax.axis_index("run")
    span = REACH // 8
    lower, upper = 0.0, 0.0
    for o in range(1, span):
        scale = math.exp(-8.0 * (o - 1) / DECAY)
        at = jnp.maximum(run - o, 0)
        lower = lower + jnp.where(run - o >= 0, scale * planes[at], 0.0)
        at = jnp.minimum(run + o, count - 1)
        upper = upper + jnp.where(run + o < count, scale * planes[at], 0.0)
    has_below = run - span >= 0
    has_above = run + span < count
    total, bone = 0.0, 0.0
    for i in range(8):
        value = weight(i + 1) * lower + weight(8 - i) * upper
        far_below, far_above = 0.0, 0.0
        for j in range(8):
            value = value + weight(abs(i - j)) * mine[j]
            if j >= i:
                far_below = far_below + weight(i - j + REACH) * below[j]
            if j <= i:
                far_above = far_above + weight(j - i + REACH) * above[j]
        value = value + jnp.where(has_below, far_below, 0.0) + jnp.where(has_above, far_above, 0.0)
        stimulus[i] = value
        share = occupancy[i].astype(jnp.float32)
        total = total + share * value
        bone = bone + share
    lane = lax.broadcasted_iota(jnp.int32, (1, 128), 1)

    def whole(block):
        return jnp.sum(jnp.sum(block, axis=0, keepdims=True), axis=1, keepdims=True)

    line = jnp.where(lane == 0, whole(total), jnp.where(lane == 1, whole(bone), 0.0))
    row_out[...] = jnp.broadcast_to(line, row_out.shape)


def remodel(lines, stimulus, occupancy, density, out):
    line = jnp.sum(lines[...], axis=0, keepdims=True)
    mean = jnp.broadcast_to(pick(line, 0) / pick(line, 1), stimulus.shape[1:])
    for k in range(8):
        rho = density[k]
        updated = jnp.minimum(rho * (1.0 + RATE * jnp.tanh(SLOPE * (stimulus[k] / mean - 1.0))), 1.0)
        out[k] = jnp.where(occupancy[k] == 1, updated, rho)


def everyone(lines):
    return lax.all_to_all(lines, PAIR, 0, 0, tiled=True)


def local(load, guess, occupancy, density):
    count = lax.axis_size("run")
    members = count * lax.axis_size("sub")
    block = density.shape
    modulus, up, down = call(
        pack_planes,
        [block, (SLOT_LO, 32, 128), (SLOT_HI, 32, 128)],
        [load, guess, occupancy, density],
    )
    low = lax.ppermute(up, "run", [(i, i + 1) for i in range(count - 1)])
    high = lax.ppermute(down, "run", [(i + 1, i) for i in range(count - 1)])
    (side,) = call(pack_rows, [(SIDE, 8, 128)], [load, guess, modulus, low, high])
    swap = [(0, 1), (1, 0)]
    side = lax.ppermute(side, "sub", swap)
    lines, guess_w, first, second = call(
        krylov,
        [(members, 128), (3, 13, ROWS, 128), (3, 11, ROWS, 128), (3, 9, ROWS, 128)],
        [load, guess, modulus, low, high, side],
        [
            (3, 11, ROWS, 128), (12, ROWS, 128), (11, ROWS, 128),
            (2, 12, ROWS, 128), (12, ROWS, 128), (12, ROWS, 128), (4, ROWS, 128),
        ],
    )
    lines = everyone(lines)
    displacement, smooth = call(
        energies,
        [guess.shape, block],
        [lines, guess_w, first, second, occupancy, density],
        [(2, 12, ROWS, 128), (3, ROWS, 128), (256, 128)],
    )
    other = lax.ppermute(smooth, "sub", swap)
    smooth, planes = call(along_y, [block, (count, 32, 128)], [smooth, other])
    span = REACH // 8
    rise = [(i, i + span) for i in range(count - span)]
    fall = [(i + span, i) for i in range(count - span)]
    if count <= 2 * span:
        below = above = lax.ppermute(smooth, "run", rise + fall)
    else:
        below = lax.ppermute(smooth, "run", rise)
        above = lax.ppermute(smooth, "run", fall)
    planes = lax.all_to_all(planes, "run", 0, 0, tiled=True)
    stimulus, lines = call(
        functools.partial(along_z, count),
        [block, (members, 128)],
        [smooth, planes, below, above, occupancy],
    )
    lines = everyone(lines)
    (new_density,) = call(remodel, [block], [lines, stimulus, occupancy, density])
    return displacement, new_density


def solution(mesh):
    field = P(None, ("grp", "run"), "sub", None)
    cells = P(("grp", "run"), "sub", None)
    return jax.shard_map(
        local,
        mesh=mesh,
        in_specs=(field, field, cells, cells),
        out_specs=(field, cells),
        check_vma=False,
    )
```

```python
import functools
import math

import jax
import jax.numpy as jnp
from jax import lax
from jax.experimental import pallas as pl
from jax.experimental.pallas import tpu as pltpu
from jax.sharding import PartitionSpec as P

REACH = 32
POISSON = 0.3
MARROW = 0.05
RATE = 0.5
SLOPE = 4.0
DECAY = REACH / 4.0

LAME = POISSON / ((1.0 + POISSON) * (1.0 - 2.0 * POISSON)) / 16.0
SHEAR = 0.5 / (1.0 + POISSON) / 16.0
ENTRY = 16.0 * (LAME + 4.0 * SHEAR) / 9.0
NORM = 1.0 / sum(math.exp(-abs(k) / DECAY) for k in range(-REACH, REACH + 1))

ROWS = 40
PAIR = ("run", "sub")

VMEM = pl.BlockSpec(memory_space=pltpu.VMEM)


def weight(distance):
    return NORM * math.exp(-distance / DECAY)


def call(kernel, outs, ins, scratch=()):
    return pl.pallas_call(
        kernel,
        out_shape=[jax.ShapeDtypeStruct(s, jnp.float32) for s in outs],
        in_specs=[VMEM] * len(ins),
        out_specs=[VMEM] * len(outs),
        scratch_shapes=[pltpu.VMEM(s, jnp.float32) for s in scratch],
        compiler_params=pltpu.CompilerParams(vmem_limit_bytes=40 * 1024 * 1024),
    )(*ins)


def lane_right(block):
    lane = lax.broadcasted_iota(jnp.int32, block.shape, 1)
    return jnp.where(lane == 0, 0.0, pltpu.roll(block, 1, 1))


def lane_left(block):
    lane = lax.broadcasted_iota(jnp.int32, block.shape, 1)
    return jnp.where(lane == block.shape[1] - 1, 0.0, pltpu.roll(block, block.shape[1] - 1, 1))


def row_down(block):
    row = lax.broadcasted_iota(jnp.int32, block.shape, 0)
    return jnp.where(row == block.shape[0] - 1, 0.0, pltpu.roll(block, block.shape[0] - 1, 0))


def stiff(occupancy, density):
    return jnp.where(occupancy == 1, density * density, MARROW)


def enter(pair, k, c, field):
    other = lane_right(field)
    pair[2 * c, k, 8:48] = field + other
    pair[2 * c + 1, k, 8:48] = field - other


def clear(pair):
    for m in range(6):
        for k in range(pair.shape[1]):
            pair[m, k, 0:8] = jnp.zeros((8, 128), jnp.float32)


def plane_modes(pair, k, tile):
    out = [None] * 12
    for c in range(3):
        for x in range(2):
            here = pair[2 * c + x, k, 8 + 8 * tile : 16 + 8 * tile]
            above = pair[2 * c + x, k, 7 + 8 * tile : 15 + 8 * tile]
            out[4 * c + x] = here + above
            out[4 * c + 2 + x] = here - above
    return out


def steps(count, body, carry):
    def turn(k, carry):
        return body(2 * k + 1, body(2 * k, carry))

    carry = lax.fori_loop(0, count // 2, turn, carry)
    return body(count - 1, carry) if count % 2 else carry


def march(pair, start, count, mod, near, far, to):
    for tile in range(ROWS // 8):
        rows = slice(8 * tile, 8 * tile + 8)

        def leave(k, totals):
            for c in range(3):
                for x in range(2):
                    s, d = totals[4 * c + x], totals[4 * c + 2 + x]
                    near[2 * c + x, k, rows] = s + d
                    far[2 * c + x, k, rows] = s - d

        def body(k, carry):
            low, kept = carry
            high = plane_modes(pair, start + k + 1, tile)
            g = stress(modes_of(low, high), mod(k, rows))
            totals, after = [None] * 12, [None] * 12
            for c in range(3):
                for m in range(4):
                    d = g[c][4 + m]
                    at = 4 * c + m
                    if m:
                        s = g[c][m]
                        totals[at] = kept[at] + (s - d)
                        after[at] = s + d
                    else:
                        totals[at] = kept[at] - d
                        after[at] = d
            leave(to + k, totals)
            return high, after

        zeros = [jnp.zeros((8, 128), jnp.float32)] * 12
        _, kept = steps(count, body, (plane_modes(pair, start, tile), zeros))
        leave(to + count, kept)


def image(near, far, k, c):
    columns = [
        near[2 * c + x, k, 0:ROWS] + far[2 * c + x, k, 1 : ROWS + 1] for x in range(2)
    ]
    return columns[0] + columns[1] + lane_left(columns[0] - columns[1])


def energy_march(pair, count, use):
    for tile in range(ROWS // 8):

        def body(k, low):
            high = plane_modes(pair, k + 1, tile)
            use(k, tile, quadratic(modes_of(low, high)))
            return high

        steps(count, body, plane_modes(pair, 0, tile))


def inverted(low, high):
    t = low + high
    t = t + row_down(t)
    t = (t + lane_left(t)) * ENTRY
    return jnp.where(t > 0.0, 1.0 / jnp.where(t > 0.0, t, 1.0), 0.0)


def whole(block):
    return jnp.sum(jnp.sum(block, axis=0, keepdims=True), axis=1, keepdims=True)


def modes_of(low, high):
    out = []
    for c in range(3):
        modes = [None] * 8
        for m in range(4):
            if m:
                modes[m] = high[4 * c + m] + low[4 * c + m]
            modes[4 + m] = high[4 * c + m] - low[4 * c + m]
        out.append(modes)
    return out


X, Y, Z = 1, 2, 4


def stress(u, mod):
    g = [[None] * 8 for _ in range(3)]
    bulk, rigid = mod * LAME, mod * SHEAR
    twice = rigid + rigid
    bulk3, rigid3 = mod * (LAME / 3.0), mod * (SHEAR / 3.0)
    last = mod * ((LAME + 4.0 * SHEAR) / 9.0)
    t = (u[0][X] + u[1][Y] + u[2][Z]) * bulk
    g[0][X] = t + u[0][X] * twice
    g[1][Y] = t + u[1][Y] * twice
    g[2][Z] = t + u[2][Z] * twice
    g[0][Y] = g[1][X] = (u[0][Y] + u[1][X]) * rigid
    g[0][Z] = g[2][X] = (u[0][Z] + u[2][X]) * rigid
    g[1][Z] = g[2][Y] = (u[1][Z] + u[2][Y]) * rigid
    for (c, m), (d, n) in (
        ((1, X | Y), (2, X | Z)),
        ((0, X | Y), (2, Y | Z)),
        ((0, X | Z), (1, Y | Z)),
    ):
        s = (u[c][m] + u[d][n]) * bulk3
        g[c][m] = s + u[c][m] * rigid
        g[d][n] = s + u[d][n] * rigid
    s = u[0][Y | Z] + u[1][X | Z] + u[2][X | Y]
    g[0][Y | Z] = (s + u[0][Y | Z]) * rigid3
    g[1][X | Z] = (s + u[1][X | Z]) * rigid3
    g[2][X | Y] = (s + u[2][X | Y]) * rigid3
    for c in range(3):
        g[c][7] = u[c][7] * last
    return g


def quadratic(u):
    def sq(v):
        return v * v

    t = sq(u[0][X] + u[1][Y] + u[2][Z])
    r2 = sq(u[0][X]) + sq(u[1][Y]) + sq(u[2][Z])
    r = sq(u[0][Y] + u[1][X]) + sq(u[0][Z] + u[2][X]) + sq(u[1][Z] + u[2][Y])
    t3 = 0.0
    for (c, m), (d, n) in (
        ((1, X | Y), (2, X | Z)),
        ((0, X | Y), (2, Y | Z)),
        ((0, X | Z), (1, Y | Z)),
    ):
        t3 = t3 + sq(u[c][m] + u[d][n])
        r = r + (sq(u[c][m]) + sq(u[d][n]))
    p, q, s = u[0][Y | Z], u[1][X | Z], u[2][X | Y]
    r3 = sq(p + q) + sq(p + s) + sq(q + s)
    last = sq(u[0][7]) + sq(u[1][7]) + sq(u[2][7])
    return (
        LAME * (t + t3 * (1.0 / 3.0))
        + SHEAR * (r + r2 + r2 + r3 * (1.0 / 3.0))
        + ((LAME + 4.0 * SHEAR) / 9.0) * last
    )


def side_rows(load, guess, occupancy, density):
    sub = lax.axis_index("sub")
    flat = lambda part: part.reshape((-1,) + part.shape[-2:])
    near = lambda part: jnp.where(sub == 0, part[..., 24:32, :], part[..., 0:8, :])
    return jnp.concatenate(
        [flat(near(guess)), flat(near(load)), stiff(near(occupancy), near(density))], axis=0
    )


def inner(
    load, guess, bone, density, side, up, down, guess_w, first_w, mod_w, inverse, square,
    pair, near, far,
):
    sub = lax.axis_index("sub")
    own = pl.ds(pl.multiple_of(8 * sub, 8), 32)
    rest = pl.ds(pl.multiple_of(32 * (1 - sub), 8), 8)
    clear(pair)
    far[:, :, ROWS : ROWS + 8] = jnp.zeros((6, 8, 8, 128), jnp.float32)
    for k in range(8):
        mod_w[k, own] = stiff(bone[k], density[k])
        mod_w[k, rest] = side[48 + k]
        for c in range(3):
            guess_w[c, k, own] = guess[c, k]
            guess_w[c, k, rest] = side[8 * c + k]
            first_w[c, k, own] = load[c, k]
            first_w[c, k, rest] = side[24 + 8 * c + k]

    def prepare(k, _):
        for c in range(3):
            enter(pair, k, c, guess_w[c, k])
        return 0

    lax.fori_loop(0, 8, prepare, 0)
    for k in range(7):
        inverse[k] = inverted(mod_w[k], mod_w[k + 1])
    march(pair, 0, 7, lambda k, rows: mod_w[k + 1, rows], near, far, 0)
    square[...] = jnp.zeros_like(square)

    def settle(k, _):
        for c in range(3):
            residual = first_w[c, k] - image(near, far, k, c)
            z = residual * inverse[k]
            first_w[c, k] = z
            square[...] += residual * z
        return 0

    for c in range(3):
        down[3 + c] = first_w[c, 0] - image(near, far, 0, c)
        up[3 + c] = first_w[c, 7] - image(near, far, 7, c)
    lax.fori_loop(1, 7, settle, 0)
    for c in range(3):
        down[c] = guess_w[c, 0]
        up[c] = guess_w[c, 7]
        up[6 + c] = first_w[c, 6]
    up[9] = mod_w[7]
    down[6] = mod_w[0]
    down[7] = inverse[0]


def krylov(
    up, down, guess_w, first_w, mod_w, inverse, square, low, high, row_out, first, second,
    pair, near, far, mods, inverses, sums,
):
    sub = lax.axis_index("sub")
    run = lax.axis_index("run")
    own = pl.ds(pl.multiple_of(8 * sub, 8), 32)
    clear(pair)
    far[:, :, ROWS : ROWS + 8] = jnp.zeros((6, 11, 8, 128), jnp.float32)
    mods[0] = low[9]
    mods[9] = high[6]
    for k in range(8):
        mods[1 + k] = mod_w[k]
    inverses[0] = jnp.where(run > 0, inverted(low[9], mod_w[0]), 0.0)
    for k in range(7):
        inverses[1 + k] = inverse[k]
    inverses[8] = inverted(mod_w[7], high[6])

    for c in range(3):
        enter(pair, 0, c, low[c])
        enter(pair, 1, c, guess_w[c, 0])
        enter(pair, 2, c, guess_w[c, 7])
        enter(pair, 3, c, high[c])
    march(pair, 0, 1, lambda k, rows: mods[1, rows], near, far, 0)
    march(pair, 2, 1, lambda k, rows: mods[9, rows], near, far, 2)
    begun = (low, down, up, high)
    invert = (inverses[0], inverses[1], inverses[8], high[7])
    sums[...] = jnp.zeros_like(sums)
    dot = square[...]
    for c in range(3):
        values = []
        for k in range(4):
            residual = begun[k][3 + c] - image(near, far, k, c)
            z = residual * invert[k]
            values.append(z)
            if k in (1, 2):
                dot = dot + residual * z
        first[c, 0] = low[6 + c]
        first[c, 1] = values[0]
        first[c, 2] = values[1]
        for k in range(1, 7):
            first[c, 2 + k] = first_w[c, k]
        first[c, 9] = values[2]
        first[c, 10] = values[3]
    sums[0] = dot

    def prepare(k, _):
        for c in range(3):
            enter(pair, k, c, first[c, k])
        return 0

    lax.fori_loop(0, 11, prepare, 0)
    march(pair, 0, 10, lambda k, rows: mods[k, rows], near, far, 0)

    def settle(k, _):
        dot, cross = 0.0, 0.0
        for c in range(3):
            w = image(near, far, k + 1, c)
            s = w * inverses[k]
            second[c, k] = s
            enter(pair, k, c, s)
            dot = dot + w * first[c, k + 1]
            cross = cross + w * s

        @pl.when(k >= 1)
        def _():
            sums[1] += dot
            sums[2] += cross

        return 0

    lax.fori_loop(0, 9, settle, 0)

    def use(k, tile, value):
        rows = slice(8 * tile, 8 * tile + 8)
        sums[3, rows] += value * mods[k + 1, rows]

    energy_march(pair, 8, use)
    lane = lax.broadcasted_iota(jnp.int32, (1, 128), 1)
    line = jnp.zeros((1, 128), jnp.float32)
    for k in range(4):
        line = jnp.where(lane == k, whole(sums[k, own]), line)
    row_out[...] = jnp.broadcast_to(line, row_out.shape)


def pick(line, k):
    lane = lax.broadcasted_iota(jnp.int32, line.shape, 1)
    return jnp.sum(jnp.where(lane == k, line, 0.0), axis=1, keepdims=True)


def energies(
    lines, guess_w, low, first, second, occupancy, density, out, smooth, pair, field, specific
):
    sub = lax.axis_index("sub")
    own = pl.ds(pl.multiple_of(8 * sub, 8), 32)
    line = jnp.sum(lines[...], axis=0, keepdims=True)
    a, b, c, e = (pick(line, k) for k in range(4))
    alpha = a / b
    fresh = alpha * alpha * c - a
    beta = fresh / a
    square = alpha * alpha * e - (1.0 + beta) * (1.0 + beta) * b
    after = fresh / square
    p = jnp.broadcast_to(alpha + after * (1.0 + beta), (ROWS, 128))
    q = jnp.broadcast_to(-after * alpha, (ROWS, 128))
    clear(pair)
    for c in range(3):
        enter(pair, 0, c, low[c] + p * first[c, 1] + q * second[c, 0])

    def advance(k, _):
        for c in range(3):
            value = guess_w[c, k] + p * first[c, k + 2] + q * second[c, k + 1]
            field[c] = value
            enter(pair, k + 1, c, value)
        for c in range(3):
            out[c, k] = field[c, own]
        return 0

    lax.fori_loop(0, 8, advance, 0)

    def use(k, tile, value):
        specific[k, 8 * tile : 8 * tile + 8] = value

    energy_march(pair, 8, use)
    parts = []
    for k in range(8):
        rho = density[k]
        share = jnp.where(occupancy[k] == 1, rho * rho / rho, 0.0)
        parts.append(0.5 * share * specific[k, own])
    row = lax.broadcasted_iota(jnp.int32, (128, 128), 0)
    col = lax.broadcasted_iota(jnp.int32, (128, 128), 1)
    gap = jnp.abs(row - col).astype(jnp.float32)
    band = jnp.where(gap <= REACH, NORM * jnp.exp(gap * (-1.0 / DECAY)), 0.0)
    smooth[...] = jnp.dot(
        jnp.concatenate(parts, axis=0), band,
        precision=lax.Precision.HIGHEST, preferred_element_type=jnp.float32,
    ).reshape(smooth.shape)


def along_y(mine, other, out, planes):
    sub = lax.axis_index("sub")
    run = lax.axis_index("run")
    row = lax.broadcasted_iota(jnp.int32, (32, 32), 0)
    col = lax.broadcasted_iota(jnp.int32, (32, 32), 1)

    def band(offset):
        gap = jnp.abs(col + offset - row).astype(jnp.float32)
        return jnp.where(gap <= REACH, NORM * jnp.exp(gap * (-1.0 / DECAY)), 0.0)

    near = band(0)
    far = band(32 - 64 * sub)
    upward, downward = 0.0, 0.0
    for k in range(8):
        value = jnp.dot(
            near, mine[k], precision=lax.Precision.HIGHEST, preferred_element_type=jnp.float32
        ) + jnp.dot(
            far, other[k], precision=lax.Precision.HIGHEST, preferred_element_type=jnp.float32
        )
        out[k] = value
        upward = upward + math.exp(-(7 - k) / DECAY) * value
        downward = downward + math.exp(-k / DECAY) * value
    for k in range(planes.shape[0]):
        planes[k] = jnp.where(k > run, upward, downward)


def along_z(count, mine, planes, below, above, occupancy, stimulus, row_out):
    run = lax.axis_index("run")
    span = REACH // 8
    lower, upper = 0.0, 0.0
    for o in range(1, span):
        scale = math.exp(-8.0 * (o - 1) / DECAY)
        at = jnp.maximum(run - o, 0)
        lower = lower + jnp.where(run - o >= 0, scale * planes[at], 0.0)
        at = jnp.minimum(run + o, count - 1)
        upper = upper + jnp.where(run + o < count, scale * planes[at], 0.0)
    has_below = run - span >= 0
    has_above = run + span < count
    total, bone = 0.0, 0.0
    for i in range(8):
        value = weight(i + 1) * lower + weight(8 - i) * upper
        far_below, far_above = 0.0, 0.0
        for j in range(8):
            value = value + weight(abs(i - j)) * mine[j]
            if j >= i:
                far_below = far_below + weight(i - j + REACH) * below[j]
            if j <= i:
                far_above = far_above + weight(j - i + REACH) * above[j]
        value = value + jnp.where(has_below, far_below, 0.0) + jnp.where(has_above, far_above, 0.0)
        stimulus[i] = value
        share = occupancy[i].astype(jnp.float32)
        total = total + share * value
        bone = bone + share
    lane = lax.broadcasted_iota(jnp.int32, (1, 128), 1)
    line = jnp.where(lane == 0, whole(total), jnp.where(lane == 1, whole(bone), 0.0))
    row_out[...] = jnp.broadcast_to(line, row_out.shape)


def remodel(lines, stimulus, occupancy, density, out):
    line = jnp.sum(lines[...], axis=0, keepdims=True)
    mean = jnp.broadcast_to(pick(line, 0) / pick(line, 1), stimulus.shape[1:])
    for k in range(8):
        rho = density[k]
        updated = jnp.minimum(rho * (1.0 + RATE * jnp.tanh(SLOPE * (stimulus[k] / mean - 1.0))), 1.0)
        out[k] = jnp.where(occupancy[k] == 1, updated, rho)


def everyone(lines):
    return lax.all_to_all(lines, PAIR, 0, 0, tiled=True)


def local(load, guess, occupancy, density):
    count = lax.axis_size("run")
    members = count * lax.axis_size("sub")
    block = density.shape
    swap = [(0, 1), (1, 0)]
    side = lax.ppermute(side_rows(load, guess, occupancy, density), "sub", swap)
    wide = (3, 8, ROWS, 128)
    kept = call(
        inner,
        [
            (10, ROWS, 128), (8, ROWS, 128), wide, wide,
            (8, ROWS, 128), (7, ROWS, 128), (ROWS, 128),
        ],
        [load, guess, occupancy, density, side],
        [(6, 8, 48, 128), (6, 8, 48, 128), (6, 8, 48, 128)],
    )
    up, down, guess_w = kept[:3]
    low = lax.ppermute(up, "run", [(i, i + 1) for i in range(count - 1)])
    high = lax.ppermute(down, "run", [(i + 1, i) for i in range(count - 1)])
    lines, first, second = call(
        krylov,
        [(members, 128), (3, 11, ROWS, 128), (3, 9, ROWS, 128)],
        [*kept, low, high],
        [
            (6, 11, 48, 128), (6, 11, 48, 128), (6, 11, 48, 128),
            (10, ROWS, 128), (9, ROWS, 128), (4, ROWS, 128),
        ],
    )
    lines = everyone(lines)
    displacement, smooth = call(
        energies,
        [guess.shape, block],
        [lines, guess_w, low, first, second, occupancy, density],
        [(6, 9, 48, 128), (3, ROWS, 128), (8, ROWS, 128)],
    )
    other = lax.ppermute(smooth, "sub", swap)
    smooth, planes = call(along_y, [block, (count, 32, 128)], [smooth, other])
    span = REACH // 8
    rise = [(i, i + span) for i in range(count - span)]
    fall = [(i + span, i) for i in range(count - span)]
    if count <= 2 * span:
        below = above = lax.ppermute(smooth, "run", rise + fall)
    else:
        below = lax.ppermute(smooth, "run", rise)
        above = lax.ppermute(smooth, "run", fall)
    planes = lax.all_to_all(planes, "run", 0, 0, tiled=True)
    stimulus, lines = call(
        functools.partial(along_z, count),
        [block, (members, 128)],
        [smooth, planes, below, above, occupancy],
    )
    lines = everyone(lines)
    (new_density,) = call(remodel, [block], [lines, stimulus, occupancy, density])
    return displacement, new_density


def solution(mesh):
    field = P(None, ("grp", "run"), "sub", None)
    cells = P(("grp", "run"), "sub", None)
    return jax.shard_map(
        local,
        mesh=mesh,
        in_specs=(field, field, cells, cells),
        out_specs=(field, cells),
        check_vma=False,
    )
```

```python
import functools
import math

import jax
import jax.numpy as jnp
from jax import lax
from jax.experimental import pallas as pl
from jax.experimental.pallas import tpu as pltpu
from jax.sharding import PartitionSpec as P

REACH = 32
POISSON = 0.3
MARROW = 0.05
RATE = 0.5
SLOPE = 4.0
DECAY = REACH / 4.0

LAME = POISSON / ((1.0 + POISSON) * (1.0 - 2.0 * POISSON)) / 16.0
SHEAR = 0.5 / (1.0 + POISSON) / 16.0
ENTRY = 16.0 * (LAME + 4.0 * SHEAR) / 9.0
NORM = 1.0 / sum(math.exp(-abs(k) / DECAY) for k in range(-REACH, REACH + 1))

ROWS = 40
PAIR = ("run", "sub")

VMEM = pl.BlockSpec(memory_space=pltpu.VMEM)


def weight(distance):
    return NORM * math.exp(-distance / DECAY)


def call(kernel, outs, ins, scratch=(), flops=None):
    cost = None
    if flops is not None:
        cost = pl.CostEstimate(flops=flops, bytes_accessed=2**20, transcendentals=0)
    return pl.pallas_call(
        kernel,
        out_shape=[jax.ShapeDtypeStruct(s, jnp.float32) for s in outs],
        in_specs=[VMEM] * len(ins),
        out_specs=[VMEM] * len(outs),
        scratch_shapes=[pltpu.VMEM(s, jnp.float32) for s in scratch],
        compiler_params=pltpu.CompilerParams(vmem_limit_bytes=40 * 1024 * 1024),
        cost_estimate=cost,
    )(*ins)


def lane_right(block):
    lane = lax.broadcasted_iota(jnp.int32, block.shape, 1)
    return jnp.where(lane == 0, 0.0, pltpu.roll(block, 1, 1))


def lane_left(block):
    lane = lax.broadcasted_iota(jnp.int32, block.shape, 1)
    return jnp.where(lane == block.shape[1] - 1, 0.0, pltpu.roll(block, block.shape[1] - 1, 1))


def row_down(block):
    row = lax.broadcasted_iota(jnp.int32, block.shape, 0)
    return jnp.where(row == block.shape[0] - 1, 0.0, pltpu.roll(block, block.shape[0] - 1, 0))


def stiff(occupancy, density):
    return jnp.where(occupancy == 1, density * density, MARROW)


def enter(pair, k, c, field):
    other = lane_right(field)
    pair[2 * c, k, 8:48] = field + other
    pair[2 * c + 1, k, 8:48] = field - other


def clear(pair):
    for m in range(6):
        for k in range(pair.shape[1]):
            pair[m, k, 0:8] = jnp.zeros((8, 128), jnp.float32)


def plane_modes(pair, k, tile):
    out = [None] * 12
    for c in range(3):
        for x in range(2):
            here = pair[2 * c + x, k, 8 + 8 * tile : 16 + 8 * tile]
            above = pair[2 * c + x, k, 7 + 8 * tile : 15 + 8 * tile]
            out[4 * c + x] = here + above
            out[4 * c + 2 + x] = here - above
    return out


def steps(count, body, carry):
    def turn(k, carry):
        return body(2 * k + 1, body(2 * k, carry))

    carry = lax.fori_loop(0, count // 2, turn, carry)
    return body(count - 1, carry) if count % 2 else carry


def march(pair, start, count, mod, near, far, to):
    for tile in range(ROWS // 8):
        rows = slice(8 * tile, 8 * tile + 8)

        def leave(k, totals):
            for c in range(3):
                for x in range(2):
                    s, d = totals[4 * c + x], totals[4 * c + 2 + x]
                    near[2 * c + x, k, rows] = s + d
                    far[2 * c + x, k, rows] = s - d

        def body(k, carry):
            low, kept = carry
            high = plane_modes(pair, start + k + 1, tile)
            g = stress(modes_of(low, high), mod(k, rows))
            totals, after = [None] * 12, [None] * 12
            for c in range(3):
                for m in range(4):
                    d = g[c][4 + m]
                    at = 4 * c + m
                    if m:
                        s = g[c][m]
                        totals[at] = kept[at] + (s - d)
                        after[at] = s + d
                    else:
                        totals[at] = kept[at] - d
                        after[at] = d
            leave(to + k, totals)
            return high, after

        zeros = [jnp.zeros((8, 128), jnp.float32)] * 12
        _, kept = steps(count, body, (plane_modes(pair, start, tile), zeros))
        leave(to + count, kept)


def image(near, far, k, c):
    columns = [
        near[2 * c + x, k, 0:ROWS] + far[2 * c + x, k, 1 : ROWS + 1] for x in range(2)
    ]
    return columns[0] + columns[1] + lane_left(columns[0] - columns[1])


def energy_march(pair, count, use):
    for tile in range(ROWS // 8):

        def body(k, low):
            high = plane_modes(pair, k + 1, tile)
            use(k, tile, quadratic(modes_of(low, high)))
            return high

        steps(count, body, plane_modes(pair, 0, tile))


def inverted(low, high):
    t = low + high
    t = t + row_down(t)
    t = (t + lane_left(t)) * ENTRY
    return jnp.where(t > 0.0, 1.0 / jnp.where(t > 0.0, t, 1.0), 0.0)


def whole(block):
    return jnp.sum(jnp.sum(block, axis=0, keepdims=True), axis=1, keepdims=True)


def modes_of(low, high):
    out = []
    for c in range(3):
        modes = [None] * 8
        for m in range(4):
            if m:
                modes[m] = high[4 * c + m] + low[4 * c + m]
            modes[4 + m] = high[4 * c + m] - low[4 * c + m]
        out.append(modes)
    return out


X, Y, Z = 1, 2, 4


def stress(u, mod):
    g = [[None] * 8 for _ in range(3)]
    bulk, rigid = mod * LAME, mod * SHEAR
    twice = rigid + rigid
    bulk3, rigid3 = mod * (LAME / 3.0), mod * (SHEAR / 3.0)
    last = mod * ((LAME + 4.0 * SHEAR) / 9.0)
    t = (u[0][X] + u[1][Y] + u[2][Z]) * bulk
    g[0][X] = t + u[0][X] * twice
    g[1][Y] = t + u[1][Y] * twice
    g[2][Z] = t + u[2][Z] * twice
    g[0][Y] = g[1][X] = (u[0][Y] + u[1][X]) * rigid
    g[0][Z] = g[2][X] = (u[0][Z] + u[2][X]) * rigid
    g[1][Z] = g[2][Y] = (u[1][Z] + u[2][Y]) * rigid
    for (c, m), (d, n) in (
        ((1, X | Y), (2, X | Z)),
        ((0, X | Y), (2, Y | Z)),
        ((0, X | Z), (1, Y | Z)),
    ):
        s = (u[c][m] + u[d][n]) * bulk3
        g[c][m] = s + u[c][m] * rigid
        g[d][n] = s + u[d][n] * rigid
    s = u[0][Y | Z] + u[1][X | Z] + u[2][X | Y]
    g[0][Y | Z] = (s + u[0][Y | Z]) * rigid3
    g[1][X | Z] = (s + u[1][X | Z]) * rigid3
    g[2][X | Y] = (s + u[2][X | Y]) * rigid3
    for c in range(3):
        g[c][7] = u[c][7] * last
    return g


def quadratic(u):
    def sq(v):
        return v * v

    t = sq(u[0][X] + u[1][Y] + u[2][Z])
    r2 = sq(u[0][X]) + sq(u[1][Y]) + sq(u[2][Z])
    r = sq(u[0][Y] + u[1][X]) + sq(u[0][Z] + u[2][X]) + sq(u[1][Z] + u[2][Y])
    t3 = 0.0
    for (c, m), (d, n) in (
        ((1, X | Y), (2, X | Z)),
        ((0, X | Y), (2, Y | Z)),
        ((0, X | Z), (1, Y | Z)),
    ):
        t3 = t3 + sq(u[c][m] + u[d][n])
        r = r + (sq(u[c][m]) + sq(u[d][n]))
    p, q, s = u[0][Y | Z], u[1][X | Z], u[2][X | Y]
    r3 = sq(p + q) + sq(p + s) + sq(q + s)
    last = sq(u[0][7]) + sq(u[1][7]) + sq(u[2][7])
    return (
        LAME * (t + t3 * (1.0 / 3.0))
        + SHEAR * (r + r2 + r2 + r3 * (1.0 / 3.0))
        + ((LAME + 4.0 * SHEAR) / 9.0) * last
    )


def side_rows(load, guess, occupancy, density):
    sub = lax.axis_index("sub")
    flat = lambda part: part.reshape((-1,) + part.shape[-2:])
    near = lambda part: jnp.where(sub == 0, part[..., 24:32, :], part[..., 0:8, :])
    return jnp.concatenate(
        [flat(near(guess)), flat(near(load)), stiff(near(occupancy), near(density))], axis=0
    )


def inner(
    load, guess, bone, density, side, up, down, guess_w, first_w, mod_w, inverse, square,
    pair, near, far,
):
    sub = lax.axis_index("sub")
    own = pl.ds(pl.multiple_of(8 * sub, 8), 32)
    rest = pl.ds(pl.multiple_of(32 * (1 - sub), 8), 8)
    clear(pair)
    far[:, :, ROWS : ROWS + 8] = jnp.zeros((6, 8, 8, 128), jnp.float32)
    for k in range(8):
        mod_w[k, own] = stiff(bone[k], density[k])
        mod_w[k, rest] = side[48 + k]
        for c in range(3):
            guess_w[c, k, own] = guess[c, k]
            guess_w[c, k, rest] = side[8 * c + k]
            first_w[c, k, own] = load[c, k]
            first_w[c, k, rest] = side[24 + 8 * c + k]

    def prepare(k, _):
        for c in range(3):
            enter(pair, k, c, guess_w[c, k])
        return 0

    lax.fori_loop(0, 8, prepare, 0)
    for k in range(7):
        inverse[k] = inverted(mod_w[k], mod_w[k + 1])
    march(pair, 0, 7, lambda k, rows: mod_w[k + 1, rows], near, far, 0)
    square[...] = jnp.zeros_like(square)

    def settle(k, _):
        for c in range(3):
            residual = first_w[c, k] - image(near, far, k, c)
            z = residual * inverse[k]
            first_w[c, k] = z
            square[...] += residual * z
        return 0

    for c in range(3):
        down[3 + c] = first_w[c, 0] - image(near, far, 0, c)
        up[3 + c] = first_w[c, 7] - image(near, far, 7, c)
    lax.fori_loop(1, 7, settle, 0)
    for c in range(3):
        down[c] = guess_w[c, 0]
        up[c] = guess_w[c, 7]
        up[6 + c] = first_w[c, 6]
    up[9] = mod_w[7]
    down[6] = mod_w[0]
    down[7] = inverse[0]


def krylov(
    up, down, guess_w, first_w, mod_w, inverse, square, low, high, row_out, first, second,
    pair, near, far, mods, inverses, sums,
):
    sub = lax.axis_index("sub")
    run = lax.axis_index("run")
    own = pl.ds(pl.multiple_of(8 * sub, 8), 32)
    clear(pair)
    far[:, :, ROWS : ROWS + 8] = jnp.zeros((6, 11, 8, 128), jnp.float32)
    mods[0] = low[9]
    mods[9] = high[6]
    for k in range(8):
        mods[1 + k] = mod_w[k]
    inverses[0] = jnp.where(run > 0, inverted(low[9], mod_w[0]), 0.0)
    for k in range(7):
        inverses[1 + k] = inverse[k]
    inverses[8] = inverted(mod_w[7], high[6])

    for c in range(3):
        enter(pair, 0, c, low[c])
        enter(pair, 1, c, guess_w[c, 0])
        enter(pair, 2, c, guess_w[c, 7])
        enter(pair, 3, c, high[c])
    march(pair, 0, 1, lambda k, rows: mods[1, rows], near, far, 0)
    march(pair, 2, 1, lambda k, rows: mods[9, rows], near, far, 2)
    begun = (low, down, up, high)
    invert = (inverses[0], inverses[1], inverses[8], high[7])
    sums[...] = jnp.zeros_like(sums)
    dot = square[...]
    for c in range(3):
        values = []
        for k in range(4):
            residual = begun[k][3 + c] - image(near, far, k, c)
            z = residual * invert[k]
            values.append(z)
            if k in (1, 2):
                dot = dot + residual * z
        first[c, 0] = low[6 + c]
        first[c, 1] = values[0]
        first[c, 2] = values[1]
        for k in range(1, 7):
            first[c, 2 + k] = first_w[c, k]
        first[c, 9] = values[2]
        first[c, 10] = values[3]
    sums[0] = dot

    def prepare(k, _):
        for c in range(3):
            enter(pair, k, c, first[c, k])
        return 0

    lax.fori_loop(0, 11, prepare, 0)
    march(pair, 0, 10, lambda k, rows: mods[k, rows], near, far, 0)

    def settle(k, _):
        dot, cross = 0.0, 0.0
        for c in range(3):
            w = image(near, far, k + 1, c)
            s = w * inverses[k]
            second[c, k] = s
            enter(pair, k, c, s)
            dot = dot + w * first[c, k + 1]
            cross = cross + w * s

        @pl.when(k >= 1)
        def _():
            sums[1] += dot
            sums[2] += cross

        return 0

    lax.fori_loop(0, 9, settle, 0)

    def use(k, tile, value):
        rows = slice(8 * tile, 8 * tile + 8)
        sums[3, rows] += value * mods[k + 1, rows]

    energy_march(pair, 8, use)
    lane = lax.broadcasted_iota(jnp.int32, (1, 128), 1)
    line = jnp.zeros((1, 128), jnp.float32)
    for k in range(4):
        line = jnp.where(lane == k, whole(sums[k, own]), line)
    row_out[...] = jnp.broadcast_to(line, row_out.shape)


def pick(line, k):
    lane = lax.broadcasted_iota(jnp.int32, line.shape, 1)
    return jnp.sum(jnp.where(lane == k, line, 0.0), axis=1, keepdims=True)


def energies(
    lines, guess_w, low, first, second, occupancy, density, out, smooth, pair, field, specific
):
    sub = lax.axis_index("sub")
    own = pl.ds(pl.multiple_of(8 * sub, 8), 32)
    line = jnp.sum(lines[...], axis=0, keepdims=True)
    a, b, c, e = (pick(line, k) for k in range(4))
    alpha = a / b
    fresh = alpha * alpha * c - a
    beta = fresh / a
    square = alpha * alpha * e - (1.0 + beta) * (1.0 + beta) * b
    after = fresh / square
    p = jnp.broadcast_to(alpha + after * (1.0 + beta), (ROWS, 128))
    q = jnp.broadcast_to(-after * alpha, (ROWS, 128))
    clear(pair)
    for c in range(3):
        enter(pair, 0, c, low[c] + p * first[c, 1] + q * second[c, 0])

    def advance(k, _):
        for c in range(3):
            value = guess_w[c, k] + p * first[c, k + 2] + q * second[c, k + 1]
            field[c] = value
            enter(pair, k + 1, c, value)
        for c in range(3):
            out[c, k] = field[c, own]
        return 0

    lax.fori_loop(0, 8, advance, 0)

    def use(k, tile, value):
        specific[k, 8 * tile : 8 * tile + 8] = value

    energy_march(pair, 8, use)
    parts = []
    for k in range(8):
        rho = density[k]
        share = jnp.where(occupancy[k] == 1, rho * rho / rho, 0.0)
        parts.append(0.5 * share * specific[k, own])
    row = lax.broadcasted_iota(jnp.int32, (128, 128), 0)
    col = lax.broadcasted_iota(jnp.int32, (128, 128), 1)
    gap = jnp.abs(row - col).astype(jnp.float32)
    band = jnp.where(gap <= REACH, NORM * jnp.exp(gap * (-1.0 / DECAY)), 0.0)
    smooth[...] = jnp.dot(
        jnp.concatenate(parts, axis=0), band,
        precision=lax.Precision.HIGHEST, preferred_element_type=jnp.float32,
    ).reshape(smooth.shape)


def along_y(mine, other, out, planes):
    sub = lax.axis_index("sub")
    run = lax.axis_index("run")
    row = lax.broadcasted_iota(jnp.int32, (32, 32), 0)
    col = lax.broadcasted_iota(jnp.int32, (32, 32), 1)

    def band(offset):
        gap = jnp.abs(col + offset - row).astype(jnp.float32)
        return jnp.where(gap <= REACH, NORM * jnp.exp(gap * (-1.0 / DECAY)), 0.0)

    near = band(0)
    far = band(32 - 64 * sub)
    upward, downward = 0.0, 0.0
    for k in range(8):
        value = jnp.dot(
            near, mine[k], precision=lax.Precision.HIGHEST, preferred_element_type=jnp.float32
        ) + jnp.dot(
            far, other[k], precision=lax.Precision.HIGHEST, preferred_element_type=jnp.float32
        )
        out[k] = value
        upward = upward + math.exp(-(7 - k) / DECAY) * value
        downward = downward + math.exp(-k / DECAY) * value
    for k in range(planes.shape[0]):
        planes[k] = jnp.where(k > run, upward, downward)


def near_z(count, planes, i):
    run = lax.axis_index("run")
    lower, upper = 0.0, 0.0
    for o in range(1, REACH // 8):
        scale = math.exp(-8.0 * (o - 1) / DECAY)
        at = jnp.maximum(run - o, 0)
        lower = lower + jnp.where(run - o >= 0, scale * planes[at, 0:32], 0.0)
        at = jnp.minimum(run + o, count - 1)
        upper = upper + jnp.where(run + o < count, scale * planes[at, 0:32], 0.0)
    return weight(i + 1) * lower + weight(8 - i) * upper


def far_z(count, mine, below, above):
    run = lax.axis_index("run")
    has_below = run - REACH // 8 >= 0
    has_above = run + REACH // 8 < count
    for i in range(8):
        value, far_below, far_above = 0.0, 0.0, 0.0
        for j in range(8):
            value = value + weight(abs(i - j)) * mine(j)
            if j >= i:
                far_below = far_below + weight(i - j + REACH) * below(j)
            if j <= i:
                far_above = far_above + weight(j - i + REACH) * above(j)
        yield value + jnp.where(has_below, far_below, 0.0) + jnp.where(has_above, far_above, 0.0)


def partial_z(count, mine, below, above, out):
    blocks = [lambda j, ref=ref: ref[j] for ref in (mine, below, above)]
    for i, value in enumerate(far_z(count, *blocks)):
        out[i] = value


def along_z(count, part, planes, occupancy, stimulus, row_out):
    total, bone = 0.0, 0.0
    for i in range(8):
        value = part[i] + near_z(count, planes, i)
        stimulus[i] = value
        share = occupancy[i].astype(jnp.float32)
        total = total + share * value
        bone = bone + share
    lane = lax.broadcasted_iota(jnp.int32, (1, 128), 1)
    line = jnp.where(lane == 0, whole(total), jnp.where(lane == 1, whole(bone), 0.0))
    row_out[...] = jnp.broadcast_to(line, row_out.shape)


def remodel(lines, stimulus, occupancy, density, out):
    line = jnp.sum(lines[...], axis=0, keepdims=True)
    mean = jnp.broadcast_to(pick(line, 0) / pick(line, 1), stimulus.shape[1:])
    for k in range(8):
        rho = density[k]
        updated = jnp.minimum(rho * (1.0 + RATE * jnp.tanh(SLOPE * (stimulus[k] / mean - 1.0))), 1.0)
        out[k] = jnp.where(occupancy[k] == 1, updated, rho)


def everyone(lines):
    return lax.all_to_all(lines, PAIR, 0, 0, tiled=True)


def local(load, guess, occupancy, density):
    count = lax.axis_size("run")
    members = count * lax.axis_size("sub")
    block = density.shape
    swap = [(0, 1), (1, 0)]
    side = lax.ppermute(side_rows(load, guess, occupancy, density), "sub", swap)
    wide = (3, 8, ROWS, 128)
    kept = call(
        inner,
        [
            (10, ROWS, 128), (8, ROWS, 128), wide, wide,
            (8, ROWS, 128), (7, ROWS, 128), (ROWS, 128),
        ],
        [load, guess, occupancy, density, side],
        [(6, 8, 48, 128), (6, 8, 48, 128), (6, 8, 48, 128)],
    )
    up, down, guess_w = kept[:3]
    low = lax.ppermute(up, "run", [(i, i + 1) for i in range(count - 1)])
    high = lax.ppermute(down, "run", [(i + 1, i) for i in range(count - 1)])
    lines, first, second = call(
        krylov,
        [(members, 128), (3, 11, ROWS, 128), (3, 9, ROWS, 128)],
        [*kept, low, high],
        [
            (6, 11, 48, 128), (6, 11, 48, 128), (6, 11, 48, 128),
            (10, ROWS, 128), (9, ROWS, 128), (4, ROWS, 128),
        ],
    )
    lines = everyone(lines)
    displacement, smooth = call(
        energies,
        [guess.shape, block],
        [lines, guess_w, low, first, second, occupancy, density],
        [(6, 9, 48, 128), (3, ROWS, 128), (8, ROWS, 128)],
    )
    other = lax.ppermute(smooth, "sub", swap)
    smooth, planes = call(along_y, [block, (count, 32, 128)], [smooth, other])
    below, above = far_slabs(smooth)
    planes = lax.all_to_all(planes, "run", 0, 0, tiled=True)
    (part,) = call(
        functools.partial(partial_z, count), [block], [smooth, below, above], flops=10**10
    )
    stimulus, lines = call(
        functools.partial(along_z, count), [block, (members, 128)], [part, planes, occupancy]
    )
    lines = everyone(lines)
    (new_density,) = call(remodel, [block], [lines, stimulus, occupancy, density])
    return displacement, new_density


def far_slabs(block):
    count = lax.axis_size("run")
    span = REACH // block.shape[0]
    rise = [(i, i + span) for i in range(count - span)]
    fall = [(i + span, i) for i in range(count - span)]
    if count <= 2 * span:
        both = lax.ppermute(block, "run", rise + fall)
        return both, both
    return lax.ppermute(block, "run", rise), lax.ppermute(block, "run", fall)


def solution(mesh):
    field = P(None, ("grp", "run"), "sub", None)
    cells = P(("grp", "run"), "sub", None)
    return jax.shard_map(
        local,
        mesh=mesh,
        in_specs=(field, field, cells, cells),
        out_specs=(field, cells),
        check_vma=False,
    )
```

```python
import functools
import math

import jax
import jax.numpy as jnp
from jax import lax
from jax.experimental import pallas as pl
from jax.experimental.pallas import tpu as pltpu
from jax.sharding import PartitionSpec as P

REACH = 32
POISSON = 0.3
MARROW = 0.05
RATE = 0.5
SLOPE = 4.0
DECAY = REACH / 4.0

LAME = POISSON / ((1.0 + POISSON) * (1.0 - 2.0 * POISSON)) / 16.0
SHEAR = 0.5 / (1.0 + POISSON) / 16.0
ENTRY = 16.0 * (LAME + 4.0 * SHEAR) / 9.0
NORM = 1.0 / sum(math.exp(-abs(k) / DECAY) for k in range(-REACH, REACH + 1))

ROWS = 40
PAIR = ("run", "sub")

VMEM = pl.BlockSpec(memory_space=pltpu.VMEM)


def weight(distance):
    return NORM * math.exp(-distance / DECAY)


def call(kernel, outs, ins, scratch=(), flops=None):
    cost = None
    if flops is not None:
        cost = pl.CostEstimate(flops=flops, bytes_accessed=2**20, transcendentals=0)
    return pl.pallas_call(
        kernel,
        out_shape=[jax.ShapeDtypeStruct(s, jnp.float32) for s in outs],
        in_specs=[VMEM] * len(ins),
        out_specs=[VMEM] * len(outs),
        scratch_shapes=[pltpu.VMEM(s, jnp.float32) for s in scratch],
        compiler_params=pltpu.CompilerParams(vmem_limit_bytes=40 * 1024 * 1024),
        cost_estimate=cost,
    )(*ins)


def lane_right(block):
    lane = lax.broadcasted_iota(jnp.int32, block.shape, 1)
    return jnp.where(lane == 0, 0.0, pltpu.roll(block, 1, 1))


def lane_left(block):
    lane = lax.broadcasted_iota(jnp.int32, block.shape, 1)
    return jnp.where(lane == block.shape[1] - 1, 0.0, pltpu.roll(block, block.shape[1] - 1, 1))


def row_down(block):
    row = lax.broadcasted_iota(jnp.int32, block.shape, 0)
    return jnp.where(row == block.shape[0] - 1, 0.0, pltpu.roll(block, block.shape[0] - 1, 0))


def stiff(occupancy, density):
    return jnp.where(occupancy == 1, density * density, MARROW)


def enter(pair, k, c, field):
    other = lane_right(field)
    pair[2 * c, k, 8:48] = field + other
    pair[2 * c + 1, k, 8:48] = field - other


def clear(pair):
    for m in range(6):
        for k in range(pair.shape[1]):
            pair[m, k, 0:8] = jnp.zeros((8, 128), jnp.float32)


def plane_modes(pair, k, tile):
    out = [None] * 12
    for c in range(3):
        for x in range(2):
            here = pair[2 * c + x, k, 8 + 8 * tile : 16 + 8 * tile]
            above = pair[2 * c + x, k, 7 + 8 * tile : 15 + 8 * tile]
            out[4 * c + x] = here + above
            out[4 * c + 2 + x] = here - above
    return out


def steps(count, body, carry):
    def turn(k, carry):
        return body(2 * k + 1, body(2 * k, carry))

    carry = lax.fori_loop(0, count // 2, turn, carry)
    return body(count - 1, carry) if count % 2 else carry


def march(pair, start, count, mod, near, far, to):
    for tile in range(ROWS // 8):
        rows = slice(8 * tile, 8 * tile + 8)

        def leave(k, totals):
            for c in range(3):
                for x in range(2):
                    s, d = totals[4 * c + x], totals[4 * c + 2 + x]
                    near[2 * c + x, k, rows] = s + d
                    far[2 * c + x, k, rows] = s - d

        def body(k, carry):
            low, kept = carry
            high = plane_modes(pair, start + k + 1, tile)
            g = stress(modes_of(low, high), mod(k, rows))
            totals, after = [None] * 12, [None] * 12
            for c in range(3):
                for m in range(4):
                    d = g[c][4 + m]
                    at = 4 * c + m
                    if m:
                        s = g[c][m]
                        totals[at] = kept[at] + (s - d)
                        after[at] = s + d
                    else:
                        totals[at] = kept[at] - d
                        after[at] = d
            leave(to + k, totals)
            return high, after

        zeros = [jnp.zeros((8, 128), jnp.float32)] * 12
        _, kept = steps(count, body, (plane_modes(pair, start, tile), zeros))
        leave(to + count, kept)


def image(near, far, k, c):
    columns = [
        near[2 * c + x, k, 0:ROWS] + far[2 * c + x, k, 1 : ROWS + 1] for x in range(2)
    ]
    return columns[0] + columns[1] + lane_left(columns[0] - columns[1])


def energy_march(pair, count, use):
    for tile in range(ROWS // 8):

        def body(k, low):
            high = plane_modes(pair, k + 1, tile)
            use(k, tile, quadratic(modes_of(low, high)))
            return high

        steps(count, body, plane_modes(pair, 0, tile))


def inverted(low, high):
    t = low + high
    t = t + row_down(t)
    t = (t + lane_left(t)) * ENTRY
    return jnp.where(t > 0.0, 1.0 / jnp.where(t > 0.0, t, 1.0), 0.0)


def whole(block):
    return jnp.sum(jnp.sum(block, axis=0, keepdims=True), axis=1, keepdims=True)


def modes_of(low, high):
    out = []
    for c in range(3):
        modes = [None] * 8
        for m in range(4):
            if m:
                modes[m] = high[4 * c + m] + low[4 * c + m]
            modes[4 + m] = high[4 * c + m] - low[4 * c + m]
        out.append(modes)
    return out


X, Y, Z = 1, 2, 4


def stress(u, mod):
    g = [[None] * 8 for _ in range(3)]
    bulk, rigid = mod * LAME, mod * SHEAR
    twice = rigid + rigid
    bulk3, rigid3 = mod * (LAME / 3.0), mod * (SHEAR / 3.0)
    last = mod * ((LAME + 4.0 * SHEAR) / 9.0)
    t = (u[0][X] + u[1][Y] + u[2][Z]) * bulk
    g[0][X] = t + u[0][X] * twice
    g[1][Y] = t + u[1][Y] * twice
    g[2][Z] = t + u[2][Z] * twice
    g[0][Y] = g[1][X] = (u[0][Y] + u[1][X]) * rigid
    g[0][Z] = g[2][X] = (u[0][Z] + u[2][X]) * rigid
    g[1][Z] = g[2][Y] = (u[1][Z] + u[2][Y]) * rigid
    for (c, m), (d, n) in (
        ((1, X | Y), (2, X | Z)),
        ((0, X | Y), (2, Y | Z)),
        ((0, X | Z), (1, Y | Z)),
    ):
        s = (u[c][m] + u[d][n]) * bulk3
        g[c][m] = s + u[c][m] * rigid
        g[d][n] = s + u[d][n] * rigid
    s = u[0][Y | Z] + u[1][X | Z] + u[2][X | Y]
    g[0][Y | Z] = (s + u[0][Y | Z]) * rigid3
    g[1][X | Z] = (s + u[1][X | Z]) * rigid3
    g[2][X | Y] = (s + u[2][X | Y]) * rigid3
    for c in range(3):
        g[c][7] = u[c][7] * last
    return g


def quadratic(u):
    def sq(v):
        return v * v

    t = sq(u[0][X] + u[1][Y] + u[2][Z])
    r2 = sq(u[0][X]) + sq(u[1][Y]) + sq(u[2][Z])
    r = sq(u[0][Y] + u[1][X]) + sq(u[0][Z] + u[2][X]) + sq(u[1][Z] + u[2][Y])
    t3 = 0.0
    for (c, m), (d, n) in (
        ((1, X | Y), (2, X | Z)),
        ((0, X | Y), (2, Y | Z)),
        ((0, X | Z), (1, Y | Z)),
    ):
        t3 = t3 + sq(u[c][m] + u[d][n])
        r = r + (sq(u[c][m]) + sq(u[d][n]))
    p, q, s = u[0][Y | Z], u[1][X | Z], u[2][X | Y]
    r3 = sq(p + q) + sq(p + s) + sq(q + s)
    last = sq(u[0][7]) + sq(u[1][7]) + sq(u[2][7])
    return (
        LAME * (t + t3 * (1.0 / 3.0))
        + SHEAR * (r + r2 + r2 + r3 * (1.0 / 3.0))
        + ((LAME + 4.0 * SHEAR) / 9.0) * last
    )


def side_rows(load, guess, occupancy, density):
    sub = lax.axis_index("sub")
    flat = lambda part: part.reshape((-1,) + part.shape[-2:])
    near = lambda part: jnp.where(sub == 0, part[..., 24:32, :], part[..., 0:8, :])
    return jnp.concatenate(
        [flat(near(guess)), flat(near(load)), stiff(near(occupancy), near(density))], axis=0
    )


def inner(
    load, guess, bone, density, side, up, down, guess_w, first_w, mod_w, inverse, square,
    pair, near, far,
):
    sub = lax.axis_index("sub")
    own = pl.ds(pl.multiple_of(8 * sub, 8), 32)
    rest = pl.ds(pl.multiple_of(32 * (1 - sub), 8), 8)
    clear(pair)
    far[:, :, ROWS : ROWS + 8] = jnp.zeros((6, 8, 8, 128), jnp.float32)
    for k in range(8):
        mod_w[k, own] = stiff(bone[k], density[k])
        mod_w[k, rest] = side[48 + k]
        for c in range(3):
            guess_w[c, k, own] = guess[c, k]
            guess_w[c, k, rest] = side[8 * c + k]
            first_w[c, k, own] = load[c, k]
            first_w[c, k, rest] = side[24 + 8 * c + k]

    def prepare(k, _):
        for c in range(3):
            enter(pair, k, c, guess_w[c, k])
        return 0

    lax.fori_loop(0, 8, prepare, 0)
    for k in range(7):
        inverse[k] = inverted(mod_w[k], mod_w[k + 1])
    march(pair, 0, 7, lambda k, rows: mod_w[k + 1, rows], near, far, 0)
    square[...] = jnp.zeros_like(square)

    def settle(k, _):
        for c in range(3):
            residual = first_w[c, k] - image(near, far, k, c)
            z = residual * inverse[k]
            first_w[c, k] = z
            square[...] += residual * z
        return 0

    for c in range(3):
        down[3 + c] = first_w[c, 0] - image(near, far, 0, c)
        up[3 + c] = first_w[c, 7] - image(near, far, 7, c)
    lax.fori_loop(1, 7, settle, 0)
    for c in range(3):
        down[c] = guess_w[c, 0]
        up[c] = guess_w[c, 7]
        up[6 + c] = first_w[c, 6]
    up[9] = mod_w[7]
    down[6] = mod_w[0]
    down[7] = inverse[0]


def krylov(
    up, down, guess_w, first_w, mod_w, inverse, square, low, high, planes_in, planes, first, second,
    pair, near, far, mods, inverses, sums,
):
    sub = lax.axis_index("sub")
    run = lax.axis_index("run")
    own = pl.ds(pl.multiple_of(8 * sub, 8), 32)
    clear(pair)
    far[:, :, ROWS : ROWS + 8] = jnp.zeros((6, 11, 8, 128), jnp.float32)
    mods[0] = low[9]
    mods[9] = high[6]
    for k in range(8):
        mods[1 + k] = mod_w[k]
    inverses[0] = jnp.where(run > 0, inverted(low[9], mod_w[0]), 0.0)
    for k in range(7):
        inverses[1 + k] = inverse[k]
    inverses[8] = inverted(mod_w[7], high[6])

    for c in range(3):
        enter(pair, 0, c, low[c])
        enter(pair, 1, c, guess_w[c, 0])
        enter(pair, 2, c, guess_w[c, 7])
        enter(pair, 3, c, high[c])
    march(pair, 0, 1, lambda k, rows: mods[1, rows], near, far, 0)
    march(pair, 2, 1, lambda k, rows: mods[9, rows], near, far, 2)
    begun = (low, down, up, high)
    invert = (inverses[0], inverses[1], inverses[8], high[7])
    sums[...] = jnp.zeros_like(sums)
    dot = square[...]
    for c in range(3):
        values = []
        for k in range(4):
            residual = begun[k][3 + c] - image(near, far, k, c)
            z = residual * invert[k]
            values.append(z)
            if k in (1, 2):
                dot = dot + residual * z
        first[c, 0] = low[6 + c]
        first[c, 1] = values[0]
        first[c, 2] = values[1]
        for k in range(1, 7):
            first[c, 2 + k] = first_w[c, k]
        first[c, 9] = values[2]
        first[c, 10] = values[3]
    sums[0] = dot

    def prepare(k, _):
        for c in range(3):
            enter(pair, k, c, first[c, k])
        return 0

    lax.fori_loop(0, 11, prepare, 0)
    march(pair, 0, 10, lambda k, rows: mods[k, rows], near, far, 0)

    def settle(k, _):
        dot, cross = 0.0, 0.0
        for c in range(3):
            w = image(near, far, k + 1, c)
            s = w * inverses[k]
            second[c, k] = s
            enter(pair, k, c, s)
            dot = dot + w * first[c, k + 1]
            cross = cross + w * s

        @pl.when(k >= 1)
        def _():
            sums[1] += dot
            sums[2] += cross

        return 0

    lax.fori_loop(0, 9, settle, 0)

    def use(k, tile, value):
        rows = slice(8 * tile, 8 * tile + 8)
        sums[3, rows] += value * mods[k + 1, rows]

    energy_march(pair, 8, use)
    lane = lax.broadcasted_iota(jnp.int32, (1, 128), 1)
    line = jnp.zeros((1, 128), jnp.float32)
    for k in range(4):
        line = jnp.where(lane == k, whole(sums[k, own]), line)
    tile = planes_in[0, 32:40] + jnp.broadcast_to(line, (8, 128))
    for k in range(planes.shape[0]):
        planes[k, 0:32] = planes_in[k, 0:32]
        planes[k, 32:40] = tile


def pick(line, k):
    lane = lax.broadcasted_iota(jnp.int32, line.shape, 1)
    return jnp.sum(jnp.where(lane == k, line, 0.0), axis=1, keepdims=True)


def energies(
    lines, lines_b, guess_w, low, first, second, occupancy, density, spread,
    out, smooth, pair, field, specific,
):
    sub = lax.axis_index("sub")
    own = pl.ds(pl.multiple_of(8 * sub, 8), 32)
    line = (jnp.sum(lines[...], axis=0) + jnp.sum(lines_b[...], axis=0))[0:1]
    a, b, c, e = (pick(line, k) for k in range(4))
    alpha = a / b
    fresh = alpha * alpha * c - a
    beta = fresh / a
    square = alpha * alpha * e - (1.0 + beta) * (1.0 + beta) * b
    after = fresh / square
    p = jnp.broadcast_to(alpha + after * (1.0 + beta), (ROWS, 128))
    q = jnp.broadcast_to(-after * alpha, (ROWS, 128))
    clear(pair)
    for c in range(3):
        enter(pair, 0, c, low[c] + p * first[c, 1] + q * second[c, 0])

    def advance(k, _):
        for c in range(3):
            value = guess_w[c, k] + p * first[c, k + 2] + q * second[c, k + 1]
            field[c] = value
            enter(pair, k + 1, c, value)
        for c in range(3):
            out[c, k] = field[c, own]
        return 0

    lax.fori_loop(0, 8, advance, 0)

    def use(k, tile, value):
        specific[k, 8 * tile : 8 * tile + 8] = value

    energy_march(pair, 8, use)
    parts = []
    for k in range(8):
        rho = density[k]
        share = jnp.where(occupancy[k] == 1, rho * rho / rho, 0.0)
        parts.append(0.5 * share * specific[k, own])
    row = lax.broadcasted_iota(jnp.int32, (128, 128), 0)
    col = lax.broadcasted_iota(jnp.int32, (128, 128), 1)
    gap = jnp.abs(row - col).astype(jnp.float32)
    band = jnp.where(gap <= REACH, NORM * jnp.exp(gap * (-1.0 / DECAY)), 0.0)
    value = jnp.dot(
        jnp.concatenate(parts, axis=0), band,
        precision=lax.Precision.HIGHEST, preferred_element_type=jnp.float32,
    )
    smooth[0:256] = value
    total = whole(value * spread[...].reshape(256, 128))
    smooth[256:264] = jnp.broadcast_to(total, (8, 128))


def decayed(block):
    upward, downward = 0.0, 0.0
    for k in range(8):
        upward = upward + math.exp(-(7 - k) / DECAY) * block[k]
        downward = downward + math.exp(-k / DECAY) * block[k]
    return upward, downward


def ladder(upward, downward, tile, out):
    run = lax.axis_index("run")
    for k in range(out.shape[0]):
        out[k, 0:32] = jnp.where(k > run, upward, downward)
        out[k, 32:40] = tile


def smooth_y(mine, other, planes=8):
    sub = lax.axis_index("sub")
    row = lax.broadcasted_iota(jnp.int32, (32, 32), 0)
    col = lax.broadcasted_iota(jnp.int32, (32, 32), 1)

    def band(offset):
        gap = jnp.abs(col + offset - row).astype(jnp.float32)
        return jnp.where(gap <= REACH, NORM * jnp.exp(gap * (-1.0 / DECAY)), 0.0)

    near = band(0)
    far = band(32 - 64 * sub)
    for k in range(planes):
        yield jnp.dot(
            near, mine(k), precision=lax.Precision.HIGHEST, preferred_element_type=jnp.float32
        ) + jnp.dot(
            far, other(k), precision=lax.Precision.HIGHEST, preferred_element_type=jnp.float32
        )


def bone_z(count, bone, below, above, out):
    blocks = [lambda j, ref=ref: ref[j].astype(jnp.float32) for ref in (bone, below, above)]
    for i, value in enumerate(far_z(count, *blocks)):
        out[i] = value
    out[8], out[9] = decayed([blocks[0](k) for k in range(8)])


def bone_y(mine, other, bone, out, planes):
    block = list(smooth_y(lambda k: mine[k], lambda k: other[k], 10))
    for k in range(8):
        out[k] = block[k]
    lane = lax.broadcasted_iota(jnp.int32, (8, 128), 1)
    total = whole(jnp.sum(bone[...].astype(jnp.float32), axis=0))
    ladder(block[8], block[9], jnp.where(lane == 4, total, 0.0), planes)


def along_y(mine, other, out, planes):
    def at(ref):
        return lambda k: ref[32 * k : 32 * k + 32]

    block = list(smooth_y(at(mine), at(other)))
    for k in range(8):
        out[k] = block[k]
    ladder(*decayed(block), mine[256:264] + other[256:264], planes)


def near_z(count, planes, i):
    run = lax.axis_index("run")
    lower, upper = 0.0, 0.0
    for o in range(1, REACH // 8):
        scale = math.exp(-8.0 * (o - 1) / DECAY)
        at = jnp.maximum(run - o, 0)
        lower = lower + jnp.where(run - o >= 0, scale * planes[at, 0:32], 0.0)
        at = jnp.minimum(run + o, count - 1)
        upper = upper + jnp.where(run + o < count, scale * planes[at, 0:32], 0.0)
    return weight(i + 1) * lower + weight(8 - i) * upper


def far_z(count, mine, below, above):
    run = lax.axis_index("run")
    has_below = run - REACH // 8 >= 0
    has_above = run + REACH // 8 < count
    for i in range(8):
        value, far_below, far_above = 0.0, 0.0, 0.0
        for j in range(8):
            value = value + weight(abs(i - j)) * mine(j)
            if j >= i:
                far_below = far_below + weight(i - j + REACH) * below(j)
            if j <= i:
                far_above = far_above + weight(j - i + REACH) * above(j)
        yield value + jnp.where(has_below, far_below, 0.0) + jnp.where(has_above, far_above, 0.0)


def partial_z(count, mine, below, above, out):
    blocks = [lambda j, ref=ref: ref[j] for ref in (mine, below, above)]
    for i, value in enumerate(far_z(count, *blocks)):
        out[i] = value


def spread_z(count, part, planes, out):
    for i in range(8):
        out[i] = part[i] + near_z(count, planes, i)


def remodel(count, part, planes, lines, lines_b, bone, density, out):
    bones = (jnp.sum(lines[...], axis=0) + jnp.sum(lines_b[...], axis=0))[0:1]
    line = jnp.sum(planes[:, 32:40], axis=0)[0:1]
    scale = jnp.broadcast_to(pick(bones, 4) / line, density.shape[1:])
    for i in range(8):
        value = part[i] + near_z(count, planes, i)
        rho = density[i]
        updated = jnp.minimum(rho * (1.0 + RATE * jnp.tanh(SLOPE * (value * scale - 1.0))), 1.0)
        out[i] = jnp.where(bone[i] == 1, updated, rho)


def local(load, guess, occupancy, density):
    count = lax.axis_size("run")
    block = density.shape
    swap = [(0, 1), (1, 0)]
    side = lax.ppermute(side_rows(load, guess, occupancy, density), "sub", swap)
    wide = (3, 8, ROWS, 128)
    kept = call(
        inner,
        [
            (10, ROWS, 128), (8, ROWS, 128), wide, wide,
            (8, ROWS, 128), (7, ROWS, 128), (ROWS, 128),
        ],
        [load, guess, occupancy, density, side],
        [(6, 8, 48, 128), (6, 8, 48, 128), (6, 8, 48, 128)],
    )
    up, down, guess_w = kept[:3]
    low = lax.ppermute(up, "run", [(i, i + 1) for i in range(count - 1)])
    high = lax.ppermute(down, "run", [(i + 1, i) for i in range(count - 1)])
    (smooth,) = call(
        functools.partial(bone_z, count), [(10, 32, 128)], [occupancy, *far_slabs(occupancy)]
    )
    spread, planes = call(
        bone_y,
        [block, (count, 40, 128)],
        [smooth, lax.ppermute(smooth, "sub", swap), occupancy],
    )
    planes, first, second = call(
        krylov,
        [(count, 40, 128), (3, 11, ROWS, 128), (3, 9, ROWS, 128)],
        [*kept, low, high, planes],
        [
            (6, 11, 48, 128), (6, 11, 48, 128), (6, 11, 48, 128),
            (10, ROWS, 128), (9, ROWS, 128), (4, ROWS, 128),
        ],
    )
    planes = lax.all_to_all(planes, "run", 0, 0, tiled=True)
    lines = planes[:, 32:40]
    lines_b = lax.ppermute(lines, "sub", swap)
    (spread,) = call(functools.partial(spread_z, count), [block], [spread, planes])
    displacement, smooth = call(
        energies,
        [guess.shape, (264, 128)],
        [lines, lines_b, guess_w, low, first, second, occupancy, density, spread],
        [(6, 9, 48, 128), (3, ROWS, 128), (8, ROWS, 128)],
    )
    other = lax.ppermute(smooth, "sub", swap)
    smooth, planes = call(along_y, [block, (count, 40, 128)], [smooth, other])
    below, above = far_slabs(smooth)
    planes = lax.all_to_all(planes, "run", 0, 0, tiled=True)
    (part,) = call(
        functools.partial(partial_z, count), [block], [smooth, below, above], flops=10**10
    )
    (new_density,) = call(
        functools.partial(remodel, count),
        [block],
        [part, planes, lines, lines_b, occupancy, density],
    )
    return displacement, new_density


def far_slabs(block):
    count = lax.axis_size("run")
    span = REACH // block.shape[0]
    rise = [(i, i + span) for i in range(count - span)]
    fall = [(i + span, i) for i in range(count - span)]
    if count <= 2 * span:
        both = lax.ppermute(block, "run", rise + fall)
        return both, both
    return lax.ppermute(block, "run", rise), lax.ppermute(block, "run", fall)


def solution(mesh):
    field = P(None, ("grp", "run"), "sub", None)
    cells = P(("grp", "run"), "sub", None)
    return jax.shard_map(
        local,
        mesh=mesh,
        in_specs=(field, field, cells, cells),
        out_specs=(field, cells),
        check_vma=False,
    )
```

```python
import functools
import math

import jax
import jax.numpy as jnp
from jax import lax
from jax.experimental import pallas as pl
from jax.experimental.pallas import tpu as pltpu
from jax.sharding import PartitionSpec as P

REACH = 32
POISSON = 0.3
MARROW = 0.05
RATE = 0.5
SLOPE = 4.0
DECAY = REACH / 4.0

LAME = POISSON / ((1.0 + POISSON) * (1.0 - 2.0 * POISSON)) / 16.0
SHEAR = 0.5 / (1.0 + POISSON) / 16.0
ENTRY = 16.0 * (LAME + 4.0 * SHEAR) / 9.0
NORM = 1.0 / sum(math.exp(-abs(k) / DECAY) for k in range(-REACH, REACH + 1))

ROWS = 40
PAIR = ("run", "sub")

VMEM = pl.BlockSpec(memory_space=pltpu.VMEM)


def weight(distance):
    return NORM * math.exp(-distance / DECAY)


def call(kernel, outs, ins, scratch=(), flops=None):
    cost = None
    if flops is not None:
        cost = pl.CostEstimate(flops=flops, bytes_accessed=2**20, transcendentals=0)
    return pl.pallas_call(
        kernel,
        out_shape=[jax.ShapeDtypeStruct(s, jnp.float32) for s in outs],
        in_specs=[VMEM] * len(ins),
        out_specs=[VMEM] * len(outs),
        scratch_shapes=[pltpu.VMEM(s, jnp.float32) for s in scratch],
        compiler_params=pltpu.CompilerParams(vmem_limit_bytes=40 * 1024 * 1024),
        cost_estimate=cost,
    )(*ins)


def lane_right(block):
    lane = lax.broadcasted_iota(jnp.int32, block.shape, 1)
    return jnp.where(lane == 0, 0.0, pltpu.roll(block, 1, 1))


def lane_left(block):
    lane = lax.broadcasted_iota(jnp.int32, block.shape, 1)
    return jnp.where(lane == block.shape[1] - 1, 0.0, pltpu.roll(block, block.shape[1] - 1, 1))


def row_down(block):
    row = lax.broadcasted_iota(jnp.int32, block.shape, 0)
    return jnp.where(row == block.shape[0] - 1, 0.0, pltpu.roll(block, block.shape[0] - 1, 0))


def stiff(occupancy, density):
    return jnp.where(occupancy == 1, density * density, MARROW)


def enter(pair, k, c, field):
    other = lane_right(field)
    pair[2 * c, k, 8:48] = field + other
    pair[2 * c + 1, k, 8:48] = field - other


def clear(pair):
    for m in range(6):
        for k in range(pair.shape[1]):
            pair[m, k, 0:8] = jnp.zeros((8, 128), jnp.float32)


def plane_modes(pair, k, tile):
    out = [None] * 12
    for c in range(3):
        for x in range(2):
            here = pair[2 * c + x, k, 8 + 8 * tile : 16 + 8 * tile]
            above = pair[2 * c + x, k, 7 + 8 * tile : 15 + 8 * tile]
            out[4 * c + x] = here + above
            out[4 * c + 2 + x] = here - above
    return out


def steps(count, body, carry):
    if count <= 3:
        for k in range(count):
            carry = body(k, carry)
        return carry

    def turn(k, carry):
        return body(2 * k + 1, body(2 * k, carry))

    carry = lax.fori_loop(0, count // 2, turn, carry)
    return body(count - 1, carry) if count % 2 else carry


def march(pair, start, count, mod, near, far, to):
    for tile in range(ROWS // 8):
        rows = slice(8 * tile, 8 * tile + 8)

        def leave(k, totals):
            for c in range(3):
                for x in range(2):
                    s, d = totals[4 * c + x], totals[4 * c + 2 + x]
                    near[2 * c + x, k, rows] = s + d
                    far[2 * c + x, k, rows] = s - d

        def body(k, carry):
            low, kept = carry
            high = plane_modes(pair, start + k + 1, tile)
            g = stress(modes_of(low, high), mod(k, rows))
            totals, after = [None] * 12, [None] * 12
            for c in range(3):
                for m in range(4):
                    d = g[c][4 + m]
                    at = 4 * c + m
                    if m:
                        s = g[c][m]
                        totals[at] = kept[at] + (s - d)
                        after[at] = s + d
                    else:
                        totals[at] = kept[at] - d
                        after[at] = d
            leave(to + k, totals)
            return high, after

        zeros = [jnp.zeros((8, 128), jnp.float32)] * 12
        _, kept = steps(count, body, (plane_modes(pair, start, tile), zeros))
        leave(to + count, kept)


def image(near, far, k, c):
    columns = [
        near[2 * c + x, k, 0:ROWS] + far[2 * c + x, k, 1 : ROWS + 1] for x in range(2)
    ]
    return columns[0] + columns[1] + lane_left(columns[0] - columns[1])


def energy_march(pair, start, count, use):
    for tile in range(ROWS // 8):

        def body(k, low):
            high = plane_modes(pair, start + k + 1, tile)
            use(k, tile, quadratic(modes_of(low, high)))
            return high

        steps(count, body, plane_modes(pair, start, tile))


def inverted(low, high):
    t = low + high
    t = t + row_down(t)
    t = (t + lane_left(t)) * ENTRY
    return jnp.where(t > 0.0, 1.0 / jnp.where(t > 0.0, t, 1.0), 0.0)


def whole(block):
    return jnp.sum(jnp.sum(block, axis=0, keepdims=True), axis=1, keepdims=True)


def modes_of(low, high):
    out = []
    for c in range(3):
        modes = [None] * 8
        for m in range(4):
            if m:
                modes[m] = high[4 * c + m] + low[4 * c + m]
            modes[4 + m] = high[4 * c + m] - low[4 * c + m]
        out.append(modes)
    return out


X, Y, Z = 1, 2, 4


def stress(u, mod):
    g = [[None] * 8 for _ in range(3)]
    bulk, rigid = mod * LAME, mod * SHEAR
    twice = rigid + rigid
    bulk3, rigid3 = mod * (LAME / 3.0), mod * (SHEAR / 3.0)
    last = mod * ((LAME + 4.0 * SHEAR) / 9.0)
    t = (u[0][X] + u[1][Y] + u[2][Z]) * bulk
    g[0][X] = t + u[0][X] * twice
    g[1][Y] = t + u[1][Y] * twice
    g[2][Z] = t + u[2][Z] * twice
    g[0][Y] = g[1][X] = (u[0][Y] + u[1][X]) * rigid
    g[0][Z] = g[2][X] = (u[0][Z] + u[2][X]) * rigid
    g[1][Z] = g[2][Y] = (u[1][Z] + u[2][Y]) * rigid
    for (c, m), (d, n) in (
        ((1, X | Y), (2, X | Z)),
        ((0, X | Y), (2, Y | Z)),
        ((0, X | Z), (1, Y | Z)),
    ):
        s = (u[c][m] + u[d][n]) * bulk3
        g[c][m] = s + u[c][m] * rigid
        g[d][n] = s + u[d][n] * rigid
    s = u[0][Y | Z] + u[1][X | Z] + u[2][X | Y]
    g[0][Y | Z] = (s + u[0][Y | Z]) * rigid3
    g[1][X | Z] = (s + u[1][X | Z]) * rigid3
    g[2][X | Y] = (s + u[2][X | Y]) * rigid3
    for c in range(3):
        g[c][7] = u[c][7] * last
    return g


def quadratic(u):
    def sq(v):
        return v * v

    t = sq(u[0][X] + u[1][Y] + u[2][Z])
    r2 = sq(u[0][X]) + sq(u[1][Y]) + sq(u[2][Z])
    r = sq(u[0][Y] + u[1][X]) + sq(u[0][Z] + u[2][X]) + sq(u[1][Z] + u[2][Y])
    t3 = 0.0
    for (c, m), (d, n) in (
        ((1, X | Y), (2, X | Z)),
        ((0, X | Y), (2, Y | Z)),
        ((0, X | Z), (1, Y | Z)),
    ):
        t3 = t3 + sq(u[c][m] + u[d][n])
        r = r + (sq(u[c][m]) + sq(u[d][n]))
    p, q, s = u[0][Y | Z], u[1][X | Z], u[2][X | Y]
    r3 = sq(p + q) + sq(p + s) + sq(q + s)
    last = sq(u[0][7]) + sq(u[1][7]) + sq(u[2][7])
    return (
        LAME * (t + t3 * (1.0 / 3.0))
        + SHEAR * (r + r2 + r2 + r3 * (1.0 / 3.0))
        + ((LAME + 4.0 * SHEAR) / 9.0) * last
    )


def side_rows(load, guess, occupancy, density):
    sub = lax.axis_index("sub")
    flat = lambda part: part.reshape((-1,) + part.shape[-2:])
    near = lambda part: jnp.where(sub == 0, part[..., 24:32, :], part[..., 0:8, :])
    return jnp.concatenate(
        [flat(near(guess)), flat(near(load)), stiff(near(occupancy), near(density))], axis=0
    )


def windows(sub, load, guess, bone, density, side):
    own = pl.ds(pl.multiple_of(8 * sub, 8), 32)
    rest = pl.ds(pl.multiple_of(32 * (1 - sub), 8), 8)

    def put_guess(out, at, c, k):
        out[c, at, own] = guess[c, k]
        out[c, at, rest] = side[8 * c + k]

    def put_load(out, at, c, k):
        out[c, at, own] = load[c, k]
        out[c, at, rest] = side[24 + 8 * c + k]

    def put_mod(out, at, k):
        out[at, own] = stiff(bone[k], density[k])
        out[at, rest] = side[48 + k]

    return put_guess, put_load, put_mod


def blank(pair, far):
    clear(pair)
    for m in range(6):
        for k in range(far.shape[1]):
            far[m, k, ROWS : ROWS + 8] = jnp.zeros((8, 128), jnp.float32)


def edge(
    load, guess, bone, density, side, up, down, guess_w, load_w, mods, pair, near, far
):
    put_guess, put_load, put_mod = windows(
        lax.axis_index("sub"), load, guess, bone, density, side
    )
    blank(pair, far)
    for at, k in enumerate((0, 1, 6, 7)):
        put_mod(mods, at, k)
    for c in range(3):
        for at, k in enumerate((0, 6, 7)):
            put_load(load_w, at, c, k)
        for at, k in enumerate((0, 1, 5, 6, 7)):
            put_guess(guess_w, at, c, k)
            enter(pair, at, c, guess_w[c, at])
    march(pair, 0, 1, lambda k, rows: mods[1, rows], near, far, 0)
    march(pair, 2, 2, lambda k, rows: mods[2 + k, rows], near, far, 2)
    inverse = inverted(mods[2], mods[3])
    for c in range(3):
        down[c] = guess_w[c, 0]
        down[3 + c] = load_w[c, 0] - image(near, far, 0, c)
        up[c] = guess_w[c, 4]
        up[3 + c] = load_w[c, 2] - image(near, far, 4, c)
        up[6 + c] = (load_w[c, 1] - image(near, far, 3, c)) * inverse
    up[9] = mods[3]
    down[6] = mods[0]
    down[7] = inverted(mods[0], mods[1])


def middle(
    count, load, guess, bone, density, side, bone_below, bone_above,
    smooth, guess_w, mod_w, inverse, inner_z, inner_s, near_m, far_m, sums,
    load_w, pair, near, far, pair_z, pair_s,
):
    put_guess, put_load, put_mod = windows(
        lax.axis_index("sub"), load, guess, bone, density, side
    )
    bone_z(count, bone, bone_below, bone_above, smooth)
    blank(pair, far)
    blank(pair_z, far_m)
    clear(pair_s)
    for k in range(8):
        put_mod(mod_w, k, k)
        for c in range(3):
            put_guess(guess_w, k, c, k)
            put_load(load_w, k, c, k)
    for k in range(7):
        inverse[k] = inverted(mod_w[k], mod_w[k + 1])

    def prepare(k, _):
        for c in range(3):
            enter(pair, k, c, guess_w[c, k])
        return 0

    lax.fori_loop(0, 8, prepare, 0)
    march(pair, 0, 7, lambda k, rows: mod_w[k + 1, rows], near, far, 0)
    sums[...] = jnp.zeros_like(sums)

    def settle_z(k, _):
        dot = 0.0
        for c in range(3):
            residual = load_w[c, k] - image(near, far, k, c)
            z = residual * inverse[k]
            inner_z[c, k - 1] = z
            enter(pair_z, k - 1, c, z)
            dot = dot + residual * z
        sums[0] += dot
        return 0

    lax.fori_loop(1, 7, settle_z, 0)
    march(pair_z, 0, 5, lambda k, rows: mod_w[k + 2, rows], near_m, far_m, 0)

    def settle_s(k, _):
        dot, cross = 0.0, 0.0
        for c in range(3):
            w = image(near_m, far_m, k - 1, c)
            s = w * inverse[k]
            inner_s[c, k - 2] = s
            enter(pair_s, k - 2, c, s)
            dot = dot + w * inner_z[c, k - 1]
            cross = cross + w * s
        sums[1] += dot
        sums[2] += cross
        return 0

    lax.fori_loop(2, 6, settle_s, 0)

    def use(k, tile, value):
        rows = slice(8 * tile, 8 * tile + 8)
        sums[3, rows] += value * mod_w[k + 3, rows]

    energy_march(pair_s, 0, 3, use)


def krylov(
    up, down, guess_w, mod_w, inverse, inner_z, inner_s, near_m, far_m, sums_in, low, high,
    row_out, first, second, pair, near, far, mods, sums,
):
    sub = lax.axis_index("sub")
    run = lax.axis_index("run")
    own = pl.ds(pl.multiple_of(8 * sub, 8), 32)
    blank(pair, far)
    sums[...] = sums_in[...]
    mods[0] = low[9]
    for k in range(3):
        mods[1 + k] = mod_w[k]
    for k in range(2):
        mods[4 + k] = mod_w[6 + k]
    mods[6] = high[6]
    bottom = jnp.where(run > 0, inverted(low[9], mod_w[0]), 0.0)
    top = inverted(mod_w[7], high[6])

    for c in range(3):
        enter(pair, 0, c, low[c])
        enter(pair, 1, c, guess_w[c, 0])
        enter(pair, 2, c, guess_w[c, 7])
        enter(pair, 3, c, high[c])
    march(pair, 0, 1, lambda k, rows: mods[1, rows], near, far, 0)
    march(pair, 2, 1, lambda k, rows: mods[6, rows], near, far, 2)
    begun = (low, down, up, high)
    invert = (bottom, inverse[0], top, high[7])
    dot = 0.0
    ends = []
    for c in range(3):
        values = []
        for k in range(4):
            residual = begun[k][3 + c] - image(near, far, k, c)
            z = residual * invert[k]
            values.append(z)
            if k in (1, 2):
                dot = dot + residual * z
        first[c, 0] = values[0]
        first[c, 1] = values[1]
        for k in range(6):
            first[c, 2 + k] = inner_z[c, k]
        first[c, 8] = values[2]
        ends.append(values[3])
    sums[0] += dot

    for c in range(3):
        enter(pair, 0, c, low[6 + c])
        for k in range(3):
            enter(pair, 1 + k, c, first[c, k])
        enter(pair, 4, c, first[c, 7])
        enter(pair, 5, c, first[c, 8])
        enter(pair, 6, c, ends[c])
    march(pair, 0, 3, lambda k, rows: mods[k, rows], near, far, 0)
    march(pair, 4, 2, lambda k, rows: mods[5 + k, rows], near, far, 4)
    dot, cross = 0.0, 0.0
    for c in range(3):
        images = {
            -1: image(near, far, 1, c),
            0: image(near, far, 2, c),
            1: image(near, far, 3, c) + image(near_m, far_m, 0, c),
            6: image(near, far, 4, c) + image(near_m, far_m, 5, c),
            7: image(near, far, 5, c),
        }
        for k, w in images.items():
            s = w * (bottom if k < 0 else top if k == 7 else inverse[k])
            second[c, k + 1] = s
            if k >= 0:
                dot = dot + w * first[c, k + 1]
                cross = cross + w * s
        for k in range(2, 6):
            second[c, k + 1] = inner_s[c, k - 2]
    sums[1] += dot
    sums[2] += cross

    for c in range(3):
        for at, k in enumerate((-1, 0, 1, 2, 5, 6, 7)):
            enter(pair, at, c, second[c, k + 1])

    def use(first_mod):
        def add(k, tile, value):
            rows = slice(8 * tile, 8 * tile + 8)
            sums[3, rows] += value * mods[first_mod + k, rows]

        return add

    energy_march(pair, 0, 3, use(1))
    energy_march(pair, 4, 2, use(4))
    lane = lax.broadcasted_iota(jnp.int32, (1, 128), 1)
    line = jnp.zeros((1, 128), jnp.float32)
    for k in range(4):
        line = jnp.where(lane == k, whole(sums[k, own]), line)
    row_out[...] = jnp.broadcast_to(line, row_out.shape)


def pick(line, k):
    lane = lax.broadcasted_iota(jnp.int32, line.shape, 1)
    return jnp.sum(jnp.where(lane == k, line, 0.0), axis=1, keepdims=True)


def energies(
    lines, lines_b, guess_w, low, first, second, occupancy, density, spread,
    out, smooth, pair, field, specific,
):
    sub = lax.axis_index("sub")
    own = pl.ds(pl.multiple_of(8 * sub, 8), 32)
    line = (jnp.sum(lines[...], axis=0) + jnp.sum(lines_b[...], axis=0))[0:1]
    a, b, c, e = (pick(line, k) for k in range(4))
    alpha = a / b
    fresh = alpha * alpha * c - a
    beta = fresh / a
    square = alpha * alpha * e - (1.0 + beta) * (1.0 + beta) * b
    after = fresh / square
    p = jnp.broadcast_to(alpha + after * (1.0 + beta), (ROWS, 128))
    q = jnp.broadcast_to(-after * alpha, (ROWS, 128))
    clear(pair)
    for c in range(3):
        enter(pair, 0, c, low[c] + p * first[c, 0] + q * second[c, 0])

    def advance(k, _):
        for c in range(3):
            value = guess_w[c, k] + p * first[c, k + 1] + q * second[c, k + 1]
            field[c] = value
            enter(pair, k + 1, c, value)
        for c in range(3):
            out[c, k] = field[c, own]
        return 0

    lax.fori_loop(0, 8, advance, 0)

    def use(k, tile, value):
        specific[k, 8 * tile : 8 * tile + 8] = value

    energy_march(pair, 0, 8, use)
    parts = []
    for k in range(8):
        rho = density[k]
        share = jnp.where(occupancy[k] == 1, rho * rho / rho, 0.0)
        parts.append(0.5 * share * specific[k, own])
    row = lax.broadcasted_iota(jnp.int32, (128, 128), 0)
    col = lax.broadcasted_iota(jnp.int32, (128, 128), 1)
    gap = jnp.abs(row - col).astype(jnp.float32)
    band = jnp.where(gap <= REACH, NORM * jnp.exp(gap * (-1.0 / DECAY)), 0.0)
    value = jnp.dot(
        jnp.concatenate(parts, axis=0), band,
        precision=lax.Precision.HIGHEST, preferred_element_type=jnp.float32,
    )
    smooth[0:256] = value
    total = whole(value * spread[...].reshape(256, 128))
    smooth[256:264] = jnp.broadcast_to(total, (8, 128))


def decayed(block):
    upward, downward = 0.0, 0.0
    for k in range(8):
        upward = upward + math.exp(-(7 - k) / DECAY) * block[k]
        downward = downward + math.exp(-k / DECAY) * block[k]
    return upward, downward


def ladder(upward, downward, tile, out):
    run = lax.axis_index("run")
    for k in range(out.shape[0]):
        out[k, 0:32] = jnp.where(k > run, upward, downward)
        out[k, 32:40] = tile


def smooth_y(mine, other, planes=8):
    sub = lax.axis_index("sub")
    row = lax.broadcasted_iota(jnp.int32, (32, 32), 0)
    col = lax.broadcasted_iota(jnp.int32, (32, 32), 1)

    def band(offset):
        gap = jnp.abs(col + offset - row).astype(jnp.float32)
        return jnp.where(gap <= REACH, NORM * jnp.exp(gap * (-1.0 / DECAY)), 0.0)

    near = band(0)
    far = band(32 - 64 * sub)
    for k in range(planes):
        yield jnp.dot(
            near, mine(k), precision=lax.Precision.HIGHEST, preferred_element_type=jnp.float32
        ) + jnp.dot(
            far, other(k), precision=lax.Precision.HIGHEST, preferred_element_type=jnp.float32
        )


def bone_z(count, bone, below, above, out):
    blocks = [lambda j, ref=ref: ref[j].astype(jnp.float32) for ref in (bone, below, above)]
    for i, value in enumerate(far_z(count, *blocks)):
        out[i] = value
    out[8], out[9] = decayed([blocks[0](k) for k in range(8)])


def bone_y(mine, other, bone, line, out, planes):
    block = list(smooth_y(lambda k: mine[k], lambda k: other[k], 10))
    for k in range(8):
        out[k] = block[k]
    lane = lax.broadcasted_iota(jnp.int32, (8, 128), 1)
    total = whole(jnp.sum(bone[...].astype(jnp.float32), axis=0))
    ladder(block[8], block[9], jnp.where(lane == 4, total, line[...]), planes)


def along_y(mine, other, out, planes):
    def at(ref):
        return lambda k: ref[32 * k : 32 * k + 32]

    block = list(smooth_y(at(mine), at(other)))
    for k in range(8):
        out[k] = block[k]
    ladder(*decayed(block), mine[256:264] + other[256:264], planes)


def near_z(count, planes, i):
    run = lax.axis_index("run")
    lower, upper = 0.0, 0.0
    for o in range(1, REACH // 8):
        scale = math.exp(-8.0 * (o - 1) / DECAY)
        at = jnp.maximum(run - o, 0)
        lower = lower + jnp.where(run - o >= 0, scale * planes[at, 0:32], 0.0)
        at = jnp.minimum(run + o, count - 1)
        upper = upper + jnp.where(run + o < count, scale * planes[at, 0:32], 0.0)
    return weight(i + 1) * lower + weight(8 - i) * upper


def far_z(count, mine, below, above):
    run = lax.axis_index("run")
    has_below = run - REACH // 8 >= 0
    has_above = run + REACH // 8 < count
    for i in range(8):
        value, far_below, far_above = 0.0, 0.0, 0.0
        for j in range(8):
            value = value + weight(abs(i - j)) * mine(j)
            if j >= i:
                far_below = far_below + weight(i - j + REACH) * below(j)
            if j <= i:
                far_above = far_above + weight(j - i + REACH) * above(j)
        yield value + jnp.where(has_below, far_below, 0.0) + jnp.where(has_above, far_above, 0.0)


def partial_z(count, mine, below, above, out):
    blocks = [lambda j, ref=ref: ref[j] for ref in (mine, below, above)]
    for i, value in enumerate(far_z(count, *blocks)):
        out[i] = value


def spread_z(count, part, planes, out):
    for i in range(8):
        out[i] = part[i] + near_z(count, planes, i)


def remodel(count, part, planes, lines, lines_b, bone, density, out):
    bones = (jnp.sum(lines[...], axis=0) + jnp.sum(lines_b[...], axis=0))[0:1]
    line = jnp.sum(planes[:, 32:40], axis=0)[0:1]
    scale = jnp.broadcast_to(pick(bones, 4) / line, density.shape[1:])
    for i in range(8):
        value = part[i] + near_z(count, planes, i)
        rho = density[i]
        updated = jnp.minimum(rho * (1.0 + RATE * jnp.tanh(SLOPE * (value * scale - 1.0))), 1.0)
        out[i] = jnp.where(bone[i] == 1, updated, rho)


def local(load, guess, occupancy, density):
    count = lax.axis_size("run")
    block = density.shape
    swap = [(0, 1), (1, 0)]
    side = lax.ppermute(side_rows(load, guess, occupancy, density), "sub", swap)
    inputs = [load, guess, occupancy, density, side]
    up, down = call(
        edge,
        [(10, ROWS, 128), (8, ROWS, 128)],
        inputs,
        [
            (3, 5, ROWS, 128), (3, 3, ROWS, 128), (4, ROWS, 128),
            (6, 5, 48, 128), (6, 5, ROWS, 128), (6, 5, 48, 128),
        ],
    )
    low = lax.ppermute(up, "run", [(i, i + 1) for i in range(count - 1)])
    high = lax.ppermute(down, "run", [(i + 1, i) for i in range(count - 1)])
    smooth, *kept = call(
        functools.partial(middle, count),
        [
            (10, 32, 128),
            (3, 8, ROWS, 128), (8, ROWS, 128), (7, ROWS, 128),
            (3, 6, ROWS, 128), (3, 4, ROWS, 128),
            (6, 6, ROWS, 128), (6, 6, 48, 128), (4, ROWS, 128),
        ],
        [*inputs, *far_slabs(occupancy)],
        [
            (3, 8, ROWS, 128), (6, 8, 48, 128), (6, 8, ROWS, 128), (6, 8, 48, 128),
            (6, 6, 48, 128), (6, 4, 48, 128),
        ],
    )
    guess_w = kept[0]
    line, first, second = call(
        krylov,
        [(8, 128), (3, 9, ROWS, 128), (3, 9, ROWS, 128)],
        [up, down, *kept, low, high],
        [
            (6, 7, 48, 128), (6, 7, ROWS, 128), (6, 7, 48, 128),
            (7, ROWS, 128), (4, ROWS, 128),
        ],
    )
    spread, planes = call(
        bone_y,
        [block, (count, 40, 128)],
        [smooth, lax.ppermute(smooth, "sub", swap), occupancy, line],
    )
    planes = lax.all_to_all(planes, "run", 0, 0, tiled=True)
    lines = planes[:, 32:40]
    lines_b = lax.ppermute(lines, "sub", swap)
    (spread,) = call(functools.partial(spread_z, count), [block], [spread, planes])
    displacement, smooth = call(
        energies,
        [guess.shape, (264, 128)],
        [lines, lines_b, guess_w, low, first, second, occupancy, density, spread],
        [(6, 9, 48, 128), (3, ROWS, 128), (8, ROWS, 128)],
    )
    other = lax.ppermute(smooth, "sub", swap)
    smooth, planes = call(along_y, [block, (count, 40, 128)], [smooth, other])
    below, above = far_slabs(smooth)
    planes = lax.all_to_all(planes, "run", 0, 0, tiled=True)
    (part,) = call(
        functools.partial(partial_z, count), [block], [smooth, below, above], flops=10**10
    )
    (new_density,) = call(
        functools.partial(remodel, count),
        [block],
        [part, planes, lines, lines_b, occupancy, density],
    )
    return displacement, new_density


def far_slabs(block):
    count = lax.axis_size("run")
    span = REACH // block.shape[0]
    rise = [(i, i + span) for i in range(count - span)]
    fall = [(i + span, i) for i in range(count - span)]
    if count <= 2 * span:
        both = lax.ppermute(block, "run", rise + fall)
        return both, both
    return lax.ppermute(block, "run", rise), lax.ppermute(block, "run", fall)


def solution(mesh):
    field = P(None, ("grp", "run"), "sub", None)
    cells = P(("grp", "run"), "sub", None)
    return jax.shard_map(
        local,
        mesh=mesh,
        in_specs=(field, field, cells, cells),
        out_specs=(field, cells),
        check_vma=False,
    )
```

```python
import functools
import math

import jax
import jax.numpy as jnp
from jax import lax
from jax.experimental import pallas as pl
from jax.experimental.pallas import tpu as pltpu
from jax.sharding import PartitionSpec as P

REACH = 32
POISSON = 0.3
MARROW = 0.05
RATE = 0.5
SLOPE = 4.0
DECAY = REACH / 4.0

LAME = POISSON / ((1.0 + POISSON) * (1.0 - 2.0 * POISSON)) / 16.0
SHEAR = 0.5 / (1.0 + POISSON) / 16.0
ENTRY = 16.0 * (LAME + 4.0 * SHEAR) / 9.0
NORM = 1.0 / sum(math.exp(-abs(k) / DECAY) for k in range(-REACH, REACH + 1))

ROWS = 40
PAIR = ("run", "sub")

VMEM = pl.BlockSpec(memory_space=pltpu.VMEM)


def weight(distance):
    return NORM * math.exp(-distance / DECAY)


def call(kernel, outs, ins, scratch=(), flops=None):
    cost = None
    if flops is not None:
        cost = pl.CostEstimate(flops=flops, bytes_accessed=2**20, transcendentals=0)
    return pl.pallas_call(
        kernel,
        out_shape=[jax.ShapeDtypeStruct(s, jnp.float32) for s in outs],
        in_specs=[VMEM] * len(ins),
        out_specs=[VMEM] * len(outs),
        scratch_shapes=[pltpu.VMEM(s, jnp.float32) for s in scratch],
        compiler_params=pltpu.CompilerParams(vmem_limit_bytes=40 * 1024 * 1024),
        cost_estimate=cost,
    )(*ins)


def lane_right(block):
    lane = lax.broadcasted_iota(jnp.int32, block.shape, 1)
    return jnp.where(lane == 0, 0.0, pltpu.roll(block, 1, 1))


def lane_left(block):
    lane = lax.broadcasted_iota(jnp.int32, block.shape, 1)
    return jnp.where(lane == block.shape[1] - 1, 0.0, pltpu.roll(block, block.shape[1] - 1, 1))


def row_down(block):
    row = lax.broadcasted_iota(jnp.int32, block.shape, 0)
    return jnp.where(row == block.shape[0] - 1, 0.0, pltpu.roll(block, block.shape[0] - 1, 0))


def stiff(occupancy, density):
    return jnp.where(occupancy == 1, density * density, MARROW)


def enter(pair, k, c, field):
    other = lane_right(field)
    pair[2 * c, k, 8:48] = field + other
    pair[2 * c + 1, k, 8:48] = field - other


def clear(pair):
    for m in range(6):
        for k in range(pair.shape[1]):
            pair[m, k, 0:8] = jnp.zeros((8, 128), jnp.float32)


def plane_modes(pair, k, tile):
    out = [None] * 12
    for c in range(3):
        for x in range(2):
            here = pair[2 * c + x, k, 8 + 8 * tile : 16 + 8 * tile]
            above = pair[2 * c + x, k, 7 + 8 * tile : 15 + 8 * tile]
            out[4 * c + x] = here + above
            out[4 * c + 2 + x] = here - above
    return out


def steps(count, body, carry):
    if count <= 3:
        for k in range(count):
            carry = body(k, carry)
        return carry

    def turn(k, carry):
        return body(2 * k + 1, body(2 * k, carry))

    carry = lax.fori_loop(0, count // 2, turn, carry)
    return body(count - 1, carry) if count % 2 else carry


def march(pair, start, count, mod, near, far, to):
    for tile in range(ROWS // 8):
        rows = slice(8 * tile, 8 * tile + 8)

        def leave(k, totals):
            for c in range(3):
                for x in range(2):
                    s, d = totals[4 * c + x], totals[4 * c + 2 + x]
                    near[2 * c + x, k, rows] = s + d
                    far[2 * c + x, k, rows] = s - d

        def body(k, carry):
            low, kept = carry
            high = plane_modes(pair, start + k + 1, tile)
            g = stress(modes_of(low, high), mod(k, rows))
            totals, after = [None] * 12, [None] * 12
            for c in range(3):
                for m in range(4):
                    d = g[c][4 + m]
                    at = 4 * c + m
                    if m:
                        s = g[c][m]
                        totals[at] = kept[at] + (s - d)
                        after[at] = s + d
                    else:
                        totals[at] = kept[at] - d
                        after[at] = d
            leave(to + k, totals)
            return high, after

        zeros = [jnp.zeros((8, 128), jnp.float32)] * 12
        _, kept = steps(count, body, (plane_modes(pair, start, tile), zeros))
        leave(to + count, kept)


def image(near, far, k, c):
    columns = [
        near[2 * c + x, k, 0:ROWS] + far[2 * c + x, k, 1 : ROWS + 1] for x in range(2)
    ]
    return columns[0] + columns[1] + lane_left(columns[0] - columns[1])


def energy_march(pair, start, count, use):
    for tile in range(ROWS // 8):

        def body(k, low):
            high = plane_modes(pair, start + k + 1, tile)
            use(k, tile, quadratic(modes_of(low, high)))
            return high

        steps(count, body, plane_modes(pair, start, tile))


def inverted(low, high):
    t = low + high
    t = t + row_down(t)
    t = (t + lane_left(t)) * ENTRY
    return jnp.where(t > 0.0, 1.0 / jnp.where(t > 0.0, t, 1.0), 0.0)


def whole(block):
    return jnp.sum(jnp.sum(block, axis=0, keepdims=True), axis=1, keepdims=True)


def modes_of(low, high):
    out = []
    for c in range(3):
        modes = [None] * 8
        for m in range(4):
            if m:
                modes[m] = high[4 * c + m] + low[4 * c + m]
            modes[4 + m] = high[4 * c + m] - low[4 * c + m]
        out.append(modes)
    return out


X, Y, Z = 1, 2, 4


def stress(u, mod):
    g = [[None] * 8 for _ in range(3)]
    bulk, rigid = mod * LAME, mod * SHEAR
    twice = rigid + rigid
    bulk3, rigid3 = mod * (LAME / 3.0), mod * (SHEAR / 3.0)
    last = mod * ((LAME + 4.0 * SHEAR) / 9.0)
    t = (u[0][X] + u[1][Y] + u[2][Z]) * bulk
    g[0][X] = t + u[0][X] * twice
    g[1][Y] = t + u[1][Y] * twice
    g[2][Z] = t + u[2][Z] * twice
    g[0][Y] = g[1][X] = (u[0][Y] + u[1][X]) * rigid
    g[0][Z] = g[2][X] = (u[0][Z] + u[2][X]) * rigid
    g[1][Z] = g[2][Y] = (u[1][Z] + u[2][Y]) * rigid
    for (c, m), (d, n) in (
        ((1, X | Y), (2, X | Z)),
        ((0, X | Y), (2, Y | Z)),
        ((0, X | Z), (1, Y | Z)),
    ):
        s = (u[c][m] + u[d][n]) * bulk3
        g[c][m] = s + u[c][m] * rigid
        g[d][n] = s + u[d][n] * rigid
    s = u[0][Y | Z] + u[1][X | Z] + u[2][X | Y]
    g[0][Y | Z] = (s + u[0][Y | Z]) * rigid3
    g[1][X | Z] = (s + u[1][X | Z]) * rigid3
    g[2][X | Y] = (s + u[2][X | Y]) * rigid3
    for c in range(3):
        g[c][7] = u[c][7] * last
    return g


def quadratic(u):
    def sq(v):
        return v * v

    t = sq(u[0][X] + u[1][Y] + u[2][Z])
    r2 = sq(u[0][X]) + sq(u[1][Y]) + sq(u[2][Z])
    r = sq(u[0][Y] + u[1][X]) + sq(u[0][Z] + u[2][X]) + sq(u[1][Z] + u[2][Y])
    t3 = 0.0
    for (c, m), (d, n) in (
        ((1, X | Y), (2, X | Z)),
        ((0, X | Y), (2, Y | Z)),
        ((0, X | Z), (1, Y | Z)),
    ):
        t3 = t3 + sq(u[c][m] + u[d][n])
        r = r + (sq(u[c][m]) + sq(u[d][n]))
    p, q, s = u[0][Y | Z], u[1][X | Z], u[2][X | Y]
    r3 = sq(p + q) + sq(p + s) + sq(q + s)
    last = sq(u[0][7]) + sq(u[1][7]) + sq(u[2][7])
    return (
        LAME * (t + t3 * (1.0 / 3.0))
        + SHEAR * (r + r2 + r2 + r3 * (1.0 / 3.0))
        + ((LAME + 4.0 * SHEAR) / 9.0) * last
    )


def side_rows(load, guess, occupancy, density):
    sub = lax.axis_index("sub")
    flat = lambda part: part.reshape((-1,) + part.shape[-2:])
    near = lambda part: jnp.where(sub == 0, part[..., 24:32, :], part[..., 0:8, :])
    fields = [flat(near(guess)), flat(near(load))]
    fields, occupancy, density = lax.optimization_barrier((fields, occupancy, density))
    return jnp.concatenate(fields + [stiff(near(occupancy), near(density))], axis=0)


def windows(sub, load, guess, bone, density, side):
    own = pl.ds(pl.multiple_of(8 * sub, 8), 32)
    rest = pl.ds(pl.multiple_of(32 * (1 - sub), 8), 8)

    def put_guess(out, at, c, k):
        out[c, at, own] = guess[c, k]
        out[c, at, rest] = side[8 * c + k]

    def put_load(out, at, c, k):
        out[c, at, own] = load[c, k]
        out[c, at, rest] = side[24 + 8 * c + k]

    def put_mod(out, at, k):
        out[at, own] = stiff(bone[k], density[k])
        out[at, rest] = side[48 + k]

    return put_guess, put_load, put_mod


def blank(pair, far):
    clear(pair)
    for m in range(6):
        for k in range(far.shape[1]):
            far[m, k, ROWS : ROWS + 8] = jnp.zeros((8, 128), jnp.float32)


def edge(
    load, guess, bone, density, side, up, down, guess_w, load_w, mods, pair, near, far
):
    put_guess, put_load, put_mod = windows(
        lax.axis_index("sub"), load, guess, bone, density, side
    )
    blank(pair, far)
    for at, k in enumerate((0, 1, 6, 7)):
        put_mod(mods, at, k)
    for c in range(3):
        for at, k in enumerate((0, 6, 7)):
            put_load(load_w, at, c, k)
        for at, k in enumerate((0, 1, 5, 6, 7)):
            put_guess(guess_w, at, c, k)
            enter(pair, at, c, guess_w[c, at])
    march(pair, 0, 1, lambda k, rows: mods[1, rows], near, far, 0)
    march(pair, 2, 2, lambda k, rows: mods[2 + k, rows], near, far, 2)
    inverse = inverted(mods[2], mods[3])
    for c in range(3):
        down[c] = guess_w[c, 0]
        down[3 + c] = load_w[c, 0] - image(near, far, 0, c)
        up[c] = guess_w[c, 4]
        up[3 + c] = load_w[c, 2] - image(near, far, 4, c)
        up[6 + c] = (load_w[c, 1] - image(near, far, 3, c)) * inverse
    up[9] = mods[3]
    down[6] = mods[0]
    down[7] = inverted(mods[0], mods[1])


def middle(
    count, load, guess, bone, density, side, bone_below, bone_above,
    smooth, guess_w, mod_w, inverse, inner_z, inner_s, near_m, far_m, sums,
    load_w, pair, near, far, pair_z, pair_s,
):
    put_guess, put_load, put_mod = windows(
        lax.axis_index("sub"), load, guess, bone, density, side
    )
    bone_z(count, bone, bone_below, bone_above, smooth)
    blank(pair, far)
    blank(pair_z, far_m)
    clear(pair_s)
    for k in range(8):
        put_mod(mod_w, k, k)
        for c in range(3):
            put_guess(guess_w, k, c, k)
            put_load(load_w, k, c, k)
    for k in range(7):
        inverse[k] = inverted(mod_w[k], mod_w[k + 1])

    def prepare(k, _):
        for c in range(3):
            enter(pair, k, c, guess_w[c, k])
        return 0

    lax.fori_loop(0, 8, prepare, 0)
    march(pair, 0, 7, lambda k, rows: mod_w[k + 1, rows], near, far, 0)
    sums[...] = jnp.zeros_like(sums)

    def settle_z(k, _):
        dot = 0.0
        for c in range(3):
            residual = load_w[c, k] - image(near, far, k, c)
            z = residual * inverse[k]
            inner_z[c, k - 1] = z
            enter(pair_z, k - 1, c, z)
            dot = dot + residual * z
        sums[0] += dot
        return 0

    lax.fori_loop(1, 7, settle_z, 0)
    march(pair_z, 0, 5, lambda k, rows: mod_w[k + 2, rows], near_m, far_m, 0)

    def settle_s(k, _):
        dot, cross = 0.0, 0.0
        for c in range(3):
            w = image(near_m, far_m, k - 1, c)
            s = w * inverse[k]
            inner_s[c, k - 2] = s
            enter(pair_s, k - 2, c, s)
            dot = dot + w * inner_z[c, k - 1]
            cross = cross + w * s
        sums[1] += dot
        sums[2] += cross
        return 0

    lax.fori_loop(2, 6, settle_s, 0)

    def use(k, tile, value):
        rows = slice(8 * tile, 8 * tile + 8)
        sums[3, rows] += value * mod_w[k + 3, rows]

    energy_march(pair_s, 0, 3, use)


def krylov(
    up, down, guess_w, mod_w, inverse, inner_z, inner_s, near_m, far_m, sums_in, low, high,
    bone, row_out, first, second, pair, near, far, mods, sums,
):
    sub = lax.axis_index("sub")
    run = lax.axis_index("run")
    own = pl.ds(pl.multiple_of(8 * sub, 8), 32)
    blank(pair, far)
    sums[...] = sums_in[...]
    mods[0] = low[9]
    for k in range(3):
        mods[1 + k] = mod_w[k]
    for k in range(2):
        mods[4 + k] = mod_w[6 + k]
    mods[6] = high[6]
    bottom = jnp.where(run > 0, inverted(low[9], mod_w[0]), 0.0)
    top = inverted(mod_w[7], high[6])

    for c in range(3):
        enter(pair, 0, c, low[c])
        enter(pair, 1, c, guess_w[c, 0])
        enter(pair, 2, c, guess_w[c, 7])
        enter(pair, 3, c, high[c])
    march(pair, 0, 1, lambda k, rows: mods[1, rows], near, far, 0)
    march(pair, 2, 1, lambda k, rows: mods[6, rows], near, far, 2)
    begun = (low, down, up, high)
    invert = (bottom, inverse[0], top, high[7])
    dot = 0.0
    ends = []
    for c in range(3):
        values = []
        for k in range(4):
            residual = begun[k][3 + c] - image(near, far, k, c)
            z = residual * invert[k]
            values.append(z)
            if k in (1, 2):
                dot = dot + residual * z
        first[c, 0] = values[0]
        first[c, 1] = values[1]
        for k in range(6):
            first[c, 2 + k] = inner_z[c, k]
        first[c, 8] = values[2]
        ends.append(values[3])
    sums[0] += dot

    for c in range(3):
        enter(pair, 0, c, low[6 + c])
        for k in range(3):
            enter(pair, 1 + k, c, first[c, k])
        enter(pair, 4, c, first[c, 7])
        enter(pair, 5, c, first[c, 8])
        enter(pair, 6, c, ends[c])
    march(pair, 0, 3, lambda k, rows: mods[k, rows], near, far, 0)
    march(pair, 4, 2, lambda k, rows: mods[5 + k, rows], near, far, 4)
    dot, cross = 0.0, 0.0
    for c in range(3):
        images = {
            -1: image(near, far, 1, c),
            0: image(near, far, 2, c),
            1: image(near, far, 3, c) + image(near_m, far_m, 0, c),
            6: image(near, far, 4, c) + image(near_m, far_m, 5, c),
            7: image(near, far, 5, c),
        }
        for k, w in images.items():
            s = w * (bottom if k < 0 else top if k == 7 else inverse[k])
            second[c, k + 1] = s
            if k >= 0:
                dot = dot + w * first[c, k + 1]
                cross = cross + w * s
        for k in range(2, 6):
            second[c, k + 1] = inner_s[c, k - 2]
    sums[1] += dot
    sums[2] += cross

    for c in range(3):
        for at, k in enumerate((-1, 0, 1, 2, 5, 6, 7)):
            enter(pair, at, c, second[c, k + 1])

    def use(first_mod):
        def add(k, tile, value):
            rows = slice(8 * tile, 8 * tile + 8)
            sums[3, rows] += value * mods[first_mod + k, rows]

        return add

    energy_march(pair, 0, 3, use(1))
    energy_march(pair, 4, 2, use(4))
    lane = lax.broadcasted_iota(jnp.int32, (1, 128), 1)
    line = jnp.zeros((1, 128), jnp.float32)
    for k in range(4):
        line = jnp.where(lane == k, whole(sums[k, own]), line)
    total = whole(jnp.sum(bone[...].astype(jnp.float32), axis=0))
    line = jnp.where(lane == 4, total, line)
    row_out[...] = jnp.broadcast_to(line, row_out.shape)


def pick(line, k):
    lane = lax.broadcasted_iota(jnp.int32, line.shape, 1)
    return jnp.sum(jnp.where(lane == k, line, 0.0), axis=1, keepdims=True)


def steplengths(lines):
    line = jnp.sum(lines[:, 32:40], axis=0)[0:1]
    a, b, c, e = (pick(line, k) for k in range(4))
    alpha = a / b
    fresh = alpha * alpha * c - a
    beta = fresh / a
    square = alpha * alpha * e - (1.0 + beta) * (1.0 + beta) * b
    after = fresh / square
    return alpha + after * (1.0 + beta), -after * alpha


def energies(
    lines, guess_w, low, first, second, occupancy, density, spread,
    smooth, pair, specific,
):
    sub = lax.axis_index("sub")
    own = pl.ds(pl.multiple_of(8 * sub, 8), 32)
    p, q = (jnp.broadcast_to(step, (ROWS, 128)) for step in steplengths(lines))
    clear(pair)
    for k in range(9):
        for c in range(3):
            start = guess_w[c, k - 1] if k else low[c]
            enter(pair, k, c, start + p * first[c, k] + q * second[c, k])

    def use(k, tile, value):
        specific[k, 8 * tile : 8 * tile + 8] = value

    energy_march(pair, 0, 8, use)
    parts = []
    for k in range(8):
        rho = density[k]
        share = jnp.where(occupancy[k] == 1, rho * rho / rho, 0.0)
        parts.append(0.5 * share * specific[k, own])
    row = lax.broadcasted_iota(jnp.int32, (128, 128), 0)
    col = lax.broadcasted_iota(jnp.int32, (128, 128), 1)
    gap = jnp.abs(row - col).astype(jnp.float32)
    band = jnp.where(gap <= REACH, NORM * jnp.exp(gap * (-1.0 / DECAY)), 0.0)
    value = jnp.dot(
        jnp.concatenate(parts, axis=0), band,
        precision=lax.Precision.HIGHEST, preferred_element_type=jnp.float32,
    )
    smooth[0:256] = value
    total = whole(value * spread[...].reshape(256, 128))
    smooth[256:264] = jnp.broadcast_to(total, (8, 128))


def decayed(block):
    upward, downward = 0.0, 0.0
    for k in range(8):
        upward = upward + math.exp(-(7 - k) / DECAY) * block[k]
        downward = downward + math.exp(-k / DECAY) * block[k]
    return upward, downward


def ladder(upward, downward, tile, out):
    run = lax.axis_index("run")
    for k in range(out.shape[0]):
        out[k, 0:32] = jnp.where(k > run, upward, downward)
        out[k, 32:40] = tile


def smooth_y(mine, other, planes=8):
    sub = lax.axis_index("sub")
    row = lax.broadcasted_iota(jnp.int32, (32, 32), 0)
    col = lax.broadcasted_iota(jnp.int32, (32, 32), 1)

    def band(offset):
        gap = jnp.abs(col + offset - row).astype(jnp.float32)
        return jnp.where(gap <= REACH, NORM * jnp.exp(gap * (-1.0 / DECAY)), 0.0)

    near = band(0)
    far = band(32 - 64 * sub)
    for k in range(planes):
        yield jnp.dot(
            near, mine(k), precision=lax.Precision.HIGHEST, preferred_element_type=jnp.float32
        ) + jnp.dot(
            far, other(k), precision=lax.Precision.HIGHEST, preferred_element_type=jnp.float32
        )


def bone_z(count, bone, below, above, out):
    blocks = [lambda j, ref=ref: ref[j].astype(jnp.float32) for ref in (bone, below, above)]
    for i, value in enumerate(far_z(count, *blocks)):
        out[i] = value
    out[8], out[9] = decayed([blocks[0](k) for k in range(8)])


def bone_y(mine, other, spread, rails):
    block = list(smooth_y(lambda k: mine[k], lambda k: other[k], 10))
    for k in range(8):
        spread[k] = block[k]
    rails[0], rails[1] = block[8], block[9]


def rungs(rails, mine, other, out):
    ladder(rails[0], rails[1], mine[...] + other[...], out)


def along_y(mine, other, out, planes):
    def at(ref):
        return lambda k: ref[32 * k : 32 * k + 32]

    block = list(smooth_y(at(mine), at(other)))
    for k in range(8):
        out[k] = block[k]
    ladder(*decayed(block), mine[256:264] + other[256:264], planes)


def near_z(count, planes, i):
    run = lax.axis_index("run")
    lower, upper = 0.0, 0.0
    for o in range(1, REACH // 8):
        scale = math.exp(-8.0 * (o - 1) / DECAY)
        at = jnp.maximum(run - o, 0)
        lower = lower + jnp.where(run - o >= 0, scale * planes[at, 0:32], 0.0)
        at = jnp.minimum(run + o, count - 1)
        upper = upper + jnp.where(run + o < count, scale * planes[at, 0:32], 0.0)
    return weight(i + 1) * lower + weight(8 - i) * upper


def far_z(count, mine, below, above):
    run = lax.axis_index("run")
    has_below = run - REACH // 8 >= 0
    has_above = run + REACH // 8 < count
    for i in range(8):
        value, far_below, far_above = 0.0, 0.0, 0.0
        for j in range(8):
            value = value + weight(abs(i - j)) * mine(j)
            if j >= i:
                far_below = far_below + weight(i - j + REACH) * below(j)
            if j <= i:
                far_above = far_above + weight(j - i + REACH) * above(j)
        yield value + jnp.where(has_below, far_below, 0.0) + jnp.where(has_above, far_above, 0.0)


def partial_z(
    count, mine, below, above, lines, guess, first, second, out, displacement
):
    blocks = [lambda j, ref=ref: ref[j] for ref in (mine, below, above)]
    for i, value in enumerate(far_z(count, *blocks)):
        out[i] = value
    own = pl.ds(pl.multiple_of(8 * lax.axis_index("sub"), 8), 32)
    p, q = (jnp.broadcast_to(step, (32, 128)) for step in steplengths(lines))
    for c in range(3):
        for k in range(8):
            displacement[c, k] = (
                guess[c, k] + p * first[c, k + 1, own] + q * second[c, k + 1, own]
            )


def spread_z(count, part, planes, out):
    for i in range(8):
        out[i] = part[i] + near_z(count, planes, i)


def remodel(count, part, planes, lines, bone, density, out):
    bones = jnp.sum(lines[:, 32:40], axis=0)[0:1]
    line = jnp.sum(planes[:, 32:40], axis=0)[0:1]
    scale = jnp.broadcast_to(pick(bones, 4) / line, density.shape[1:])
    for i in range(8):
        value = part[i] + near_z(count, planes, i)
        rho = density[i]
        updated = jnp.minimum(rho * (1.0 + RATE * jnp.tanh(SLOPE * (value * scale - 1.0))), 1.0)
        out[i] = jnp.where(bone[i] == 1, updated, rho)


def local(load, guess, occupancy, density):
    count = lax.axis_size("run")
    block = density.shape
    swap = [(0, 1), (1, 0)]
    side = lax.ppermute(side_rows(load, guess, occupancy, density), "sub", swap)
    inputs = [load, guess, occupancy, density, side]
    up, down = call(
        edge,
        [(10, ROWS, 128), (8, ROWS, 128)],
        inputs,
        [
            (3, 5, ROWS, 128), (3, 3, ROWS, 128), (4, ROWS, 128),
            (6, 5, 48, 128), (6, 5, ROWS, 128), (6, 5, 48, 128),
        ],
    )
    low = lax.ppermute(up, "run", [(i, i + 1) for i in range(count - 1)])
    high = lax.ppermute(down, "run", [(i + 1, i) for i in range(count - 1)])
    smooth, *kept = call(
        functools.partial(middle, count),
        [
            (10, 32, 128),
            (3, 8, ROWS, 128), (8, ROWS, 128), (7, ROWS, 128),
            (3, 6, ROWS, 128), (3, 4, ROWS, 128),
            (6, 6, ROWS, 128), (6, 6, 48, 128), (4, ROWS, 128),
        ],
        [*inputs, *far_slabs(occupancy)],
        [
            (3, 8, ROWS, 128), (6, 8, 48, 128), (6, 8, ROWS, 128), (6, 8, 48, 128),
            (6, 6, 48, 128), (6, 4, 48, 128),
        ],
    )
    guess_w = kept[0]
    line, first, second = call(
        krylov,
        [(8, 128), (3, 9, ROWS, 128), (3, 9, ROWS, 128)],
        [up, down, *kept, low, high, occupancy],
        [
            (6, 7, 48, 128), (6, 7, ROWS, 128), (6, 7, 48, 128),
            (7, ROWS, 128), (4, ROWS, 128),
        ],
    )
    spread, rails = call(
        bone_y, [block, (2, 32, 128)], [smooth, lax.ppermute(smooth, "sub", swap)]
    )
    (planes,) = call(
        rungs, [(count, 40, 128)], [rails, line, lax.ppermute(line, "sub", swap)]
    )
    planes = lax.all_to_all(planes, "run", 0, 0, tiled=True)
    lines = planes
    (spread,) = call(functools.partial(spread_z, count), [block], [spread, planes])
    (smooth,) = call(
        energies,
        [(264, 128)],
        [lines, guess_w, low, first, second, occupancy, density, spread],
        [(6, 9, 48, 128), (8, ROWS, 128)],
    )
    other = lax.ppermute(smooth, "sub", swap)
    smooth, planes = call(along_y, [block, (count, 40, 128)], [smooth, other])
    below, above = far_slabs(smooth)
    planes = lax.all_to_all(planes, "run", 0, 0, tiled=True)
    part, displacement = call(
        functools.partial(partial_z, count),
        [block, guess.shape],
        [smooth, below, above, lines, guess, first, second],
        flops=10**10,
    )
    (new_density,) = call(
        functools.partial(remodel, count),
        [block],
        [part, planes, lines, occupancy, density],
    )
    return displacement, new_density


def far_slabs(block):
    count = lax.axis_size("run")
    span = REACH // block.shape[0]
    rise = [(i, i + span) for i in range(count - span)]
    fall = [(i + span, i) for i in range(count - span)]
    if count <= 2 * span:
        both = lax.ppermute(block, "run", rise + fall)
        return both, both
    return lax.ppermute(block, "run", rise), lax.ppermute(block, "run", fall)


def solution(mesh):
    field = P(None, ("grp", "run"), "sub", None)
    cells = P(("grp", "run"), "sub", None)
    return jax.shard_map(
        local,
        mesh=mesh,
        in_specs=(field, field, cells, cells),
        out_specs=(field, cells),
        check_vma=False,
    )
```

```python
import functools
import math

import jax
import jax.numpy as jnp
from jax import lax
from jax.experimental import pallas as pl
from jax.experimental.pallas import tpu as pltpu
from jax.sharding import PartitionSpec as P

REACH = 32
POISSON = 0.3
MARROW = 0.05
RATE = 0.5
SLOPE = 4.0
DECAY = REACH / 4.0

LAME = POISSON / ((1.0 + POISSON) * (1.0 - 2.0 * POISSON)) / 16.0
SHEAR = 0.5 / (1.0 + POISSON) / 16.0
ENTRY = 16.0 * (LAME + 4.0 * SHEAR) / 9.0
NORM = 1.0 / sum(math.exp(-abs(k) / DECAY) for k in range(-REACH, REACH + 1))

ROWS = 40
PAIR = ("run", "sub")

VMEM = pl.BlockSpec(memory_space=pltpu.VMEM)


def weight(distance):
    return NORM * math.exp(-distance / DECAY)


def call(kernel, outs, ins, scratch=(), flops=None):
    cost = None
    if flops is not None:
        cost = pl.CostEstimate(flops=flops, bytes_accessed=2**20, transcendentals=0)
    return pl.pallas_call(
        kernel,
        out_shape=[jax.ShapeDtypeStruct(s, jnp.float32) for s in outs],
        in_specs=[VMEM] * len(ins),
        out_specs=[VMEM] * len(outs),
        scratch_shapes=[pltpu.VMEM(s, jnp.float32) for s in scratch],
        compiler_params=pltpu.CompilerParams(vmem_limit_bytes=40 * 1024 * 1024),
        cost_estimate=cost,
    )(*ins)


def lane_right(block):
    lane = lax.broadcasted_iota(jnp.int32, block.shape, 1)
    return jnp.where(lane == 0, 0.0, pltpu.roll(block, 1, 1))


def lane_left(block):
    lane = lax.broadcasted_iota(jnp.int32, block.shape, 1)
    return jnp.where(lane == block.shape[1] - 1, 0.0, pltpu.roll(block, block.shape[1] - 1, 1))


def row_down(block):
    row = lax.broadcasted_iota(jnp.int32, block.shape, 0)
    return jnp.where(row == block.shape[0] - 1, 0.0, pltpu.roll(block, block.shape[0] - 1, 0))


def stiff(occupancy, density):
    return jnp.where(occupancy == 1, density * density, MARROW)


def enter(pair, k, c, field):
    other = lane_right(field)
    pair[2 * c, k, 8:48] = field + other
    pair[2 * c + 1, k, 8:48] = field - other


def clear(pair):
    for m in range(6):
        for k in range(pair.shape[1]):
            pair[m, k, 0:8] = jnp.zeros((8, 128), jnp.float32)


def plane_modes(pair, k, tile):
    out = [None] * 12
    for c in range(3):
        for x in range(2):
            here = pair[2 * c + x, k, 8 + 8 * tile : 16 + 8 * tile]
            above = pair[2 * c + x, k, 7 + 8 * tile : 15 + 8 * tile]
            out[4 * c + x] = here + above
            out[4 * c + 2 + x] = here - above
    return out


def steps(count, body, carry, straight=3):
    if count <= straight:
        for k in range(count):
            carry = body(k, carry)
        return carry

    def turn(k, carry):
        return body(2 * k + 1, body(2 * k, carry))

    carry = lax.fori_loop(0, count // 2, turn, carry)
    return body(count - 1, carry) if count % 2 else carry


def march(pair, start, count, mod, near, far, to):
    for tile in range(ROWS // 8):
        rows = slice(8 * tile, 8 * tile + 8)

        def leave(k, totals):
            for c in range(3):
                for x in range(2):
                    s, d = totals[4 * c + x], totals[4 * c + 2 + x]
                    near[2 * c + x, k, rows] = s + d
                    far[2 * c + x, k, rows] = s - d

        def body(k, carry):
            low, kept = carry
            high = plane_modes(pair, start + k + 1, tile)
            g = stress(modes_of(low, high), mod(k, rows))
            totals, after = [None] * 12, [None] * 12
            for c in range(3):
                for m in range(4):
                    d = g[c][4 + m]
                    at = 4 * c + m
                    if m:
                        s = g[c][m]
                        totals[at] = kept[at] + (s - d)
                        after[at] = s + d
                    else:
                        totals[at] = kept[at] - d
                        after[at] = d
            leave(to + k, totals)
            return high, after

        zeros = [jnp.zeros((8, 128), jnp.float32)] * 12
        _, kept = steps(count, body, (plane_modes(pair, start, tile), zeros))
        leave(to + count, kept)


def image(near, far, k, c):
    columns = [
        near[2 * c + x, k, 0:ROWS] + far[2 * c + x, k, 1 : ROWS + 1] for x in range(2)
    ]
    return columns[0] + columns[1] + lane_left(columns[0] - columns[1])


def energy_march(pair, start, count, use, straight=3):
    for tile in range(ROWS // 8):

        def body(k, low):
            high = plane_modes(pair, start + k + 1, tile)
            use(k, tile, quadratic(modes_of(low, high)))
            return high

        steps(count, body, plane_modes(pair, start, tile), straight)


def inverted(low, high):
    t = low + high
    t = t + row_down(t)
    t = (t + lane_left(t)) * ENTRY
    return jnp.where(t > 0.0, 1.0 / jnp.where(t > 0.0, t, 1.0), 0.0)


def whole(block):
    return jnp.sum(jnp.sum(block, axis=0, keepdims=True), axis=1, keepdims=True)


def modes_of(low, high):
    out = []
    for c in range(3):
        modes = [None] * 8
        for m in range(4):
            if m:
                modes[m] = high[4 * c + m] + low[4 * c + m]
            modes[4 + m] = high[4 * c + m] - low[4 * c + m]
        out.append(modes)
    return out


X, Y, Z = 1, 2, 4


def stress(u, mod):
    g = [[None] * 8 for _ in range(3)]
    bulk, rigid = mod * LAME, mod * SHEAR
    twice = rigid + rigid
    bulk3, rigid3 = mod * (LAME / 3.0), mod * (SHEAR / 3.0)
    last = mod * ((LAME + 4.0 * SHEAR) / 9.0)
    t = (u[0][X] + u[1][Y] + u[2][Z]) * bulk
    g[0][X] = t + u[0][X] * twice
    g[1][Y] = t + u[1][Y] * twice
    g[2][Z] = t + u[2][Z] * twice
    g[0][Y] = g[1][X] = (u[0][Y] + u[1][X]) * rigid
    g[0][Z] = g[2][X] = (u[0][Z] + u[2][X]) * rigid
    g[1][Z] = g[2][Y] = (u[1][Z] + u[2][Y]) * rigid
    for (c, m), (d, n) in (
        ((1, X | Y), (2, X | Z)),
        ((0, X | Y), (2, Y | Z)),
        ((0, X | Z), (1, Y | Z)),
    ):
        s = (u[c][m] + u[d][n]) * bulk3
        g[c][m] = s + u[c][m] * rigid
        g[d][n] = s + u[d][n] * rigid
    s = u[0][Y | Z] + u[1][X | Z] + u[2][X | Y]
    g[0][Y | Z] = (s + u[0][Y | Z]) * rigid3
    g[1][X | Z] = (s + u[1][X | Z]) * rigid3
    g[2][X | Y] = (s + u[2][X | Y]) * rigid3
    for c in range(3):
        g[c][7] = u[c][7] * last
    return g


def quadratic(u):
    def sq(v):
        return v * v

    t = sq(u[0][X] + u[1][Y] + u[2][Z])
    r2 = sq(u[0][X]) + sq(u[1][Y]) + sq(u[2][Z])
    r = sq(u[0][Y] + u[1][X]) + sq(u[0][Z] + u[2][X]) + sq(u[1][Z] + u[2][Y])
    t3 = 0.0
    for (c, m), (d, n) in (
        ((1, X | Y), (2, X | Z)),
        ((0, X | Y), (2, Y | Z)),
        ((0, X | Z), (1, Y | Z)),
    ):
        t3 = t3 + sq(u[c][m] + u[d][n])
        r = r + (sq(u[c][m]) + sq(u[d][n]))
    p, q, s = u[0][Y | Z], u[1][X | Z], u[2][X | Y]
    r3 = sq(p + q) + sq(p + s) + sq(q + s)
    last = sq(u[0][7]) + sq(u[1][7]) + sq(u[2][7])
    return (
        LAME * (t + t3 * (1.0 / 3.0))
        + SHEAR * (r + r2 + r2 + r3 * (1.0 / 3.0))
        + ((LAME + 4.0 * SHEAR) / 9.0) * last
    )


def side_rows(load, guess, occupancy, density):
    sub = lax.axis_index("sub")
    flat = lambda part: part.reshape((-1,) + part.shape[-2:])
    near = lambda part: jnp.where(sub == 0, part[..., 24:32, :], part[..., 0:8, :])
    fields = [flat(near(guess)), flat(near(load))]
    fields, occupancy, density = lax.optimization_barrier((fields, occupancy, density))
    return jnp.concatenate(fields + [stiff(near(occupancy), near(density))], axis=0)


def windows(sub, load, guess, bone, density, side):
    own = pl.ds(pl.multiple_of(8 * sub, 8), 32)
    rest = pl.ds(pl.multiple_of(32 * (1 - sub), 8), 8)

    def put_guess(out, at, c, k):
        out[c, at, own] = guess[c, k]
        out[c, at, rest] = side[8 * c + k]

    def put_load(out, at, c, k):
        out[c, at, own] = load[c, k]
        out[c, at, rest] = side[24 + 8 * c + k]

    def put_mod(out, at, k):
        out[at, own] = stiff(bone[k], density[k])
        out[at, rest] = side[48 + k]

    return put_guess, put_load, put_mod


def blank(pair, far):
    clear(pair)
    for m in range(6):
        for k in range(far.shape[1]):
            far[m, k, ROWS : ROWS + 8] = jnp.zeros((8, 128), jnp.float32)


def edge(
    load, guess, bone, density, side, up, down, guess_w, load_w, mods, pair, near, far
):
    put_guess, put_load, put_mod = windows(
        lax.axis_index("sub"), load, guess, bone, density, side
    )
    blank(pair, far)
    for at, k in enumerate((0, 1, 6, 7)):
        put_mod(mods, at, k)
    for c in range(3):
        for at, k in enumerate((0, 6, 7)):
            put_load(load_w, at, c, k)
        for at, k in enumerate((0, 1, 5, 6, 7)):
            put_guess(guess_w, at, c, k)
            enter(pair, at, c, guess_w[c, at])
    march(pair, 0, 1, lambda k, rows: mods[1, rows], near, far, 0)
    march(pair, 2, 2, lambda k, rows: mods[2 + k, rows], near, far, 2)
    inverse = inverted(mods[2], mods[3])
    for c in range(3):
        down[c] = guess_w[c, 0]
        down[3 + c] = load_w[c, 0] - image(near, far, 0, c)
        up[c] = guess_w[c, 4]
        up[3 + c] = load_w[c, 2] - image(near, far, 4, c)
        up[6 + c] = (load_w[c, 1] - image(near, far, 3, c)) * inverse
    up[9] = mods[3]
    down[6] = mods[0]
    down[7] = inverted(mods[0], mods[1])


def middle(
    load, guess, bone, density, side,
    guess_w, mod_w, inverse, inner_z, inner_s, near_m, far_m, sums,
    load_w, pair, near, far, pair_z, pair_s,
):
    put_guess, put_load, put_mod = windows(
        lax.axis_index("sub"), load, guess, bone, density, side
    )
    blank(pair, far)
    blank(pair_z, far_m)
    clear(pair_s)
    for k in range(8):
        put_mod(mod_w, k, k)
        for c in range(3):
            put_guess(guess_w, k, c, k)
            put_load(load_w, k, c, k)
    for k in range(7):
        inverse[k] = inverted(mod_w[k], mod_w[k + 1])

    def prepare(k, _):
        for c in range(3):
            enter(pair, k, c, guess_w[c, k])
        return 0

    lax.fori_loop(0, 8, prepare, 0)
    march(pair, 0, 7, lambda k, rows: mod_w[k + 1, rows], near, far, 0)
    sums[...] = jnp.zeros_like(sums)

    def settle_z(k, _):
        dot = 0.0
        for c in range(3):
            residual = load_w[c, k] - image(near, far, k, c)
            z = residual * inverse[k]
            inner_z[c, k - 1] = z
            enter(pair_z, k - 1, c, z)
            dot = dot + residual * z
        sums[0] += dot
        return 0

    lax.fori_loop(1, 7, settle_z, 0)
    march(pair_z, 0, 5, lambda k, rows: mod_w[k + 2, rows], near_m, far_m, 0)

    def settle_s(k, _):
        dot, cross = 0.0, 0.0
        for c in range(3):
            w = image(near_m, far_m, k - 1, c)
            s = w * inverse[k]
            inner_s[c, k - 2] = s
            enter(pair_s, k - 2, c, s)
            dot = dot + w * inner_z[c, k - 1]
            cross = cross + w * s
        sums[1] += dot
        sums[2] += cross
        return 0

    lax.fori_loop(2, 6, settle_s, 0)

    def use(k, tile, value):
        rows = slice(8 * tile, 8 * tile + 8)
        sums[3, rows] += value * mod_w[k + 3, rows]

    energy_march(pair_s, 0, 3, use)


def krylov(
    up, down, guess_w, mod_w, inverse, inner_z, inner_s, near_m, far_m, sums_in, low, high,
    bone, row_out, first, second, pair, near, far, mods, sums,
):
    sub = lax.axis_index("sub")
    run = lax.axis_index("run")
    own = pl.ds(pl.multiple_of(8 * sub, 8), 32)
    blank(pair, far)
    sums[...] = sums_in[...]
    mods[0] = low[9]
    for k in range(3):
        mods[1 + k] = mod_w[k]
    for k in range(2):
        mods[4 + k] = mod_w[6 + k]
    mods[6] = high[6]
    bottom = jnp.where(run > 0, inverted(low[9], mod_w[0]), 0.0)
    top = inverted(mod_w[7], high[6])

    for c in range(3):
        enter(pair, 0, c, low[c])
        enter(pair, 1, c, guess_w[c, 0])
        enter(pair, 2, c, guess_w[c, 7])
        enter(pair, 3, c, high[c])
    march(pair, 0, 1, lambda k, rows: mods[1, rows], near, far, 0)
    march(pair, 2, 1, lambda k, rows: mods[6, rows], near, far, 2)
    begun = (low, down, up, high)
    invert = (bottom, inverse[0], top, high[7])
    dot = 0.0
    ends = []
    for c in range(3):
        values = []
        for k in range(4):
            residual = begun[k][3 + c] - image(near, far, k, c)
            z = residual * invert[k]
            values.append(z)
            if k in (1, 2):
                dot = dot + residual * z
        first[c, 0] = values[0]
        first[c, 1] = values[1]
        for k in range(6):
            first[c, 2 + k] = inner_z[c, k]
        first[c, 8] = values[2]
        ends.append(values[3])
    sums[0] += dot

    for c in range(3):
        enter(pair, 0, c, low[6 + c])
        for k in range(3):
            enter(pair, 1 + k, c, first[c, k])
        enter(pair, 4, c, first[c, 7])
        enter(pair, 5, c, first[c, 8])
        enter(pair, 6, c, ends[c])
    march(pair, 0, 3, lambda k, rows: mods[k, rows], near, far, 0)
    march(pair, 4, 2, lambda k, rows: mods[5 + k, rows], near, far, 4)
    dot, cross = 0.0, 0.0
    for c in range(3):
        images = {
            -1: image(near, far, 1, c),
            0: image(near, far, 2, c),
            1: image(near, far, 3, c) + image(near_m, far_m, 0, c),
            6: image(near, far, 4, c) + image(near_m, far_m, 5, c),
            7: image(near, far, 5, c),
        }
        for k, w in images.items():
            s = w * (bottom if k < 0 else top if k == 7 else inverse[k])
            second[c, k + 1] = s
            if k >= 0:
                dot = dot + w * first[c, k + 1]
                cross = cross + w * s
        for k in range(2, 6):
            second[c, k + 1] = inner_s[c, k - 2]
    sums[1] += dot
    sums[2] += cross

    for c in range(3):
        for at, k in enumerate((-1, 0, 1, 2, 5, 6, 7)):
            enter(pair, at, c, second[c, k + 1])

    def use(first_mod):
        def add(k, tile, value):
            rows = slice(8 * tile, 8 * tile + 8)
            sums[3, rows] += value * mods[first_mod + k, rows]

        return add

    energy_march(pair, 0, 3, use(1))
    energy_march(pair, 4, 2, use(4))
    lane = lax.broadcasted_iota(jnp.int32, (1, 128), 1)
    line = jnp.zeros((1, 128), jnp.float32)
    for k in range(4):
        line = jnp.where(lane == k, whole(sums[k, own]), line)
    total = whole(jnp.sum(bone[...].astype(jnp.float32), axis=0))
    line = jnp.where(lane == 4, total, line)
    row_out[...] = jnp.broadcast_to(line, row_out.shape)


def pick(line, k):
    lane = lax.broadcasted_iota(jnp.int32, line.shape, 1)
    return jnp.sum(jnp.where(lane == k, line, 0.0), axis=1, keepdims=True)


def steplengths(lines):
    line = jnp.sum(lines[:, 32:40], axis=0)[0:1]
    a, b, c, e = (pick(line, k) for k in range(4))
    alpha = a / b
    fresh = alpha * alpha * c - a
    beta = fresh / a
    square = alpha * alpha * e - (1.0 + beta) * (1.0 + beta) * b
    after = fresh / square
    return alpha + after * (1.0 + beta), -after * alpha


def energies(
    lines, guess_w, low, first, second, occupancy, density, spread,
    smooth, pair, specific,
):
    sub = lax.axis_index("sub")
    own = pl.ds(pl.multiple_of(8 * sub, 8), 32)
    p, q = (jnp.broadcast_to(step, (ROWS, 128)) for step in steplengths(lines))
    clear(pair)
    for k in range(9):
        for c in range(3):
            start = guess_w[c, k - 1] if k else low[c]
            enter(pair, k, c, start + p * first[c, k] + q * second[c, k])

    def use(k, tile, value):
        specific[k, 8 * tile : 8 * tile + 8] = value

    energy_march(pair, 0, 8, use, 8)
    parts = []
    for k in range(8):
        rho = density[k]
        share = jnp.where(occupancy[k] == 1, rho * rho / rho, 0.0)
        parts.append(0.5 * share * specific[k, own])
    row = lax.broadcasted_iota(jnp.int32, (128, 128), 0)
    col = lax.broadcasted_iota(jnp.int32, (128, 128), 1)
    gap = jnp.abs(row - col).astype(jnp.float32)
    band = jnp.where(gap <= REACH, NORM * jnp.exp(gap * (-1.0 / DECAY)), 0.0)
    value = jnp.dot(
        jnp.concatenate(parts, axis=0), band,
        precision=lax.Precision.HIGHEST, preferred_element_type=jnp.float32,
    )
    smooth[0:256] = value
    total = whole(value * spread[...].reshape(256, 128))
    smooth[256:264] = jnp.broadcast_to(total, (8, 128))


def decayed(block):
    upward, downward = 0.0, 0.0
    for k in range(8):
        upward = upward + math.exp(-(7 - k) / DECAY) * block[k]
        downward = downward + math.exp(-k / DECAY) * block[k]
    return upward, downward


def ladder(upward, downward, tile, out):
    run = lax.axis_index("run")
    for k in range(out.shape[0]):
        out[k, 0:32] = jnp.where(k > run, upward, downward)
        out[k, 32:40] = tile


def smooth_y(mine, other, planes=8):
    sub = lax.axis_index("sub")
    row = lax.broadcasted_iota(jnp.int32, (32, 32), 0)
    col = lax.broadcasted_iota(jnp.int32, (32, 32), 1)

    def band(offset):
        gap = jnp.abs(col + offset - row).astype(jnp.float32)
        return jnp.where(gap <= REACH, NORM * jnp.exp(gap * (-1.0 / DECAY)), 0.0)

    near = band(0)
    far = band(32 - 64 * sub)
    for k in range(planes):
        yield jnp.dot(
            near, mine(k), precision=lax.Precision.HIGHEST, preferred_element_type=jnp.float32
        ) + jnp.dot(
            far, other(k), precision=lax.Precision.HIGHEST, preferred_element_type=jnp.float32
        )


def bone_z(count, bone, below, above, _, out):
    blocks = [lambda j, ref=ref: ref[j].astype(jnp.float32) for ref in (bone, below, above)]
    for i, (own, far) in enumerate(zip(own_z(blocks[0]), far_z(count, *blocks[1:]))):
        out[i] = own + far
    out[8], out[9] = decayed([blocks[0](k) for k in range(8)])


def bone_y(mine, other, spread, rails):
    block = list(smooth_y(lambda k: mine[k], lambda k: other[k], 10))
    for k in range(8):
        spread[k] = block[k]
    rails[0], rails[1] = block[8], block[9]


def rungs(rails, mine, other, out):
    ladder(rails[0], rails[1], mine[...] + other[...], out)


def along_y(mine, other, out, planes):
    def at(ref):
        return lambda k: ref[32 * k : 32 * k + 32]

    block = list(smooth_y(at(mine), at(other)))
    for k in range(8):
        out[k] = block[k]
    ladder(*decayed(block), mine[256:264] + other[256:264], planes)


def near_z(count, planes):
    run = lax.axis_index("run")
    lower, upper = 0.0, 0.0
    for o in range(1, REACH // 8):
        scale = math.exp(-8.0 * (o - 1) / DECAY)
        at = jnp.maximum(run - o, 0)
        lower = lower + jnp.where(run - o >= 0, scale * planes[at, 0:32], 0.0)
        at = jnp.minimum(run + o, count - 1)
        upper = upper + jnp.where(run + o < count, scale * planes[at, 0:32], 0.0)
    return [weight(i + 1) * lower + weight(8 - i) * upper for i in range(8)]


def own_z(mine):
    for i in range(8):
        value = 0.0
        for j in range(8):
            value = value + weight(abs(i - j)) * mine(j)
        yield value


def far_z(count, below, above):
    run = lax.axis_index("run")
    has_below = run - REACH // 8 >= 0
    has_above = run + REACH // 8 < count
    for i in range(8):
        far_below, far_above = 0.0, 0.0
        for j in range(8):
            if j >= i:
                far_below = far_below + weight(i - j + REACH) * below(j)
            if j <= i:
                far_above = far_above + weight(j - i + REACH) * above(j)
        yield jnp.where(has_below, far_below, 0.0) + jnp.where(has_above, far_above, 0.0)


def distant_z(count, below, above, lines, guess, first, second, out, displacement):
    blocks = [lambda j, ref=ref: ref[32 * j : 32 * j + 32] for ref in (below, above)]
    for i, value in enumerate(far_z(count, *blocks)):
        out[i] = value
    own = pl.ds(pl.multiple_of(8 * lax.axis_index("sub"), 8), 32)
    p, q = (jnp.broadcast_to(step, (32, 128)) for step in steplengths(lines))
    for c in range(3):
        for k in range(8):
            displacement[c, k] = (
                guess[c, k] + p * first[c, k + 1, own] + q * second[c, k + 1, own]
            )


def distant_y(smooth, mine, other, out):
    far = smooth_y(lambda k: mine[k], lambda k: other[k])
    for i, (near, value) in enumerate(zip(own_z(lambda j: smooth[j]), far)):
        out[i] = near + value


def spread_z(count, part, planes, out):
    for i, share in enumerate(near_z(count, planes)):
        out[i] = part[i] + share


def remodel(count, part, planes, lines, bone, density, out):
    bones = jnp.sum(lines[:, 32:40], axis=0)[0:1]
    line = jnp.sum(planes[:, 32:40], axis=0)[0:1]
    scale = jnp.broadcast_to(pick(bones, 4) / line, density.shape[1:])
    for i, share in enumerate(near_z(count, planes)):
        value = part[i] + share
        rho = density[i]
        updated = jnp.minimum(rho * (1.0 + RATE * jnp.tanh(SLOPE * (value * scale - 1.0))), 1.0)
        out[i] = jnp.where(bone[i] == 1, updated, rho)


def local(load, guess, occupancy, density):
    count = lax.axis_size("run")
    block = density.shape
    depth = block[0]
    swap = [(0, 1), (1, 0)]
    side = lax.ppermute(side_rows(load, guess, occupancy, density), "sub", swap)
    inputs = [load, guess, occupancy, density, side]
    up, down = call(
        edge,
        [(10, ROWS, 128), (8, ROWS, 128)],
        inputs,
        [
            (3, 5, ROWS, 128), (3, 3, ROWS, 128), (4, ROWS, 128),
            (6, 5, 48, 128), (6, 5, ROWS, 128), (6, 5, 48, 128),
        ],
    )
    low = lax.ppermute(up, "run", [(i, i + 1) for i in range(count - 1)])
    high = lax.ppermute(down, "run", [(i + 1, i) for i in range(count - 1)])
    kept = call(
        middle,
        [
            (3, 8, ROWS, 128), (8, ROWS, 128), (7, ROWS, 128),
            (3, 6, ROWS, 128), (3, 4, ROWS, 128),
            (6, 6, ROWS, 128), (6, 6, 48, 128), (4, ROWS, 128),
        ],
        inputs,
        [
            (3, 8, ROWS, 128), (6, 8, 48, 128), (6, 8, ROWS, 128), (6, 8, 48, 128),
            (6, 6, 48, 128), (6, 4, 48, 128),
        ],
    )
    guess_w = kept[0]
    line, first, second = call(
        krylov,
        [(8, 128), (3, 9, ROWS, 128), (3, 9, ROWS, 128)],
        [up, down, *kept, low, high, occupancy],
        [
            (6, 7, 48, 128), (6, 7, ROWS, 128), (6, 7, 48, 128),
            (7, ROWS, 128), (4, ROWS, 128),
        ],
    )
    (smooth,) = call(
        functools.partial(bone_z, count), [(10, 32, 128)], [occupancy, *far_slabs(occupancy, depth), kept[-1]]
    )
    spread, rails = call(
        bone_y, [block, (2, 32, 128)], [smooth, lax.ppermute(smooth, "sub", swap)]
    )
    (planes,) = call(
        rungs, [(count, 40, 128)], [rails, line, lax.ppermute(line, "sub", swap)]
    )
    planes = lax.all_to_all(planes, "run", 0, 0, tiled=True)
    lines = planes
    (spread,) = call(functools.partial(spread_z, count), [block], [spread, planes])
    (smooth,) = call(
        energies,
        [(264, 128)],
        [lines, guess_w, low, first, second, occupancy, density, spread],
        [(6, 9, 48, 128), (8, ROWS, 128)],
    )
    below, above = far_slabs(smooth, depth)
    other = lax.ppermute(smooth, "sub", swap)
    smooth, planes = call(along_y, [block, (count, 40, 128)], [smooth, other])
    planes = lax.all_to_all(planes, "run", 0, 0, tiled=True)
    distant, displacement = call(
        functools.partial(distant_z, count),
        [block, guess.shape],
        [below, above, lines, guess, first, second],
        flops=10**10,
    )
    (part,) = call(
        distant_y, [block], [smooth, distant, lax.ppermute(distant, "sub", swap)]
    )
    (new_density,) = call(
        functools.partial(remodel, count),
        [block],
        [part, planes, lines, occupancy, density],
    )
    return displacement, new_density


def far_slabs(block, depth):
    count = lax.axis_size("run")
    span = REACH // depth
    rise = [(i, i + span) for i in range(count - span)]
    fall = [(i + span, i) for i in range(count - span)]
    if count <= 2 * span:
        both = lax.ppermute(block, "run", rise + fall)
        return both, both
    return lax.ppermute(block, "run", rise), lax.ppermute(block, "run", fall)


def solution(mesh):
    field = P(None, ("grp", "run"), "sub", None)
    cells = P(("grp", "run"), "sub", None)
    return jax.shard_map(
        local,
        mesh=mesh,
        in_specs=(field, field, cells, cells),
        out_specs=(field, cells),
        check_vma=False,
    )
```

```python
import functools
import math

import jax
import jax.numpy as jnp
from jax import lax
from jax.experimental import pallas as pl
from jax.experimental.pallas import tpu as pltpu
from jax.sharding import PartitionSpec as P

REACH = 32
POISSON = 0.3
MARROW = 0.05
RATE = 0.5
SLOPE = 4.0
DECAY = REACH / 4.0

LAME = POISSON / ((1.0 + POISSON) * (1.0 - 2.0 * POISSON)) / 16.0
SHEAR = 0.5 / (1.0 + POISSON) / 16.0
ENTRY = 16.0 * (LAME + 4.0 * SHEAR) / 9.0
NORM = 1.0 / sum(math.exp(-abs(k) / DECAY) for k in range(-REACH, REACH + 1))

ROWS = 40
PAIR = ("run", "sub")

VMEM = pl.BlockSpec(memory_space=pltpu.VMEM)


def weight(distance):
    return NORM * math.exp(-distance / DECAY)


def call(kernel, outs, ins, scratch=(), flops=None):
    cost = None
    if flops is not None:
        cost = pl.CostEstimate(flops=flops, bytes_accessed=2**20, transcendentals=0)
    return pl.pallas_call(
        kernel,
        out_shape=[jax.ShapeDtypeStruct(s, jnp.float32) for s in outs],
        in_specs=[VMEM] * len(ins),
        out_specs=[VMEM] * len(outs),
        scratch_shapes=[pltpu.VMEM(s, jnp.float32) for s in scratch],
        compiler_params=pltpu.CompilerParams(vmem_limit_bytes=40 * 1024 * 1024),
        cost_estimate=cost,
    )(*ins)


def lane_right(block):
    lane = lax.broadcasted_iota(jnp.int32, block.shape, 1)
    return jnp.where(lane == 0, 0.0, pltpu.roll(block, 1, 1))


def lane_left(block):
    lane = lax.broadcasted_iota(jnp.int32, block.shape, 1)
    return jnp.where(lane == block.shape[1] - 1, 0.0, pltpu.roll(block, block.shape[1] - 1, 1))


def row_down(block):
    row = lax.broadcasted_iota(jnp.int32, block.shape, 0)
    return jnp.where(row == block.shape[0] - 1, 0.0, pltpu.roll(block, block.shape[0] - 1, 0))


def stiff(occupancy, density):
    return jnp.where(occupancy == 1, density * density, MARROW)


def enter(pair, k, c, field):
    other = lane_right(field)
    pair[2 * c, k, 8:48] = field + other
    pair[2 * c + 1, k, 8:48] = field - other


def clear(pair):
    for m in range(6):
        for k in range(pair.shape[1]):
            pair[m, k, 0:8] = jnp.zeros((8, 128), jnp.float32)


def plane_modes(pair, k, tile):
    out = [None] * 12
    for c in range(3):
        for x in range(2):
            here = pair[2 * c + x, k, 8 + 8 * tile : 16 + 8 * tile]
            above = pair[2 * c + x, k, 7 + 8 * tile : 15 + 8 * tile]
            out[4 * c + x] = here + above
            out[4 * c + 2 + x] = here - above
    return out


def steps(count, body, carry, straight=3):
    if count <= straight:
        for k in range(count):
            carry = body(k, carry)
        return carry

    def turn(k, carry):
        return body(2 * k + 1, body(2 * k, carry))

    carry = lax.fori_loop(0, count // 2, turn, carry)
    return body(count - 1, carry) if count % 2 else carry


def march(pair, start, count, mod, near, far, to):
    for tile in range(ROWS // 8):
        rows = slice(8 * tile, 8 * tile + 8)

        def leave(k, totals):
            for c in range(3):
                for x in range(2):
                    s, d = totals[4 * c + x], totals[4 * c + 2 + x]
                    near[2 * c + x, k, rows] = s + d
                    far[2 * c + x, k, rows] = s - d

        def body(k, carry):
            low, kept = carry
            high = plane_modes(pair, start + k + 1, tile)
            g = stress(modes_of(low, high), mod(k, rows))
            totals, after = [None] * 12, [None] * 12
            for c in range(3):
                for m in range(4):
                    d = g[c][4 + m]
                    at = 4 * c + m
                    if m:
                        s = g[c][m]
                        totals[at] = kept[at] + (s - d)
                        after[at] = s + d
                    else:
                        totals[at] = kept[at] - d
                        after[at] = d
            leave(to + k, totals)
            return high, after

        zeros = [jnp.zeros((8, 128), jnp.float32)] * 12
        _, kept = steps(count, body, (plane_modes(pair, start, tile), zeros))
        leave(to + count, kept)


def image(near, far, k, c):
    columns = [
        near[2 * c + x, k, 0:ROWS] + far[2 * c + x, k, 1 : ROWS + 1] for x in range(2)
    ]
    return columns[0] + columns[1] + lane_left(columns[0] - columns[1])


def energy_march(pair, start, count, use, straight=3):
    for tile in range(ROWS // 8):

        def body(k, low):
            high = plane_modes(pair, start + k + 1, tile)
            use(k, tile, quadratic(modes_of(low, high)))
            return high

        steps(count, body, plane_modes(pair, start, tile), straight)


def inverted(low, high):
    t = low + high
    t = t + row_down(t)
    t = (t + lane_left(t)) * ENTRY
    return jnp.where(t > 0.0, 1.0 / jnp.where(t > 0.0, t, 1.0), 0.0)


def whole(block):
    return jnp.sum(jnp.sum(block, axis=0, keepdims=True), axis=1, keepdims=True)


def modes_of(low, high):
    out = []
    for c in range(3):
        modes = [None] * 8
        for m in range(4):
            if m:
                modes[m] = high[4 * c + m] + low[4 * c + m]
            modes[4 + m] = high[4 * c + m] - low[4 * c + m]
        out.append(modes)
    return out


X, Y, Z = 1, 2, 4


def stress(u, mod):
    g = [[None] * 8 for _ in range(3)]
    bulk, rigid = mod * LAME, mod * SHEAR
    twice = rigid + rigid
    bulk3, rigid3 = mod * (LAME / 3.0), mod * (SHEAR / 3.0)
    last = mod * ((LAME + 4.0 * SHEAR) / 9.0)
    t = (u[0][X] + u[1][Y] + u[2][Z]) * bulk
    g[0][X] = t + u[0][X] * twice
    g[1][Y] = t + u[1][Y] * twice
    g[2][Z] = t + u[2][Z] * twice
    g[0][Y] = g[1][X] = (u[0][Y] + u[1][X]) * rigid
    g[0][Z] = g[2][X] = (u[0][Z] + u[2][X]) * rigid
    g[1][Z] = g[2][Y] = (u[1][Z] + u[2][Y]) * rigid
    for (c, m), (d, n) in (
        ((1, X | Y), (2, X | Z)),
        ((0, X | Y), (2, Y | Z)),
        ((0, X | Z), (1, Y | Z)),
    ):
        s = (u[c][m] + u[d][n]) * bulk3
        g[c][m] = s + u[c][m] * rigid
        g[d][n] = s + u[d][n] * rigid
    s = u[0][Y | Z] + u[1][X | Z] + u[2][X | Y]
    g[0][Y | Z] = (s + u[0][Y | Z]) * rigid3
    g[1][X | Z] = (s + u[1][X | Z]) * rigid3
    g[2][X | Y] = (s + u[2][X | Y]) * rigid3
    for c in range(3):
        g[c][7] = u[c][7] * last
    return g


def quadratic(u):
    def sq(v):
        return v * v

    t = sq(u[0][X] + u[1][Y] + u[2][Z])
    r2 = sq(u[0][X]) + sq(u[1][Y]) + sq(u[2][Z])
    r = sq(u[0][Y] + u[1][X]) + sq(u[0][Z] + u[2][X]) + sq(u[1][Z] + u[2][Y])
    t3 = 0.0
    for (c, m), (d, n) in (
        ((1, X | Y), (2, X | Z)),
        ((0, X | Y), (2, Y | Z)),
        ((0, X | Z), (1, Y | Z)),
    ):
        t3 = t3 + sq(u[c][m] + u[d][n])
        r = r + (sq(u[c][m]) + sq(u[d][n]))
    p, q, s = u[0][Y | Z], u[1][X | Z], u[2][X | Y]
    r3 = sq(p + q) + sq(p + s) + sq(q + s)
    last = sq(u[0][7]) + sq(u[1][7]) + sq(u[2][7])
    return (
        LAME * (t + t3 * (1.0 / 3.0))
        + SHEAR * (r + r2 + r2 + r3 * (1.0 / 3.0))
        + ((LAME + 4.0 * SHEAR) / 9.0) * last
    )


def side_rows(load, guess, occupancy, density):
    sub = lax.axis_index("sub")
    flat = lambda part: part.reshape((-1,) + part.shape[-2:])
    near = lambda part: jnp.where(sub == 0, part[..., 24:32, :], part[..., 0:8, :])
    fields = [flat(near(guess)), flat(near(load))]
    fields, occupancy, density = lax.optimization_barrier((fields, occupancy, density))
    return jnp.concatenate(fields + [stiff(near(occupancy), near(density))], axis=0)


def windows(sub, load, guess, bone, density, side):
    own = pl.ds(pl.multiple_of(8 * sub, 8), 32)
    rest = pl.ds(pl.multiple_of(32 * (1 - sub), 8), 8)

    def put_guess(out, at, c, k):
        out[c, at, own] = guess[c, k]
        out[c, at, rest] = side[8 * c + k]

    def put_load(out, at, c, k):
        out[c, at, own] = load[c, k]
        out[c, at, rest] = side[24 + 8 * c + k]

    def put_mod(out, at, k):
        out[at, own] = stiff(bone[k], density[k])
        out[at, rest] = side[48 + k]

    return put_guess, put_load, put_mod


def blank(pair, far):
    clear(pair)
    for m in range(6):
        for k in range(far.shape[1]):
            far[m, k, ROWS : ROWS + 8] = jnp.zeros((8, 128), jnp.float32)


def narrow(wide, out):
    sub = lax.axis_index("sub")
    own = pl.ds(pl.multiple_of(8 * sub, 8), 32)
    planes = wide.shape[0]
    out[planes] = jnp.zeros((32, 128), jnp.float32)
    for k in range(planes):
        out[k] = wide[k, own]
        out[planes, 3 * k : 3 * k + 3] = jnp.where(sub == 0, wide[k, 32:35], wide[k, 5:8])


def widen(sent, out):
    sub = lax.axis_index("sub")
    own = pl.ds(pl.multiple_of(8 * sub, 8), 32)
    rest = pl.ds(pl.multiple_of(32 * (1 - sub), 8), 8)
    planes = out.shape[0]
    gap = jnp.zeros((5, 128), jnp.float32)
    for k in range(planes):
        rows = sent[planes, 3 * k : 3 * k + 3]
        out[k, own] = sent[k]
        out[k, rest] = jnp.where(
            sub == 0,
            jnp.concatenate([rows, gap], axis=0),
            jnp.concatenate([gap, rows], axis=0),
        )


def edge(
    load, guess, bone, density, side, up, down, up_sent, down_sent, guess_w, load_w, mods, pair, near, far
):
    put_guess, put_load, put_mod = windows(
        lax.axis_index("sub"), load, guess, bone, density, side
    )
    blank(pair, far)
    for at, k in enumerate((0, 1, 6, 7)):
        put_mod(mods, at, k)
    for c in range(3):
        for at, k in enumerate((0, 6, 7)):
            put_load(load_w, at, c, k)
        for at, k in enumerate((0, 1, 5, 6, 7)):
            put_guess(guess_w, at, c, k)
            enter(pair, at, c, guess_w[c, at])
    march(pair, 0, 1, lambda k, rows: mods[1, rows], near, far, 0)
    march(pair, 2, 2, lambda k, rows: mods[2 + k, rows], near, far, 2)
    inverse = inverted(mods[2], mods[3])
    for c in range(3):
        down[c] = guess_w[c, 0]
        down[3 + c] = load_w[c, 0] - image(near, far, 0, c)
        up[c] = guess_w[c, 4]
        up[3 + c] = load_w[c, 2] - image(near, far, 4, c)
        up[6 + c] = (load_w[c, 1] - image(near, far, 3, c)) * inverse
    up[9] = mods[3]
    down[6] = mods[0]
    down[7] = inverted(mods[0], mods[1])
    narrow(up, up_sent)
    narrow(down, down_sent)


def middle(
    load, guess, bone, density, side,
    guess_w, mod_w, inverse, inner_z, inner_s, near_m, far_m, sums,
    load_w, pair, near, far, pair_z, pair_s,
):
    put_guess, put_load, put_mod = windows(
        lax.axis_index("sub"), load, guess, bone, density, side
    )
    blank(pair, far)
    blank(pair_z, far_m)
    clear(pair_s)
    for k in range(8):
        put_mod(mod_w, k, k)
        for c in range(3):
            put_guess(guess_w, k, c, k)
            put_load(load_w, k, c, k)
    for k in range(7):
        inverse[k] = inverted(mod_w[k], mod_w[k + 1])

    def prepare(k, _):
        for c in range(3):
            enter(pair, k, c, guess_w[c, k])
        return 0

    lax.fori_loop(0, 8, prepare, 0)
    march(pair, 0, 7, lambda k, rows: mod_w[k + 1, rows], near, far, 0)
    sums[...] = jnp.zeros_like(sums)

    def settle_z(k, _):
        dot = 0.0
        for c in range(3):
            residual = load_w[c, k] - image(near, far, k, c)
            z = residual * inverse[k]
            inner_z[c, k - 1] = z
            enter(pair_z, k - 1, c, z)
            dot = dot + residual * z
        sums[0] += dot
        return 0

    lax.fori_loop(1, 7, settle_z, 0)
    march(pair_z, 0, 5, lambda k, rows: mod_w[k + 2, rows], near_m, far_m, 0)

    def settle_s(k, _):
        dot, cross = 0.0, 0.0
        for c in range(3):
            w = image(near_m, far_m, k - 1, c)
            s = w * inverse[k]
            inner_s[c, k - 2] = s
            enter(pair_s, k - 2, c, s)
            dot = dot + w * inner_z[c, k - 1]
            cross = cross + w * s
        sums[1] += dot
        sums[2] += cross
        return 0

    lax.fori_loop(2, 6, settle_s, 0)

    def use(k, tile, value):
        rows = slice(8 * tile, 8 * tile + 8)
        sums[3, rows] += value * mod_w[k + 3, rows]

    energy_march(pair_s, 0, 3, use)


def krylov(
    up, down, guess_w, mod_w, inverse, inner_z, inner_s, near_m, far_m, sums_in, low_sent, high_sent,
    bone, row_out, low, first, second, pair, near, far, mods, sums, high,
):
    sub = lax.axis_index("sub")
    run = lax.axis_index("run")
    own = pl.ds(pl.multiple_of(8 * sub, 8), 32)
    widen(low_sent, low)
    widen(high_sent, high)
    blank(pair, far)
    sums[...] = sums_in[...]
    mods[0] = low[9]
    for k in range(3):
        mods[1 + k] = mod_w[k]
    for k in range(2):
        mods[4 + k] = mod_w[6 + k]
    mods[6] = high[6]
    bottom = jnp.where(run > 0, inverted(low[9], mod_w[0]), 0.0)
    top = inverted(mod_w[7], high[6])

    for c in range(3):
        enter(pair, 0, c, low[c])
        enter(pair, 1, c, guess_w[c, 0])
        enter(pair, 2, c, guess_w[c, 7])
        enter(pair, 3, c, high[c])
    march(pair, 0, 1, lambda k, rows: mods[1, rows], near, far, 0)
    march(pair, 2, 1, lambda k, rows: mods[6, rows], near, far, 2)
    begun = (low, down, up, high)
    invert = (bottom, inverse[0], top, high[7])
    dot = 0.0
    ends = []
    for c in range(3):
        values = []
        for k in range(4):
            residual = begun[k][3 + c] - image(near, far, k, c)
            z = residual * invert[k]
            values.append(z)
            if k in (1, 2):
                dot = dot + residual * z
        first[c, 0] = values[0]
        first[c, 1] = values[1]
        for k in range(6):
            first[c, 2 + k] = inner_z[c, k]
        first[c, 8] = values[2]
        ends.append(values[3])
    sums[0] += dot

    for c in range(3):
        enter(pair, 0, c, low[6 + c])
        for k in range(3):
            enter(pair, 1 + k, c, first[c, k])
        enter(pair, 4, c, first[c, 7])
        enter(pair, 5, c, first[c, 8])
        enter(pair, 6, c, ends[c])
    march(pair, 0, 3, lambda k, rows: mods[k, rows], near, far, 0)
    march(pair, 4, 2, lambda k, rows: mods[5 + k, rows], near, far, 4)
    dot, cross = 0.0, 0.0
    for c in range(3):
        images = {
            -1: image(near, far, 1, c),
            0: image(near, far, 2, c),
            1: image(near, far, 3, c) + image(near_m, far_m, 0, c),
            6: image(near, far, 4, c) + image(near_m, far_m, 5, c),
            7: image(near, far, 5, c),
        }
        for k, w in images.items():
            s = w * (bottom if k < 0 else top if k == 7 else inverse[k])
            second[c, k + 1] = s
            if k >= 0:
                dot = dot + w * first[c, k + 1]
                cross = cross + w * s
        for k in range(2, 6):
            second[c, k + 1] = inner_s[c, k - 2]
    sums[1] += dot
    sums[2] += cross

    for c in range(3):
        for at, k in enumerate((-1, 0, 1, 2, 5, 6, 7)):
            enter(pair, at, c, second[c, k + 1])

    def use(first_mod):
        def add(k, tile, value):
            rows = slice(8 * tile, 8 * tile + 8)
            sums[3, rows] += value * mods[first_mod + k, rows]

        return add

    energy_march(pair, 0, 3, use(1))
    energy_march(pair, 4, 2, use(4))
    lane = lax.broadcasted_iota(jnp.int32, (1, 128), 1)
    line = jnp.zeros((1, 128), jnp.float32)
    for k in range(4):
        line = jnp.where(lane == k, whole(sums[k, own]), line)
    total = whole(jnp.sum(bone[...].astype(jnp.float32), axis=0))
    line = jnp.where(lane == 4, total, line)
    row_out[...] = jnp.broadcast_to(line, row_out.shape)


def pick(line, k):
    lane = lax.broadcasted_iota(jnp.int32, line.shape, 1)
    return jnp.sum(jnp.where(lane == k, line, 0.0), axis=1, keepdims=True)


def steplengths(lines):
    line = jnp.sum(lines[:, 32:40], axis=0)[0:1]
    a, b, c, e = (pick(line, k) for k in range(4))
    alpha = a / b
    fresh = alpha * alpha * c - a
    beta = fresh / a
    square = alpha * alpha * e - (1.0 + beta) * (1.0 + beta) * b
    after = fresh / square
    return alpha + after * (1.0 + beta), -after * alpha


def energies(
    lines, guess_w, low, first, second, occupancy, density, spread,
    smooth, pair, specific,
):
    sub = lax.axis_index("sub")
    own = pl.ds(pl.multiple_of(8 * sub, 8), 32)
    p, q = (jnp.broadcast_to(step, (ROWS, 128)) for step in steplengths(lines))
    clear(pair)
    for k in range(9):
        for c in range(3):
            start = guess_w[c, k - 1] if k else low[c]
            enter(pair, k, c, start + p * first[c, k] + q * second[c, k])

    def use(k, tile, value):
        specific[k, 8 * tile : 8 * tile + 8] = value

    energy_march(pair, 0, 8, use, 8)
    parts = []
    for k in range(8):
        rho = density[k]
        share = jnp.where(occupancy[k] == 1, rho * rho / rho, 0.0)
        parts.append(0.5 * share * specific[k, own])
    row = lax.broadcasted_iota(jnp.int32, (128, 128), 0)
    col = lax.broadcasted_iota(jnp.int32, (128, 128), 1)
    gap = jnp.abs(row - col).astype(jnp.float32)
    band = jnp.where(gap <= REACH, NORM * jnp.exp(gap * (-1.0 / DECAY)), 0.0)
    value = jnp.dot(
        jnp.concatenate(parts, axis=0), band,
        precision=lax.Precision.HIGHEST, preferred_element_type=jnp.float32,
    )
    smooth[0:256] = value
    total = whole(value * spread[...].reshape(256, 128))
    smooth[256:264] = jnp.broadcast_to(total, (8, 128))


def decayed(block):
    upward, downward = 0.0, 0.0
    for k in range(8):
        upward = upward + math.exp(-(7 - k) / DECAY) * block[k]
        downward = downward + math.exp(-k / DECAY) * block[k]
    return upward, downward


def ladder(upward, downward, tile, out):
    run = lax.axis_index("run")
    for k in range(out.shape[0]):
        out[k, 0:32] = jnp.where(k > run, upward, downward)
        out[k, 32:40] = tile


def smooth_y(mine, other, planes=8):
    sub = lax.axis_index("sub")
    row = lax.broadcasted_iota(jnp.int32, (32, 32), 0)
    col = lax.broadcasted_iota(jnp.int32, (32, 32), 1)

    def band(offset):
        gap = jnp.abs(col + offset - row).astype(jnp.float32)
        return jnp.where(gap <= REACH, NORM * jnp.exp(gap * (-1.0 / DECAY)), 0.0)

    near = band(0)
    far = band(32 - 64 * sub)
    for k in range(planes):
        yield jnp.dot(
            near, mine(k), precision=lax.Precision.HIGHEST, preferred_element_type=jnp.float32
        ) + jnp.dot(
            far, other(k), precision=lax.Precision.HIGHEST, preferred_element_type=jnp.float32
        )


def bone_z(count, bone, below, above, _, out, rails):
    blocks = [lambda j, ref=ref: ref[j].astype(jnp.float32) for ref in (bone, below, above)]
    for i, (own, far) in enumerate(zip(own_z(blocks[0]), far_z(count, *blocks[1:]))):
        out[i] = own + far
    rails[0], rails[1] = decayed([blocks[0](k) for k in range(8)])


def bone_y(mine, other, rails_mine, rails_other, spread, rails):
    for k, value in enumerate(smooth_y(lambda k: mine[k], lambda k: other[k])):
        spread[k] = value
    for k, value in enumerate(smooth_y(lambda k: rails_mine[k], lambda k: rails_other[k], 2)):
        rails[k] = value


def rungs(rails, mine, other, out):
    ladder(rails[0], rails[1], mine[...] + other[...], out)


def along_y(mine, other, out, planes):
    def at(ref):
        return lambda k: ref[32 * k : 32 * k + 32]

    block = list(smooth_y(at(mine), at(other)))
    for k in range(8):
        out[k] = block[k]
    ladder(*decayed(block), mine[256:264] + other[256:264], planes)


def near_z(count, planes):
    run = lax.axis_index("run")
    lower, upper = 0.0, 0.0
    for o in range(1, REACH // 8):
        scale = math.exp(-8.0 * (o - 1) / DECAY)
        at = jnp.maximum(run - o, 0)
        lower = lower + jnp.where(run - o >= 0, scale * planes[at, 0:32], 0.0)
        at = jnp.minimum(run + o, count - 1)
        upper = upper + jnp.where(run + o < count, scale * planes[at, 0:32], 0.0)
    return [weight(i + 1) * lower + weight(8 - i) * upper for i in range(8)]


def own_z(mine):
    for i in range(8):
        value = 0.0
        for j in range(8):
            value = value + weight(abs(i - j)) * mine(j)
        yield value


def far_z(count, below, above):
    run = lax.axis_index("run")
    has_below = run - REACH // 8 >= 0
    has_above = run + REACH // 8 < count
    for i in range(8):
        far_below, far_above = 0.0, 0.0
        for j in range(8):
            if j >= i:
                far_below = far_below + weight(i - j + REACH) * below(j)
            if j <= i:
                far_above = far_above + weight(j - i + REACH) * above(j)
        yield jnp.where(has_below, far_below, 0.0) + jnp.where(has_above, far_above, 0.0)


def distant_z(count, below, above, lines, guess, first, second, out, displacement):
    blocks = [lambda j, ref=ref: ref[32 * j : 32 * j + 32] for ref in (below, above)]
    for i, value in enumerate(far_z(count, *blocks)):
        out[i] = value
    own = pl.ds(pl.multiple_of(8 * lax.axis_index("sub"), 8), 32)
    p, q = (jnp.broadcast_to(step, (32, 128)) for step in steplengths(lines))
    for c in range(3):
        for k in range(8):
            displacement[c, k] = (
                guess[c, k] + p * first[c, k + 1, own] + q * second[c, k + 1, own]
            )


def distant_y(smooth, mine, other, out):
    far = smooth_y(lambda k: mine[k], lambda k: other[k])
    for i, (near, value) in enumerate(zip(own_z(lambda j: smooth[j]), far)):
        out[i] = near + value


def spread_z(count, part, planes, out):
    for i, share in enumerate(near_z(count, planes)):
        out[i] = part[i] + share


def remodel(count, part, planes, lines, bone, density, out):
    bones = jnp.sum(lines[:, 32:40], axis=0)[0:1]
    line = jnp.sum(planes[:, 32:40], axis=0)[0:1]
    scale = jnp.broadcast_to(pick(bones, 4) / line, density.shape[1:])
    for i, share in enumerate(near_z(count, planes)):
        value = part[i] + share
        rho = density[i]
        updated = jnp.minimum(rho * (1.0 + RATE * jnp.tanh(SLOPE * (value * scale - 1.0))), 1.0)
        out[i] = jnp.where(bone[i] == 1, updated, rho)


def local(load, guess, occupancy, density):
    count = lax.axis_size("run")
    block = density.shape
    depth = block[0]
    swap = [(0, 1), (1, 0)]
    side = lax.ppermute(side_rows(load, guess, occupancy, density), "sub", swap)
    inputs = [load, guess, occupancy, density, side]
    up, down, up_sent, down_sent = call(
        edge,
        [(10, ROWS, 128), (8, ROWS, 128), (11, 32, 128), (9, 32, 128)],
        inputs,
        [
            (3, 5, ROWS, 128), (3, 3, ROWS, 128), (4, ROWS, 128),
            (6, 5, 48, 128), (6, 5, ROWS, 128), (6, 5, 48, 128),
        ],
    )
    low = lax.ppermute(up_sent, "run", [(i, i + 1) for i in range(count - 1)])
    high = lax.ppermute(down_sent, "run", [(i + 1, i) for i in range(count - 1)])
    kept = call(
        middle,
        [
            (3, 8, ROWS, 128), (8, ROWS, 128), (7, ROWS, 128),
            (3, 6, ROWS, 128), (3, 4, ROWS, 128),
            (6, 6, ROWS, 128), (6, 6, 48, 128), (4, ROWS, 128),
        ],
        inputs,
        [
            (3, 8, ROWS, 128), (6, 8, 48, 128), (6, 8, ROWS, 128), (6, 8, 48, 128),
            (6, 6, 48, 128), (6, 4, 48, 128),
        ],
    )
    guess_w = kept[0]
    line, low, first, second = call(
        krylov,
        [(8, 128), (10, ROWS, 128), (3, 9, ROWS, 128), (3, 9, ROWS, 128)],
        [up, down, *kept, low, high, occupancy],
        [
            (6, 7, 48, 128), (6, 7, ROWS, 128), (6, 7, 48, 128),
            (7, ROWS, 128), (4, ROWS, 128), (8, ROWS, 128),
        ],
    )
    smooth, rails = call(
        functools.partial(bone_z, count),
        [block, (2, 32, 128)],
        [occupancy, *far_slabs(occupancy, depth), kept[-1]]
    )
    spread, rails = call(
        bone_y,
        [block, (2, 32, 128)],
        [smooth, lax.ppermute(smooth, "sub", swap), rails, lax.ppermute(rails, "sub", swap)],
    )
    (planes,) = call(
        rungs, [(count, 40, 128)], [rails, line, lax.ppermute(line, "sub", swap)]
    )
    planes = lax.all_to_all(planes, "run", 0, 0, tiled=True)
    lines = planes
    (spread,) = call(functools.partial(spread_z, count), [block], [spread, planes])
    (smooth,) = call(
        energies,
        [(264, 128)],
        [lines, guess_w, low, first, second, occupancy, density, spread],
        [(6, 9, 48, 128), (8, ROWS, 128)],
    )
    below, above = far_slabs(smooth, depth)
    other = lax.ppermute(smooth, "sub", swap)
    smooth, planes = call(along_y, [block, (count, 40, 128)], [smooth, other])
    planes = lax.all_to_all(planes, "run", 0, 0, tiled=True)
    distant, displacement = call(
        functools.partial(distant_z, count),
        [block, guess.shape],
        [below, above, lines, guess, first, second],
        flops=10**10,
    )
    (part,) = call(
        distant_y, [block], [smooth, distant, lax.ppermute(distant, "sub", swap)]
    )
    (new_density,) = call(
        functools.partial(remodel, count),
        [block],
        [part, planes, lines, occupancy, density],
    )
    return displacement, new_density


def far_slabs(block, depth):
    count = lax.axis_size("run")
    span = REACH // depth
    rise = [(i, i + span) for i in range(count - span)]
    fall = [(i + span, i) for i in range(count - span)]
    if count <= 2 * span:
        both = lax.ppermute(block, "run", rise + fall)
        return both, both
    return lax.ppermute(block, "run", rise), lax.ppermute(block, "run", fall)


def solution(mesh):
    field = P(None, ("grp", "run"), "sub", None)
    cells = P(("grp", "run"), "sub", None)
    return jax.shard_map(
        local,
        mesh=mesh,
        in_specs=(field, field, cells, cells),
        out_specs=(field, cells),
        check_vma=False,
    )
```

```python
import functools
import math

import jax
import jax.numpy as jnp
from jax import lax
from jax.experimental import pallas as pl
from jax.experimental.pallas import tpu as pltpu
from jax.sharding import PartitionSpec as P

REACH = 32
POISSON = 0.3
MARROW = 0.05
RATE = 0.5
SLOPE = 4.0
DECAY = REACH / 4.0

LAME = POISSON / ((1.0 + POISSON) * (1.0 - 2.0 * POISSON)) / 16.0
SHEAR = 0.5 / (1.0 + POISSON) / 16.0
ENTRY = 16.0 * (LAME + 4.0 * SHEAR) / 9.0
NORM = 1.0 / sum(math.exp(-abs(k) / DECAY) for k in range(-REACH, REACH + 1))

ROWS = 40
PAIR = ("run", "sub")

VMEM = pl.BlockSpec(memory_space=pltpu.VMEM)


def weight(distance):
    return NORM * math.exp(-distance / DECAY)


def call(kernel, outs, ins, scratch=(), flops=None):
    cost = None
    if flops is not None:
        cost = pl.CostEstimate(flops=flops, bytes_accessed=2**20, transcendentals=0)
    return pl.pallas_call(
        kernel,
        out_shape=[jax.ShapeDtypeStruct(s, jnp.float32) for s in outs],
        in_specs=[VMEM] * len(ins),
        out_specs=[VMEM] * len(outs),
        scratch_shapes=[pltpu.VMEM(s, jnp.float32) for s in scratch],
        compiler_params=pltpu.CompilerParams(vmem_limit_bytes=40 * 1024 * 1024),
        cost_estimate=cost,
    )(*ins)


def lane_right(block):
    lane = lax.broadcasted_iota(jnp.int32, block.shape, 1)
    return jnp.where(lane == 0, 0.0, pltpu.roll(block, 1, 1))


def lane_left(block):
    lane = lax.broadcasted_iota(jnp.int32, block.shape, 1)
    return jnp.where(lane == block.shape[1] - 1, 0.0, pltpu.roll(block, block.shape[1] - 1, 1))


def row_down(block):
    row = lax.broadcasted_iota(jnp.int32, block.shape, 0)
    return jnp.where(row == block.shape[0] - 1, 0.0, pltpu.roll(block, block.shape[0] - 1, 0))


def stiff(occupancy, density):
    return jnp.where(occupancy == 1, density * density, MARROW)


def enter(pair, k, c, field):
    other = lane_right(field)
    pair[2 * c, k, 8:48] = field + other
    pair[2 * c + 1, k, 8:48] = field - other


def clear(pair):
    for m in range(6):
        for k in range(pair.shape[1]):
            pair[m, k, 0:8] = jnp.zeros((8, 128), jnp.float32)


def plane_modes(pair, k, tile):
    out = [None] * 12
    for c in range(3):
        for x in range(2):
            here = pair[2 * c + x, k, 8 + 8 * tile : 16 + 8 * tile]
            above = pair[2 * c + x, k, 7 + 8 * tile : 15 + 8 * tile]
            out[4 * c + x] = here + above
            out[4 * c + 2 + x] = here - above
    return out


def steps(count, body, carry, straight=3):
    if count <= straight:
        for k in range(count):
            carry = body(k, carry)
        return carry

    def turn(k, carry):
        return body(2 * k + 1, body(2 * k, carry))

    carry = lax.fori_loop(0, count // 2, turn, carry)
    return body(count - 1, carry) if count % 2 else carry


def march(pair, start, count, mod, near, far, to):
    for tile in range(ROWS // 8):
        rows = slice(8 * tile, 8 * tile + 8)

        def leave(k, totals):
            for c in range(3):
                for x in range(2):
                    s, d = totals[4 * c + x], totals[4 * c + 2 + x]
                    near[2 * c + x, k, rows] = s + d
                    far[2 * c + x, k, rows] = s - d

        def body(k, carry):
            low, kept = carry
            high = plane_modes(pair, start + k + 1, tile)
            g = stress(modes_of(low, high), mod(k, rows))
            totals, after = [None] * 12, [None] * 12
            for c in range(3):
                for m in range(4):
                    d = g[c][4 + m]
                    at = 4 * c + m
                    if m:
                        s = g[c][m]
                        totals[at] = kept[at] + (s - d)
                        after[at] = s + d
                    else:
                        totals[at] = kept[at] - d
                        after[at] = d
            leave(to + k, totals)
            return high, after

        zeros = [jnp.zeros((8, 128), jnp.float32)] * 12
        _, kept = steps(count, body, (plane_modes(pair, start, tile), zeros))
        leave(to + count, kept)


def image(near, far, k, c):
    columns = [
        near[2 * c + x, k, 0:ROWS] + far[2 * c + x, k, 1 : ROWS + 1] for x in range(2)
    ]
    return columns[0] + columns[1] + lane_left(columns[0] - columns[1])


def energy_march(pair, start, count, use, straight=3):
    for tile in range(ROWS // 8):

        def body(k, low):
            high = plane_modes(pair, start + k + 1, tile)
            use(k, tile, quadratic(modes_of(low, high)))
            return high

        steps(count, body, plane_modes(pair, start, tile), straight)


def inverted(low, high):
    t = low + high
    t = t + row_down(t)
    t = (t + lane_left(t)) * ENTRY
    return jnp.where(t > 0.0, 1.0 / jnp.where(t > 0.0, t, 1.0), 0.0)


def whole(block):
    return jnp.sum(jnp.sum(block, axis=0, keepdims=True), axis=1, keepdims=True)


def modes_of(low, high):
    out = []
    for c in range(3):
        modes = [None] * 8
        for m in range(4):
            if m:
                modes[m] = high[4 * c + m] + low[4 * c + m]
            modes[4 + m] = high[4 * c + m] - low[4 * c + m]
        out.append(modes)
    return out


X, Y, Z = 1, 2, 4


def stress(u, mod):
    g = [[None] * 8 for _ in range(3)]
    bulk, rigid = mod * LAME, mod * SHEAR
    twice = rigid + rigid
    bulk3, rigid3 = mod * (LAME / 3.0), mod * (SHEAR / 3.0)
    last = mod * ((LAME + 4.0 * SHEAR) / 9.0)
    t = (u[0][X] + u[1][Y] + u[2][Z]) * bulk
    g[0][X] = t + u[0][X] * twice
    g[1][Y] = t + u[1][Y] * twice
    g[2][Z] = t + u[2][Z] * twice
    g[0][Y] = g[1][X] = (u[0][Y] + u[1][X]) * rigid
    g[0][Z] = g[2][X] = (u[0][Z] + u[2][X]) * rigid
    g[1][Z] = g[2][Y] = (u[1][Z] + u[2][Y]) * rigid
    for (c, m), (d, n) in (
        ((1, X | Y), (2, X | Z)),
        ((0, X | Y), (2, Y | Z)),
        ((0, X | Z), (1, Y | Z)),
    ):
        s = (u[c][m] + u[d][n]) * bulk3
        g[c][m] = s + u[c][m] * rigid
        g[d][n] = s + u[d][n] * rigid
    s = u[0][Y | Z] + u[1][X | Z] + u[2][X | Y]
    g[0][Y | Z] = (s + u[0][Y | Z]) * rigid3
    g[1][X | Z] = (s + u[1][X | Z]) * rigid3
    g[2][X | Y] = (s + u[2][X | Y]) * rigid3
    for c in range(3):
        g[c][7] = u[c][7] * last
    return g


def quadratic(u):
    def sq(v):
        return v * v

    t = sq(u[0][X] + u[1][Y] + u[2][Z])
    r2 = sq(u[0][X]) + sq(u[1][Y]) + sq(u[2][Z])
    r = sq(u[0][Y] + u[1][X]) + sq(u[0][Z] + u[2][X]) + sq(u[1][Z] + u[2][Y])
    t3 = 0.0
    for (c, m), (d, n) in (
        ((1, X | Y), (2, X | Z)),
        ((0, X | Y), (2, Y | Z)),
        ((0, X | Z), (1, Y | Z)),
    ):
        t3 = t3 + sq(u[c][m] + u[d][n])
        r = r + (sq(u[c][m]) + sq(u[d][n]))
    p, q, s = u[0][Y | Z], u[1][X | Z], u[2][X | Y]
    r3 = sq(p + q) + sq(p + s) + sq(q + s)
    last = sq(u[0][7]) + sq(u[1][7]) + sq(u[2][7])
    return (
        LAME * (t + t3 * (1.0 / 3.0))
        + SHEAR * (r + r2 + r2 + r3 * (1.0 / 3.0))
        + ((LAME + 4.0 * SHEAR) / 9.0) * last
    )


def side_rows(load, guess, occupancy, density):
    sub = lax.axis_index("sub")
    flat = lambda part: part.reshape((-1,) + part.shape[-2:])
    near = lambda part: jnp.where(sub == 0, part[..., 24:32, :], part[..., 0:8, :])
    fields = [flat(near(guess)), flat(near(load))]
    fields, occupancy, density = lax.optimization_barrier((fields, occupancy, density))
    return jnp.concatenate(fields + [stiff(near(occupancy), near(density))], axis=0)


def windows(sub, load, guess, bone, density, side):
    own = pl.ds(pl.multiple_of(8 * sub, 8), 32)
    rest = pl.ds(pl.multiple_of(32 * (1 - sub), 8), 8)

    def put_guess(out, at, c, k):
        out[c, at, own] = guess[c, k]
        out[c, at, rest] = side[8 * c + k]

    def put_load(out, at, c, k):
        out[c, at, own] = load[c, k]
        out[c, at, rest] = side[24 + 8 * c + k]

    def put_mod(out, at, k):
        out[at, own] = stiff(bone[k], density[k])
        out[at, rest] = side[48 + k]

    return put_guess, put_load, put_mod


def blank(pair, far):
    clear(pair)
    for m in range(6):
        for k in range(far.shape[1]):
            far[m, k, ROWS : ROWS + 8] = jnp.zeros((8, 128), jnp.float32)


def narrow(wide, out):
    sub = lax.axis_index("sub")
    own = pl.ds(pl.multiple_of(8 * sub, 8), 32)
    planes = wide.shape[0]
    out[planes] = jnp.zeros((32, 128), jnp.float32)
    for k in range(planes):
        out[k] = wide[k, own]
        out[planes, 3 * k : 3 * k + 3] = jnp.where(sub == 0, wide[k, 32:35], wide[k, 5:8])


def widen(sent, out):
    sub = lax.axis_index("sub")
    own = pl.ds(pl.multiple_of(8 * sub, 8), 32)
    rest = pl.ds(pl.multiple_of(32 * (1 - sub), 8), 8)
    planes = out.shape[0]
    gap = jnp.zeros((5, 128), jnp.float32)
    for k in range(planes):
        rows = sent[planes, 3 * k : 3 * k + 3]
        out[k, own] = sent[k]
        out[k, rest] = jnp.where(
            sub == 0,
            jnp.concatenate([rows, gap], axis=0),
            jnp.concatenate([gap, rows], axis=0),
        )


def edge(
    load, guess, bone, density, side, up, down, up_sent, down_sent, guess_w, load_w, mods, pair, near, far
):
    put_guess, put_load, put_mod = windows(
        lax.axis_index("sub"), load, guess, bone, density, side
    )
    blank(pair, far)
    for at, k in enumerate((0, 1, 6, 7)):
        put_mod(mods, at, k)
    for c in range(3):
        for at, k in enumerate((0, 6, 7)):
            put_load(load_w, at, c, k)
        for at, k in enumerate((0, 1, 5, 6, 7)):
            put_guess(guess_w, at, c, k)
            enter(pair, at, c, guess_w[c, at])
    march(pair, 0, 1, lambda k, rows: mods[1, rows], near, far, 0)
    march(pair, 2, 2, lambda k, rows: mods[2 + k, rows], near, far, 2)
    inverse = inverted(mods[2], mods[3])
    for c in range(3):
        down[c] = guess_w[c, 0]
        down[3 + c] = load_w[c, 0] - image(near, far, 0, c)
        up[c] = guess_w[c, 4]
        up[3 + c] = load_w[c, 2] - image(near, far, 4, c)
        up[6 + c] = (load_w[c, 1] - image(near, far, 3, c)) * inverse
    up[9] = mods[3]
    down[6] = mods[0]
    down[7] = inverted(mods[0], mods[1])
    narrow(up, up_sent)
    narrow(down, down_sent)


def middle(
    load, guess, bone, density, side,
    guess_w, mod_w, inverse, inner_z, inner_s, near_m, far_m, sums,
    load_w, pair, near, far, pair_z, pair_s,
):
    put_guess, put_load, put_mod = windows(
        lax.axis_index("sub"), load, guess, bone, density, side
    )
    blank(pair, far)
    blank(pair_z, far_m)
    clear(pair_s)
    for k in range(8):
        put_mod(mod_w, k, k)
        for c in range(3):
            put_guess(guess_w, k, c, k)
            put_load(load_w, k, c, k)
    for k in range(7):
        inverse[k] = inverted(mod_w[k], mod_w[k + 1])

    def prepare(k, _):
        for c in range(3):
            enter(pair, k, c, guess_w[c, k])
        return 0

    lax.fori_loop(0, 8, prepare, 0)
    march(pair, 0, 7, lambda k, rows: mod_w[k + 1, rows], near, far, 0)
    sums[...] = jnp.zeros_like(sums)

    def settle_z(k, _):
        dot = 0.0
        for c in range(3):
            residual = load_w[c, k] - image(near, far, k, c)
            z = residual * inverse[k]
            inner_z[c, k - 1] = z
            enter(pair_z, k - 1, c, z)
            dot = dot + residual * z
        sums[0] += dot
        return 0

    lax.fori_loop(1, 7, settle_z, 0)
    march(pair_z, 0, 5, lambda k, rows: mod_w[k + 2, rows], near_m, far_m, 0)

    def settle_s(k, _):
        dot, cross = 0.0, 0.0
        for c in range(3):
            w = image(near_m, far_m, k - 1, c)
            s = w * inverse[k]
            inner_s[c, k - 2] = s
            enter(pair_s, k - 2, c, s)
            dot = dot + w * inner_z[c, k - 1]
            cross = cross + w * s
        sums[1] += dot
        sums[2] += cross
        return 0

    lax.fori_loop(2, 6, settle_s, 0)

    def use(k, tile, value):
        rows = slice(8 * tile, 8 * tile + 8)
        sums[3, rows] += value * mod_w[k + 3, rows]

    energy_march(pair_s, 0, 3, use)


def krylov(
    up, down, guess_w, mod_w, inverse, inner_z, inner_s, near_m, far_m, sums_in, low_sent, high_sent,
    bone, row_out, low, first, second, pair, near, far, mods, sums, high,
):
    sub = lax.axis_index("sub")
    run = lax.axis_index("run")
    own = pl.ds(pl.multiple_of(8 * sub, 8), 32)
    widen(low_sent, low)
    widen(high_sent, high)
    blank(pair, far)
    sums[...] = sums_in[...]
    mods[0] = low[9]
    for k in range(3):
        mods[1 + k] = mod_w[k]
    for k in range(2):
        mods[4 + k] = mod_w[6 + k]
    mods[6] = high[6]
    bottom = jnp.where(run > 0, inverted(low[9], mod_w[0]), 0.0)
    top = inverted(mod_w[7], high[6])

    for c in range(3):
        enter(pair, 0, c, low[c])
        enter(pair, 1, c, guess_w[c, 0])
        enter(pair, 2, c, guess_w[c, 7])
        enter(pair, 3, c, high[c])
    march(pair, 0, 1, lambda k, rows: mods[1, rows], near, far, 0)
    march(pair, 2, 1, lambda k, rows: mods[6, rows], near, far, 2)
    begun = (low, down, up, high)
    invert = (bottom, inverse[0], top, high[7])
    dot = 0.0
    ends = []
    for c in range(3):
        values = []
        for k in range(4):
            residual = begun[k][3 + c] - image(near, far, k, c)
            z = residual * invert[k]
            values.append(z)
            if k in (1, 2):
                dot = dot + residual * z
        first[c, 0] = values[0]
        first[c, 1] = values[1]
        for k in range(6):
            first[c, 2 + k] = inner_z[c, k]
        first[c, 8] = values[2]
        ends.append(values[3])
    sums[0] += dot

    for c in range(3):
        enter(pair, 0, c, low[6 + c])
        for k in range(3):
            enter(pair, 1 + k, c, first[c, k])
        enter(pair, 4, c, first[c, 7])
        enter(pair, 5, c, first[c, 8])
        enter(pair, 6, c, ends[c])
    march(pair, 0, 3, lambda k, rows: mods[k, rows], near, far, 0)
    march(pair, 4, 2, lambda k, rows: mods[5 + k, rows], near, far, 4)
    dot, cross = 0.0, 0.0
    for c in range(3):
        images = {
            -1: image(near, far, 1, c),
            0: image(near, far, 2, c),
            1: image(near, far, 3, c) + image(near_m, far_m, 0, c),
            6: image(near, far, 4, c) + image(near_m, far_m, 5, c),
            7: image(near, far, 5, c),
        }
        for k, w in images.items():
            s = w * (bottom if k < 0 else top if k == 7 else inverse[k])
            second[c, k + 1] = s
            if k >= 0:
                dot = dot + w * first[c, k + 1]
                cross = cross + w * s
        for k in range(2, 6):
            second[c, k + 1] = inner_s[c, k - 2]
    sums[1] += dot
    sums[2] += cross

    for c in range(3):
        for at, k in enumerate((-1, 0, 1, 2, 5, 6, 7)):
            enter(pair, at, c, second[c, k + 1])

    def use(first_mod):
        def add(k, tile, value):
            rows = slice(8 * tile, 8 * tile + 8)
            sums[3, rows] += value * mods[first_mod + k, rows]

        return add

    energy_march(pair, 0, 3, use(1))
    energy_march(pair, 4, 2, use(4))
    lane = lax.broadcasted_iota(jnp.int32, (1, 128), 1)
    line = jnp.zeros((1, 128), jnp.float32)
    for k in range(4):
        line = jnp.where(lane == k, whole(sums[k, own]), line)
    total = whole(jnp.sum(bone[...].astype(jnp.float32), axis=0))
    line = jnp.where(lane == 4, total, line)
    row_out[...] = jnp.broadcast_to(line, row_out.shape)


def pick(line, k):
    lane = lax.broadcasted_iota(jnp.int32, line.shape, 1)
    return jnp.sum(jnp.where(lane == k, line, 0.0), axis=1, keepdims=True)


def steplengths(lines):
    line = jnp.sum(lines[:, 32:40], axis=0)[0:1]
    a, b, c, e = (pick(line, k) for k in range(4))
    alpha = a / b
    fresh = alpha * alpha * c - a
    beta = fresh / a
    square = alpha * alpha * e - (1.0 + beta) * (1.0 + beta) * b
    after = fresh / square
    return alpha + after * (1.0 + beta), -after * alpha


def energies(
    lines, guess_w, low, first, second, occupancy, density, spread,
    smooth, pair, specific,
):
    sub = lax.axis_index("sub")
    own = pl.ds(pl.multiple_of(8 * sub, 8), 32)
    p, q = (jnp.broadcast_to(step, (ROWS, 128)) for step in steplengths(lines))
    clear(pair)
    for k in range(9):
        for c in range(3):
            start = guess_w[c, k - 1] if k else low[c]
            enter(pair, k, c, start + p * first[c, k] + q * second[c, k])

    def use(k, tile, value):
        specific[k, 8 * tile : 8 * tile + 8] = value

    energy_march(pair, 0, 8, use, 8)
    parts = []
    for k in range(8):
        rho = density[k]
        share = jnp.where(occupancy[k] == 1, rho * rho / rho, 0.0)
        parts.append(0.5 * share * specific[k, own])
    row = lax.broadcasted_iota(jnp.int32, (128, 128), 0)
    col = lax.broadcasted_iota(jnp.int32, (128, 128), 1)
    gap = jnp.abs(row - col).astype(jnp.float32)
    band = jnp.where(gap <= REACH, NORM * jnp.exp(gap * (-1.0 / DECAY)), 0.0)
    value = jnp.dot(
        jnp.concatenate(parts, axis=0), band,
        precision=lax.Precision.HIGHEST, preferred_element_type=jnp.float32,
    )
    smooth[0:256] = value
    total = whole(value * spread[...].reshape(256, 128))
    smooth[256:264] = jnp.broadcast_to(total, (8, 128))


def decayed(block):
    upward, downward = 0.0, 0.0
    for k in range(8):
        upward = upward + math.exp(-(7 - k) / DECAY) * block[k]
        downward = downward + math.exp(-k / DECAY) * block[k]
    return upward, downward


def ladder(upward, downward, tile, out):
    run = lax.axis_index("run")
    for k in range(out.shape[0]):
        out[k, 0:32] = jnp.where(k > run, upward, downward)
        out[k, 32:40] = tile


def smooth_y(mine, other, planes=8):
    sub = lax.axis_index("sub")
    row = lax.broadcasted_iota(jnp.int32, (32, 32), 0)
    col = lax.broadcasted_iota(jnp.int32, (32, 32), 1)

    def band(offset):
        gap = jnp.abs(col + offset - row).astype(jnp.float32)
        return jnp.where(gap <= REACH, NORM * jnp.exp(gap * (-1.0 / DECAY)), 0.0)

    near = band(0)
    far = band(32 - 64 * sub)
    for k in range(planes):
        yield jnp.dot(
            near, mine(k), precision=lax.Precision.HIGHEST, preferred_element_type=jnp.float32
        ) + jnp.dot(
            far, other(k), precision=lax.Precision.HIGHEST, preferred_element_type=jnp.float32
        )


def bone_z(count, bone, below, above, _, out, rails):
    blocks = [lambda j, ref=ref: ref[j].astype(jnp.float32) for ref in (bone, below, above)]
    for i, (own, far) in enumerate(zip(own_z(blocks[0]), far_z(count, *blocks[1:]))):
        out[i] = own + far
    rails[0], rails[1] = decayed([blocks[0](k) for k in range(8)])


def bone_y(mine, other, rails_mine, rails_other, spread, rails):
    for k, value in enumerate(smooth_y(lambda k: mine[k], lambda k: other[k])):
        spread[k] = value
    for k, value in enumerate(smooth_y(lambda k: rails_mine[k], lambda k: rails_other[k], 2)):
        rails[k] = value


def rungs(rails, mine, other, out):
    ladder(rails[0], rails[1], mine[...] + other[...], out)


def along_y(mine, other, planes):
    sums = [decayed([ref[32 * k : 32 * k + 32] for k in range(8)]) for ref in (mine, other)]
    upward, downward = smooth_y(lambda k: sums[0][k], lambda k: sums[1][k], 2)
    ladder(upward, downward, mine[256:264] + other[256:264], planes)


def near_z(count, planes):
    run = lax.axis_index("run")
    lower, upper = 0.0, 0.0
    for o in range(1, REACH // 8):
        scale = math.exp(-8.0 * (o - 1) / DECAY)
        at = jnp.maximum(run - o, 0)
        lower = lower + jnp.where(run - o >= 0, scale * planes[at, 0:32], 0.0)
        at = jnp.minimum(run + o, count - 1)
        upper = upper + jnp.where(run + o < count, scale * planes[at, 0:32], 0.0)
    return [weight(i + 1) * lower + weight(8 - i) * upper for i in range(8)]


def own_z(mine):
    for i in range(8):
        value = 0.0
        for j in range(8):
            value = value + weight(abs(i - j)) * mine(j)
        yield value


def far_z(count, below, above):
    run = lax.axis_index("run")
    has_below = run - REACH // 8 >= 0
    has_above = run + REACH // 8 < count
    for i in range(8):
        far_below, far_above = 0.0, 0.0
        for j in range(8):
            if j >= i:
                far_below = far_below + weight(i - j + REACH) * below(j)
            if j <= i:
                far_above = far_above + weight(j - i + REACH) * above(j)
        yield jnp.where(has_below, far_below, 0.0) + jnp.where(has_above, far_above, 0.0)


def distant_z(count, mine, below, above, lines, guess, first, second, out, displacement):
    blocks = [lambda j, ref=ref: ref[32 * j : 32 * j + 32] for ref in (mine, below, above)]
    for i, (near, far) in enumerate(zip(own_z(blocks[0]), far_z(count, *blocks[1:]))):
        out[i] = near + far
    own = pl.ds(pl.multiple_of(8 * lax.axis_index("sub"), 8), 32)
    p, q = (jnp.broadcast_to(step, (32, 128)) for step in steplengths(lines))
    for c in range(3):
        for k in range(8):
            displacement[c, k] = (
                guess[c, k] + p * first[c, k + 1, own] + q * second[c, k + 1, own]
            )


def distant_y(mine, other, out):
    for k, value in enumerate(smooth_y(lambda k: mine[k], lambda k: other[k])):
        out[k] = value


def spread_z(count, part, planes, out):
    for i, share in enumerate(near_z(count, planes)):
        out[i] = part[i] + share


def remodel(count, part, planes, lines, bone, density, out):
    bones = jnp.sum(lines[:, 32:40], axis=0)[0:1]
    line = jnp.sum(planes[:, 32:40], axis=0)[0:1]
    scale = jnp.broadcast_to(pick(bones, 4) / line, density.shape[1:])
    for i, share in enumerate(near_z(count, planes)):
        value = part[i] + share
        rho = density[i]
        updated = jnp.minimum(rho * (1.0 + RATE * jnp.tanh(SLOPE * (value * scale - 1.0))), 1.0)
        out[i] = jnp.where(bone[i] == 1, updated, rho)


def local(load, guess, occupancy, density):
    count = lax.axis_size("run")
    block = density.shape
    depth = block[0]
    swap = [(0, 1), (1, 0)]
    side = lax.ppermute(side_rows(load, guess, occupancy, density), "sub", swap)
    inputs = [load, guess, occupancy, density, side]
    up, down, up_sent, down_sent = call(
        edge,
        [(10, ROWS, 128), (8, ROWS, 128), (11, 32, 128), (9, 32, 128)],
        inputs,
        [
            (3, 5, ROWS, 128), (3, 3, ROWS, 128), (4, ROWS, 128),
            (6, 5, 48, 128), (6, 5, ROWS, 128), (6, 5, 48, 128),
        ],
    )
    low = lax.ppermute(up_sent, "run", [(i, i + 1) for i in range(count - 1)])
    high = lax.ppermute(down_sent, "run", [(i + 1, i) for i in range(count - 1)])
    kept = call(
        middle,
        [
            (3, 8, ROWS, 128), (8, ROWS, 128), (7, ROWS, 128),
            (3, 6, ROWS, 128), (3, 4, ROWS, 128),
            (6, 6, ROWS, 128), (6, 6, 48, 128), (4, ROWS, 128),
        ],
        inputs,
        [
            (3, 8, ROWS, 128), (6, 8, 48, 128), (6, 8, ROWS, 128), (6, 8, 48, 128),
            (6, 6, 48, 128), (6, 4, 48, 128),
        ],
    )
    guess_w = kept[0]
    line, low, first, second = call(
        krylov,
        [(8, 128), (10, ROWS, 128), (3, 9, ROWS, 128), (3, 9, ROWS, 128)],
        [up, down, *kept, low, high, occupancy],
        [
            (6, 7, 48, 128), (6, 7, ROWS, 128), (6, 7, 48, 128),
            (7, ROWS, 128), (4, ROWS, 128), (8, ROWS, 128),
        ],
    )
    smooth, rails = call(
        functools.partial(bone_z, count),
        [block, (2, 32, 128)],
        [occupancy, *far_slabs(occupancy, depth), kept[-1]]
    )
    spread, rails = call(
        bone_y,
        [block, (2, 32, 128)],
        [smooth, lax.ppermute(smooth, "sub", swap), rails, lax.ppermute(rails, "sub", swap)],
    )
    (planes,) = call(
        rungs, [(count, 40, 128)], [rails, line, lax.ppermute(line, "sub", swap)]
    )
    planes = lax.all_to_all(planes, "run", 0, 0, tiled=True)
    lines = planes
    (spread,) = call(functools.partial(spread_z, count), [block], [spread, planes])
    (smooth,) = call(
        energies,
        [(264, 128)],
        [lines, guess_w, low, first, second, occupancy, density, spread],
        [(6, 9, 48, 128), (8, ROWS, 128)],
    )
    below, above = far_slabs(smooth, depth)
    other = lax.ppermute(smooth, "sub", swap)
    (planes,) = call(along_y, [(count, 40, 128)], [smooth, other])
    planes = lax.all_to_all(planes, "run", 0, 0, tiled=True)
    distant, displacement = call(
        functools.partial(distant_z, count),
        [block, guess.shape],
        [smooth, below, above, lines, guess, first, second],
        flops=10**10,
    )
    (part,) = call(
        distant_y, [block], [distant, lax.ppermute(distant, "sub", swap)]
    )
    (new_density,) = call(
        functools.partial(remodel, count),
        [block],
        [part, planes, lines, occupancy, density],
    )
    return displacement, new_density


def far_slabs(block, depth):
    count = lax.axis_size("run")
    span = REACH // depth
    rise = [(i, i + span) for i in range(count - span)]
    fall = [(i + span, i) for i in range(count - span)]
    if count <= 2 * span:
        both = lax.ppermute(block, "run", rise + fall)
        return both, both
    return lax.ppermute(block, "run", rise), lax.ppermute(block, "run", fall)


def solution(mesh):
    field = P(None, ("grp", "run"), "sub", None)
    cells = P(("grp", "run"), "sub", None)
    return jax.shard_map(
        local,
        mesh=mesh,
        in_specs=(field, field, cells, cells),
        out_specs=(field, cells),
        check_vma=False,
    )
```
